128 devices in a mesh: seq: 8 (over y, x_hi), vocab: 16 (over z, x_lo, core).
Axes of the slice: x: 4 (x_hi: 2, x_lo: 2; x = x_hi * 2 + x_lo), y: 4, z: 4, core: 2. Of those that a mesh axis runs over, the one named last changes fastest.
Arguments:
- hidden: bfloat16 [1024, 7168], P('seq', 'vocab'), may hold values from -150 to 150
- next_ids: int32 [1024], P('seq'), may hold values from 0 to 65535
- targets: int32 [1024], P('seq'), may hold values from 0 to 65535
- embed_table: bfloat16 [65536, 7168], P('seq', 'vocab'), may hold values from -80 to 80
- gain_hidden: float32 [7168], P('vocab'), may hold values from 0.5 to 1.5
- gain_embed: float32 [7168], P('vocab'), may hold values from 0.5 to 1.5
- proj_hidden: bfloat16 [7168, 7168], P('vocab', 'seq'), may hold values from -0.0625 to 0.0625
- proj_embed: bfloat16 [7168, 7168], P('vocab', 'seq'), may hold values from -0.0625 to 0.0625
- gain_final: float32 [7168], P('seq'), may hold values from 0.5 to 1.5
- head_weight: bfloat16 [65536, 7168], P(('seq', 'vocab')), may hold values from -3.30718914 to 3.30718914
Outputs:
- loss_mean: float32 [], replicated
- head_grad: bfloat16 [65536, 7168], P(('seq', 'vocab'))
The draws below stay inside these ranges and needn't reach their ends.
All inputs are finite; a program needn't handle non-finite values.
Results may differ from the reference program's by a relative error of at most 0.011.
Values may be sent and summed in bfloat16 or wider, within the bound.
A program may use at most 128 MiB of HBM per device.

```python
import math
import jax
import jax.numpy as jnp
import numpy as np
from jax import lax

D = 7168
VOCAB = 65536
TOKENS = 1024


def column_scales(key_col, width):
    rising = 3.0 ** (0.5 * jnp.arange(width, dtype=jnp.float32) / width)
    rough = jnp.exp(jax.random.uniform(key_col, (width,), jnp.float32, math.log(0.5), math.log(1.5)))
    return rising * rough


def draw_hidden(key, part):
    key = jax.random.fold_in(key, 11)
    key_val, key_row, key_col = jax.random.split(key, 3)
    col_scale = column_scales(key_col, D)
    values = jnp.clip(jax.random.normal(key_val, (TOKENS, D), jnp.float32), -4.0, 4.0)
    row_scale = jnp.exp(jax.random.uniform(key_row, (TOKENS, 1), jnp.float32, 0.0, math.log(10.0)))
    return (values * row_scale * col_scale[None, :]).astype(jnp.bfloat16)


def draw_embed_table(key, part):
    key = jax.random.fold_in(key, 12)
    key_val, key_row, key_col = jax.random.split(key, 3)
    col_scale = column_scales(key_col, D)
    row_scale = jnp.exp(jax.random.uniform(key_row, (VOCAB, 1), jnp.float32, math.log(0.5), math.log(5.0)))
    values = jnp.clip(jax.random.normal(key_val, (VOCAB, D), jnp.float32), -4.0, 4.0)
    return (values * row_scale * col_scale[None, :]).astype(jnp.bfloat16)


def draw_head_weight(key, part):
    key = jax.random.fold_in(key, 13)
    key_val, key_row = jax.random.split(key, 2)
    row_scale = jnp.exp(jax.random.uniform(key_row, (VOCAB, 1), jnp.float32, 0.0, math.log(10.0)))
    root = float(D) ** 0.5
    values = jnp.clip(jax.random.normal(key_val, (VOCAB, D), jnp.float32), -4.0, 4.0) * row_scale / root
    return values.astype(jnp.bfloat16)


def set_ends(drawn, own_key, least, high):
    dims = drawn.shape
    place = [jax.random.randint(jax.random.fold_in(own_key, axis), (), 0, dims[axis]) for axis in range(len(dims))]
    drawn = drawn.at[tuple(place)].set(least)
    longest = dims.index(max(dims))
    place[longest] = (place[longest] + 1) % dims[longest]
    return drawn.at[tuple(place)].set(high)


def steps_of(own_key, shape, cuts, smallest, high):
    def one(position, shards_of):
        draws = jax.random.uniform(jax.random.fold_in(jax.random.fold_in(own_key, 6), position), (shards_of,), jnp.float32, smallest / len(cuts), high / len(cuts))
        return jnp.repeat(jnp.exp(draws), shape[position] // shards_of).reshape((-1,) + (1,) * (len(shape) - position - 1))

    level = one(*cuts[0])
    for cut in cuts[1:]:
        level = level * one(*cut)
    return level


def cumulative_ranks(count, skew):
    weights = [(1 << 20) // math.isqrt(standing ** skew) + 1 for standing in range(1, count + 1)]
    spread = 1 + sum(weights) // (1 << 30)
    return np.cumsum(np.array([max(1, weight // spread) for weight in weights]))


def skewed_ids(own_key, dims, amount, slope):
    grid = cumulative_ranks(amount, slope)
    pick = jax.random.randint(jax.random.fold_in(own_key, 1), dims, 0, int(grid[amount - 1]))
    rank = jnp.searchsorted(jnp.asarray(grid, jnp.int32), pick, side="right")
    return jax.random.permutation(jax.random.fold_in(own_key, 2), amount)[rank].astype(jnp.int32)


def gaussian(key, extent, scale, reach, cuts=(), kind=jnp.bfloat16):
    array = jax.random.normal(key, extent, jnp.float32) * scale
    if len(cuts) > 0:
        array = steps_of(key, extent, cuts, -0.22, 0.18) * array
    return jnp.clip(array, min=-reach, max=reach).astype(kind)


def setup_inputs(seed: int = 0) -> dict:
    key_list = jax.random.split(jax.random.key(seed), 11)
    hidden = draw_hidden(jax.random.fold_in(key_list[10], 71), 0)
    next_ids = set_ends(skewed_ids(key_list[1], (TOKENS,), VOCAB, 2), jax.random.fold_in(key_list[1], 3), 0, VOCAB - 1).astype(jnp.int32)
    targets = set_ends(skewed_ids(key_list[2], (TOKENS,), VOCAB, 2), jax.random.fold_in(key_list[2], 3), 0, VOCAB - 1).astype(jnp.int32)
    embed_table = draw_embed_table(jax.random.fold_in(key_list[10], 71), 0)
    gain_hidden = jnp.clip(1.0 + 0.1 * jax.random.normal(key_list[4], (D,), jnp.float32), 0.5, 1.5)
    gain_embed = jnp.clip(1.0 + 0.1 * jax.random.normal(key_list[5], (D,), jnp.float32), 0.5, 1.5)
    proj_hidden = gaussian(key_list[6], (D, D), D ** -0.5, 0.0625, ((0, 16), (1, 8)))
    proj_embed = gaussian(key_list[7], (D, D), D ** -0.5, 0.0625, ((0, 16), (1, 8)))
    gain_final = jnp.clip(1.0 + 0.1 * jax.random.normal(key_list[8], (D,), jnp.float32), 0.5, 1.5)
    head_weight = draw_head_weight(jax.random.fold_in(key_list[10], 71), 0)
    return dict(hidden=hidden, next_ids=next_ids, targets=targets, embed_table=embed_table, gain_hidden=gain_hidden, gain_embed=gain_embed, proj_hidden=proj_hidden, proj_embed=proj_embed, gain_final=gain_final, head_weight=head_weight)


EPSILON = 1e-06

def rms_normed(values, gain):
    mean_square = lax.optimization_barrier(jnp.mean(values * values, axis=1, keepdims=True))
    return values * lax.rsqrt(mean_square + EPSILON) * gain

def reference(hidden, next_ids, targets, embed_table, gain_hidden, gain_embed, proj_hidden, proj_embed, gain_final, head_weight):
    embedded = jnp.take(embed_table, next_ids, axis=0)
    normed_hidden = rms_normed(hidden.astype(jnp.float32), gain_hidden).astype(jnp.bfloat16)
    normed_embed = rms_normed(embedded.astype(jnp.float32), gain_embed).astype(jnp.bfloat16)
    projected = jnp.dot(normed_hidden, proj_hidden, preferred_element_type=jnp.float32) + jnp.dot(normed_embed, proj_embed, preferred_element_type=jnp.float32)
    final_rows = rms_normed(projected, gain_final).astype(jnp.bfloat16)
    logits = lax.dot_general(final_rows, head_weight, (((1,), (1,)), ((), ())), preferred_element_type=jnp.float32)
    row_peak = lax.optimization_barrier(jnp.max(logits, axis=1, keepdims=True))
    log_total = row_peak + jnp.log(lax.optimization_barrier(jnp.sum(jnp.exp(logits - row_peak), axis=1, keepdims=True)))
    columns = lax.broadcasted_iota(jnp.int32, logits.shape, 1)
    matches = columns == targets.astype(jnp.int32)[:, None]
    chosen = lax.optimization_barrier(jnp.sum(jnp.where(matches, logits, 0.0), axis=1, keepdims=True))
    loss_mean = jnp.mean(log_total - chosen)
    logit_grad = (jnp.exp(logits - log_total) - matches.astype(jnp.float32)).astype(jnp.bfloat16)
    head_grad = lax.dot_general(logit_grad, final_rows, (((0,), (0,)), ((), ())), preferred_element_type=jnp.float32).astype(jnp.bfloat16)
    return (loss_mean, head_grad)
```

```python
import jax
import jax.numpy as jnp
from jax import lax
from jax.experimental import pallas as pl
from jax.experimental.pallas import tpu as pltpu
from jax.sharding import PartitionSpec as P

MESH = pl.DeviceIdType.MESH
D = 7168
EPSILON = 1e-06
HIGH, LOW = 48, 16
ORDERS = (((2, 0, 1), (0, 1, 2)), ((2, 1, 0), (1, 0, 2)))
ROWS = ((0, HIGH), (HIGH, LOW))


def coordinates():
    seq, vocab = lax.axis_index("seq"), lax.axis_index("vocab")
    return (
        (2 * lax.rem(seq, 2) + lax.rem(lax.div(vocab, 2), 2), lax.div(seq, 2), lax.div(vocab, 4)),
        lax.rem(vocab, 2),
    )


def device(pos, core):
    x, y, z = pos
    return (2 * y + lax.div(x, 2), 4 * z + 2 * lax.rem(x, 2) + core)


def shifted(pos, axis, by):
    moved = list(pos)
    moved[axis] = lax.rem(pos[axis] + (by + 4), 4)
    return tuple(moved)


def greet(peers):
    barrier = pltpu.get_barrier_semaphore()
    for peer in peers:
        pl.semaphore_signal(barrier, inc=1, device_id=peer, device_id_type=MESH)
    pl.semaphore_wait(barrier, len(peers))


def head_kernel(
    block_ref, head_ref, target_ref, grad_ref, loss_ref, rows_out,
    rows, head, scores, stats, vstats, sstats,
    ring_send, ring_recv, pair_send, pair_recv, stat_send, stat_recv, local_sem, out_sem,
):
    pos, core = coordinates()
    seq, vocab = lax.axis_index("seq"), lax.axis_index("vocab")
    x, y, z = pos
    head_copies = [
        pltpu.make_async_copy(
            head_ref.at[:, pl.ds(896 * i, 896)], head.at[i], local_sem.at[i]
        )
        for i in range(8)
    ]
    for copy in head_copies:
        copy.start()
    vocab_peers = [(seq, lax.rem(vocab + i, 16)) for i in range(1, 16)]
    seq_peers = [(lax.rem(seq + i, 8), vocab) for i in range(1, 8)]
    across = device(shifted(pos, 0, 1 - 2 * (1 - lax.rem(x, 2))), core)
    greet(vocab_peers + seq_peers + [across])

    rows[x, y, z, core] = block_ref[...]

    def unit(part, at, axis, half=None):
        index = list(at)
        if axis is not None:
            index[axis] = pl.ds(0, 4) if half is None else pl.ds(2 * half, 2)
        return index, ROWS[part]

    def ref_of(where, which):
        index, (first, count) = where
        return rows.at[index[0], index[1], index[2], which, pl.ds(first, count), :]

    def ring(mine, part, number, where, to):
        target = device(to, mine)
        piece = ref_of(where, mine)
        return pltpu.make_async_remote_copy(
            src_ref=piece, dst_ref=piece,
            send_sem=ring_send.at[part, number], recv_sem=ring_recv.at[part, number],
            device_id=target, device_id_type=MESH,
        )

    def pair(part, number, where, which, mine):
        piece = ref_of(where, which)
        return pltpu.make_async_remote_copy(
            src_ref=piece, dst_ref=piece,
            send_sem=pair_send.at[part, number], recv_sem=pair_recv.at[part, number],
            device_id=device(pos, 1 - mine), device_id_type=MESH,
        )

    def line_units(order, part):
        a, b, c = order
        lines = [(1, pos)]
        lines += [(2, shifted(pos, b, -1)), (2, shifted(pos, b, 1)), (3, shifted(pos, b, 2))]
        middles = [lines[i][1] for i in range(4)]
        for j, middle in enumerate(middles):
            lines += [(4 + j, shifted(middle, c, -1)), (4 + j, shifted(middle, c, 1))]
        for j, middle in enumerate(middles):
            lines.append((8 + j, shifted(middle, c, 2)))
        return [(step, unit(part, at, a)) for step, at in lines]

    def own_step(mine, step):
        for part in range(2):
            a, b, c = ORDERS[mine][part]

            def send(number, where, to):
                ring(mine, part, number, where, to).start()

            def recv(number, where):
                ring(mine, part, number, where, pos).wait_recv()

            def up(axis):
                return shifted(pos, axis, 1)

            def down(axis):
                return shifted(pos, axis, -1)

            middles = [pos, down(b), up(b), shifted(pos, b, 2)]

            def spread(j):
                send(7 + 4 * j, unit(part, middles[j], a), up(c))
                send(8 + 4 * j, unit(part, middles[j], a), down(c))

            if step == 0:
                send(0, unit(part, pos, None), up(a))
                send(1, unit(part, pos, None), down(a))
            elif step == 1:
                recv(0, unit(part, down(a), None))
                send(2, unit(part, down(a), None), up(a))
                recv(1, unit(part, up(a), None))
                recv(2, unit(part, shifted(pos, a, 2), None))
                send(3, unit(part, pos, a), up(b))
                send(4, unit(part, pos, a), down(b))
                spread(0)
            elif step == 2:
                recv(3, unit(part, middles[1], a))
                send(5, unit(part, middles[1], a, 0), up(b))
                recv(4, unit(part, middles[2], a))
                send(6, unit(part, middles[2], a, 1), down(b))
                spread(1)
                spread(2)
            elif step == 3:
                recv(5, unit(part, middles[3], a, 0))
                recv(6, unit(part, middles[3], a, 1))
                spread(3)
            elif step < 8:
                j = step - 4
                before, after = shifted(middles[j], c, -1), shifted(middles[j], c, 1)
                recv(7 + 4 * j, unit(part, before, a))
                send(9 + 4 * j, unit(part, before, a, 0), up(c))
                recv(8 + 4 * j, unit(part, after, a))
                send(10 + 4 * j, unit(part, after, a, 1), down(c))
            else:
                j = step - 8
                far = shifted(middles[j], c, 2)
                recv(9 + 4 * j, unit(part, far, a, 0))
                recv(10 + 4 * j, unit(part, far, a, 1))
            for number, (when, where) in enumerate(line_units(ORDERS[mine][part], part)):
                if when == step:
                    pair(part, number, where, mine, mine).start()

    def pair_step(mine, step):
        for part in range(2):
            for number, (when, where) in enumerate(line_units(ORDERS[1 - mine][part], part)):
                if when == step:
                    pair(part, number, where, 1 - mine, mine).wait_recv()

    def by_core(action, step):
        for mine in range(2):

            @pl.when(core == mine)
            def _():
                action(mine, step)

    x_hi = lax.div(x, 2)

    def multiply(dy, other, part):
        y_at = lax.rem(y + dy + 4, 4)
        hi_at = lax.rem(x_hi + other, 2)
        first, count = ROWS[part]
        taken = rows[pl.ds(2 * hi_at, 2), y_at, :, :, pl.ds(first, count), :].reshape(-1, 896)
        product = lax.dot_general(
            head[2 * y_at + hi_at], taken, (((1,), (1,)), ((), ())), preferred_element_type=jnp.float32
        )
        columns = slice(0, 16 * HIGH) if part == 0 else slice(16 * HIGH, 1024)
        if (dy, other) == (0, 0):
            scores[:, columns] = product
        else:
            scores[:, columns] += product

    out_copies = []

    def write_out(dy, other):
        y_at = lax.rem(y + dy + 4, 4)
        hi_at = lax.rem(x_hi + other, 2)
        piece = (pl.ds(2 * hi_at, 2), y_at)
        copy = pltpu.make_async_copy(rows.at[piece], rows_out.at[piece], out_sem.at[len(out_copies)])
        copy.start()
        out_copies.append(copy)

    ready = {
        4: [(0, 0, 0)],
        6: [(-1, 0, 0), (1, 0, 0)],
        8: [(0, 1, 0)],
        9: [(-1, 1, 0)],
        10: [(2, 0, 0), (1, 1, 0), (0, 0, 1), (-1, 0, 1), (1, 0, 1)],
        11: [(2, 1, 0), (2, 0, 1), (0, 1, 1), (-1, 1, 1), (1, 1, 1), (2, 1, 1)],
    }
    for step in range(13):
        if step < 12:
            by_core(own_step, step)
        if step == 3:
            for copy in head_copies:
                copy.wait()
        if step >= 2:
            by_core(pair_step, step - 1)
            for dy, other, part in ready.get(step - 1, []):
                multiply(dy, other, part)
                if part == 1:
                    write_out(dy, other)

    first_entry = (seq * 16 + vocab) * 512
    entries = first_entry + lax.broadcasted_iota(jnp.int32, (512, 128), 0)
    for q in range(8):
        columns = slice(128 * q, 128 * q + 128)
        part = scores[:, columns]
        peak = jnp.max(part, axis=0, keepdims=True)
        matches = entries == target_ref[q : q + 1, :]
        chosen = jnp.sum(jnp.where(matches, part, 0.0), axis=0, keepdims=True)
        powers = jnp.exp(part - peak)
        scores[:, columns] = powers
        stats[0, q : q + 1, :] = peak
        stats[1, q : q + 1, :] = jnp.sum(powers, axis=0, keepdims=True)
        stats[2, q : q + 1, :] = chosen

    def exchange(slots, me, peers, count, base):
        slots[me] = stats[...]
        copies = []
        for i, peer in enumerate(peers):
            copies.append(pltpu.make_async_remote_copy(
                src_ref=stats, dst_ref=slots.at[me],
                send_sem=stat_send.at[base + i], recv_sem=stat_recv.at[base + i],
                device_id=peer, device_id_type=MESH,
            ))
            copies[-1].start()
        for i in range(len(peers)):
            sender = lax.rem(me - (i + 1) + count, count)
            pltpu.make_async_remote_copy(
                src_ref=stats, dst_ref=slots.at[sender],
                send_sem=stat_send.at[base + i], recv_sem=stat_recv.at[base + i],
                device_id=peers[i], device_id_type=MESH,
            ).wait_recv()
        for copy in copies:
            copy.wait_send()
        peaks = slots[:, 0]
        top = jnp.max(peaks, axis=0)
        total = jnp.sum(slots[:, 1] * jnp.exp(peaks - top[None]), axis=0)
        chosen = jnp.sum(slots[:, 2], axis=0)
        return top, total, chosen

    own_peak = stats[0]
    top, total, chosen = exchange(vstats, vocab, vocab_peers, 16, 0)
    stats[0], stats[1], stats[2] = top, total, chosen
    top, total, chosen = exchange(sstats, seq, seq_peers, 8, 15)
    log_total = top + jnp.log(total)
    loss_ref[0, 0] = jnp.sum(log_total - chosen) / 1024
    stats[0] = jnp.exp(own_peak - log_total)
    for q in range(8):
        columns = slice(128 * q, 128 * q + 128)
        matches = entries == target_ref[q : q + 1, :]
        grad = scores[:, columns] * stats[0, q : q + 1, :] - jnp.where(matches, 1.0, 0.0)
        grad_ref[:, columns] = grad.astype(jnp.bfloat16)

    def finish(mine, _):
        for part in range(2):
            a, b, c = ORDERS[mine][part]
            sizes = [(pos, None, None)] * 3 + [(pos, a, None)] * 2 + [(pos, a, 0)] * 2
            sizes += ([(pos, a, None)] * 2 + [(pos, a, 0)] * 2) * 4
            for number, (at, axis, half) in enumerate(sizes):
                ring(mine, part, number, unit(part, at, axis, half), pos).wait_send()
            for number, (_, where) in enumerate(line_units(ORDERS[mine][part], part)):
                pair(part, number, where, mine, mine).wait_send()

    by_core(finish, 0)
    for copy in out_copies:
        copy.wait()


def head_part(block, head_weight, targets):
    return pl.pallas_call(
        head_kernel,
        out_shape=(
            jax.ShapeDtypeStruct((512, 1024), jnp.bfloat16),
            jax.ShapeDtypeStruct((1, 1), jnp.float32),
            jax.ShapeDtypeStruct((4, 4, 4, 2, 64, 896), jnp.bfloat16),
        ),
        in_specs=[
            pl.BlockSpec(memory_space=pltpu.VMEM),
            pl.BlockSpec(memory_space=pl.ANY),
            pl.BlockSpec(memory_space=pltpu.VMEM),
        ],
        out_specs=(
            pl.BlockSpec(memory_space=pltpu.VMEM),
            pl.BlockSpec(memory_space=pltpu.SMEM),
            pl.BlockSpec(memory_space=pl.ANY),
        ),
        scratch_shapes=[
            pltpu.VMEM((4, 4, 4, 2, 64, 896), jnp.bfloat16),
            pltpu.VMEM((8, 512, 896), jnp.bfloat16),
            pltpu.VMEM((512, 1024), jnp.float32),
            pltpu.VMEM((3, 8, 128), jnp.float32),
            pltpu.VMEM((16, 3, 8, 128), jnp.float32),
            pltpu.VMEM((8, 3, 8, 128), jnp.float32),
            pltpu.SemaphoreType.DMA((2, 23)),
            pltpu.SemaphoreType.DMA((2, 23)),
            pltpu.SemaphoreType.DMA((2, 16)),
            pltpu.SemaphoreType.DMA((2, 16)),
            pltpu.SemaphoreType.DMA((22,)),
            pltpu.SemaphoreType.DMA((22,)),
            pltpu.SemaphoreType.DMA((8,)),
            pltpu.SemaphoreType.DMA((8,)),
        ],
        compiler_params=pltpu.CompilerParams(
            collective_id=2, has_side_effects=True, vmem_limit_bytes=56 * 1024 * 1024
        ),
    )(block, head_weight, targets)


def grad_kernel(grad_ref, rows_ref, out_ref):
    high = rows_ref[:, 0, :, :, 0:HIGH, :].reshape(16 * HIGH, 896)
    low = rows_ref[:, 0, :, :, HIGH:64, :].reshape(16 * LOW, 896)
    out_ref[...] = (
        jnp.dot(grad_ref[:, : 16 * HIGH], high, preferred_element_type=jnp.float32)
        + jnp.dot(grad_ref[:, 16 * HIGH :], low, preferred_element_type=jnp.float32)
    ).astype(jnp.bfloat16)


def head_gradient(grad, rows):
    return pl.pallas_call(
        grad_kernel,
        out_shape=jax.ShapeDtypeStruct((512, D), jnp.bfloat16),
        grid=(8,),
        in_specs=[
            pl.BlockSpec((512, 1024), lambda i: (0, 0)),
            pl.BlockSpec((2, 1, 4, 2, 64, 896), lambda i: (i % 2, i // 2, 0, 0, 0, 0)),
        ],
        out_specs=pl.BlockSpec((512, 896), lambda i: (0, i)),
        compiler_params=pltpu.CompilerParams(vmem_limit_bytes=40 * 1024 * 1024),
    )(grad, rows)


def kernel_order(values):
    split = values.reshape(4, 2, 2, 64).transpose(1, 0, 2, 3)
    parts = [split[..., :HIGH].reshape(-1), split[..., HIGH:].reshape(-1)]
    return jnp.concatenate(parts).reshape(8, 128)


def body(
    hidden,
    next_ids,
    targets,
    embed_table,
    gain_hidden,
    gain_embed,
    proj_hidden,
    proj_embed,
    gain_final,
    head_weight,
):
    seq_pos = lax.axis_index("seq")
    all_ids, all_targets = (
        lax.all_gather(next_ids, "seq", axis=0, tiled=True),
        lax.all_gather(targets, "seq", axis=0, tiled=True),
    )
    table_rows = embed_table.shape[0]
    local_ids = all_ids - seq_pos * table_rows
    inside = (local_ids >= 0) & (local_ids < table_rows)
    looked_up = jnp.take(embed_table, jnp.clip(local_ids, 0, table_rows - 1), axis=0)
    looked_up = jnp.where(inside[:, None], looked_up, jnp.zeros((), jnp.bfloat16))
    embedded = lax.psum(looked_up, "seq").astype(jnp.float32)
    all_hidden = lax.all_gather(hidden, "seq", axis=0, tiled=True).astype(jnp.float32)
    hidden_sq, embed_sq = lax.psum(
        (jnp.sum(all_hidden * all_hidden, axis=1), jnp.sum(embedded * embedded, axis=1)), "vocab"
    )
    normed_hidden = (all_hidden * lax.rsqrt(hidden_sq / D + EPSILON)[:, None] * gain_hidden).astype(
        jnp.bfloat16
    )
    normed_embed = (embedded * lax.rsqrt(embed_sq / D + EPSILON)[:, None] * gain_embed).astype(
        jnp.bfloat16
    )
    projected = lax.psum_scatter(
        jnp.dot(normed_hidden, proj_hidden, preferred_element_type=jnp.float32)
        + jnp.dot(normed_embed, proj_embed, preferred_element_type=jnp.float32),
        "vocab",
        scatter_dimension=0,
        tiled=True,
    )
    proj_sq = lax.psum(jnp.sum(projected * projected, axis=1), "seq")
    final_rows = (projected * lax.rsqrt(proj_sq / D + EPSILON)[:, None] * gain_final).astype(
        jnp.bfloat16
    )
    grad, loss, rows = head_part(final_rows, head_weight, kernel_order(all_targets))
    return loss[0, 0], head_gradient(grad, rows)


def solution(mesh):
    in_specs = (
        P("seq", "vocab"),
        P("seq"),
        P("seq"),
        P("seq", "vocab"),
        P("vocab"),
        P("vocab"),
        P("vocab", "seq"),
        P("vocab", "seq"),
        P("seq"),
        P(("seq", "vocab"), None),
    )
    out_specs = (P(), P(("seq", "vocab"), None))
    return jax.shard_map(body, mesh=mesh, in_specs=in_specs, out_specs=out_specs, check_vma=False)
```

```python
import jax
import jax.numpy as jnp
from jax import lax
from jax.experimental import pallas as pl
from jax.experimental.pallas import tpu as pltpu
from jax.sharding import PartitionSpec as P

MESH = pl.DeviceIdType.MESH
D = 7168
EPSILON = 1e-06
HIGH, LOW = 48, 16
ORDERS = (((2, 0, 1), (0, 1, 2)), ((2, 1, 0), (1, 0, 2)))
ROWS = ((0, HIGH), (HIGH, LOW))


def coordinates():
    seq, vocab = lax.axis_index("seq"), lax.axis_index("vocab")
    return (
        (2 * lax.rem(seq, 2) + lax.rem(lax.div(vocab, 2), 2), lax.div(seq, 2), lax.div(vocab, 4)),
        lax.rem(vocab, 2),
    )


def device(pos, core):
    x, y, z = pos
    return (2 * y + lax.div(x, 2), 4 * z + 2 * lax.rem(x, 2) + core)


def shifted(pos, axis, by):
    moved = list(pos)
    moved[axis] = lax.rem(pos[axis] + (by + 4), 4)
    return tuple(moved)


def greet(peers):
    barrier = pltpu.get_barrier_semaphore()
    for peer in peers:
        pl.semaphore_signal(barrier, inc=1, device_id=peer, device_id_type=MESH)
    pl.semaphore_wait(barrier, len(peers))


def row_to_columns(row):
    return jnp.transpose(jnp.broadcast_to(row, (128, 128)))


def lane_sums(values):
    total = jnp.zeros((values.shape[0], 128), jnp.float32)
    for first in range(0, values.shape[1], 128):
        total += values[:, first : first + 128] * values[:, first : first + 128]
    return total


def join_kernel(
    hidden_ref, ids_ref, targets_ref, table_ref, gain_hidden_ref, gain_embed_ref,
    proj_hidden_ref, proj_embed_ref, gain_final_ref,
    table, tokens, hidden, embed, gains, parts, relay_in, sums_in, x_out, x_in,
    squares, square_slots, projected, pair_in, z_out, z_relay, z_in, xl_out, xl_in,
    final_squares, final_slots, s_send, s_recv, v_send, v_recv, q_send, q_recv, table_sem,
    vocab_peers, seq_peers, finish_block,
):
    pos, core = coordinates()
    x, y, z = pos
    seq, vocab = lax.axis_index("seq"), lax.axis_index("vocab")
    x_hi, x_lo = lax.div(x, 2), lax.rem(x, 2)
    y_up, y_down, y_far = lax.rem(y + 1, 4), lax.rem(y + 3, 4), lax.rem(y + 2, 4)
    z_up, z_down, z_far = lax.rem(z + 1, 4), lax.rem(z + 3, 4), lax.rem(z + 2, 4)
    to_y_up, to_y_down = (2 * y_up + x_hi, vocab), (2 * y_down + x_hi, vocab)
    to_x = (2 * y + 1 - x_hi, vocab)
    inner = 2 * x_lo + core
    to_z_up, to_z_down = (seq, 4 * z_up + inner), (seq, 4 * z_down + inner)
    to_pair, to_xl = (seq, 4 * z + 2 * x_lo + 1 - core), (seq, 4 * z + 2 * (1 - x_lo) + core)
    sent = []

    def copy_to(source, there, sems, number, to):
        copy = pltpu.make_async_remote_copy(
            src_ref=source, dst_ref=there, send_sem=sems[0].at[number], recv_sem=sems[1].at[number],
            device_id=to, device_id_type=MESH,
        )
        copy.start()
        sent.append(copy)

    def arrived(place, sems, number, to):
        pltpu.make_async_remote_copy(
            src_ref=place, dst_ref=place, send_sem=sems[0].at[number], recv_sem=sems[1].at[number],
            device_id=to, device_id_type=MESH,
        ).wait_recv()

    s_sems, v_sems, q_sems = (s_send, s_recv), (v_send, v_recv), (q_send, q_recv)

    def all_to_all(buffer, me, peers, sems, base):
        for i, peer in enumerate(peers):
            copy_to(buffer.at[me], buffer.at[me], sems, base + i, peer)

    def all_from_all(buffer, me, peers, sems, base):
        count = len(peers) + 1
        for i, peer in enumerate(peers):
            arrived(buffer.at[lax.rem(me - (i + 1) + count, count)], sems, base + i, peer)

    table_copy = pltpu.make_async_copy(table_ref, table, table_sem.at[0])
    table_copy.start()
    tokens[seq, 0:1] = ids_ref[...]
    tokens[seq, 1:2] = targets_ref[...]
    all_to_all(tokens, seq, seq_peers, q_sems, 0)
    hidden[seq] = hidden_ref[...]
    copy_to(hidden.at[seq], hidden.at[seq], s_sems, 0, to_x)
    copy_to(hidden.at[seq], hidden.at[seq], s_sems, 1, to_y_up)
    copy_to(hidden.at[seq], hidden.at[seq], s_sems, 2, to_y_down)
    for which, gain_ref in enumerate((gain_hidden_ref, gain_embed_ref)):
        for first in range(0, 448, 128):
            row = gain_ref[:, first : min(first + 128, 448)]
            if first == 384:
                row = jnp.concatenate([row, jnp.zeros((1, 64), jnp.float32)], axis=1)
            gains[which, first : min(first + 128, 448)] = row_to_columns(row)[: min(448 - first, 128)]
    all_from_all(tokens, seq, seq_peers, q_sems, 0)
    table_copy.wait()

    def look_up(y_at):
        ids = jnp.concatenate([tokens[2 * y_at, 0:1], tokens[2 * y_at + 1, 0:1]], axis=1) - seq * 8192
        total = jnp.zeros((448, 256), jnp.float32)
        for first in range(0, 8192, 1024):
            entries = lax.broadcasted_iota(jnp.int32, (1024, 256), 0) + first
            chosen = jnp.where(entries == ids, 1.0, 0.0).astype(jnp.bfloat16)
            total += jnp.dot(table[:, first : first + 1024], chosen, preferred_element_type=jnp.float32)
        return total.astype(jnp.bfloat16)

    def store_part(y_at, columns):
        for i in range(2):
            parts[y_at, i] = columns[:, 128 * i : 128 * i + 128]

    store_part(y_far, look_up(y_far))
    copy_to(parts.at[y_far, 0], relay_in.at[0], s_sems, 7, to_y_up)
    copy_to(parts.at[y_far, 1], relay_in.at[1], s_sems, 8, to_y_down)

    other = 2 * y + 1 - x_hi
    arrived(hidden.at[other], s_sems, 0, to_x)
    copy_to(hidden.at[other], hidden.at[other], s_sems, 3, to_y_up)
    copy_to(hidden.at[other], hidden.at[other], s_sems, 4, to_y_down)

    store_part(y_up, look_up(y_up))
    arrived(relay_in.at[0], s_sems, 7, to_y_down)
    parts[y_up, 0] += relay_in[0]
    copy_to(parts.at[y_up], sums_in.at[0], s_sems, 9, to_y_up)

    below, above = 2 * y_down + x_hi, 2 * y_up + x_hi
    other_below, other_above = 2 * y_down + 1 - x_hi, 2 * y_up + 1 - x_hi
    far, other_far = 2 * y_far + x_hi, 2 * y_far + 1 - x_hi
    arrived(hidden.at[below], s_sems, 1, to_y_down)
    copy_to(hidden.at[below], hidden.at[below], s_sems, 5, to_y_up)

    store_part(y_down, look_up(y_down))
    arrived(relay_in.at[1], s_sems, 8, to_y_up)
    parts[y_down, 1] += relay_in[1]
    copy_to(parts.at[y_down], sums_in.at[1], s_sems, 10, to_y_down)

    arrived(hidden.at[other_above], s_sems, 4, to_y_up)
    copy_to(hidden.at[other_above], hidden.at[other_above], s_sems, 6, to_y_down)

    own = look_up(y)
    arrived(sums_in.at[0], s_sems, 9, to_y_down)
    arrived(sums_in.at[1], s_sems, 10, to_y_up)
    for i in range(2):
        x_out[i] = own[:, 128 * i : 128 * i + 128] + (sums_in[0, i] + sums_in[1, i])
        copy_to(x_out.at[i], x_in.at[i], s_sems, 11 + i, to_x)

    arrived(hidden.at[above], s_sems, 2, to_y_up)
    arrived(hidden.at[other_below], s_sems, 3, to_y_down)
    arrived(hidden.at[far], s_sems, 5, to_y_down)
    arrived(hidden.at[other_far], s_sems, 6, to_y_up)

    def send_squares(source, which):
        for i in range(8):
            values = source[i].astype(jnp.float32)
            square_slots[which, vocab, i : i + 1] = jnp.sum(values * values, axis=0, keepdims=True)
        slots = square_slots.at[which]
        all_to_all(slots, vocab, vocab_peers, v_sems, 15 * which)

    def scales(which):
        slots = square_slots.at[which]
        all_from_all(slots, vocab, vocab_peers, v_sems, 15 * which)
        squares[which] = lax.rsqrt(jnp.sum(slots[...], axis=0) / D + EPSILON)

    def project(source, which, weight_ref, z_at):
        normed = []
        for i in range(2):
            scale = squares[which, pl.ds(2 * z_at + i, 1)]
            values = source[2 * z_at + i].astype(jnp.float32) * scale * gains[which]
            normed.append(values.astype(jnp.bfloat16))
        return lax.dot_general(
            jnp.concatenate(normed, axis=1), weight_ref[...], (((0,), (0,)), ((), ())),
            preferred_element_type=jnp.float32,
        ).reshape(2, 2, 64, 896)

    send_squares(hidden, 0)
    for i in range(2):
        arrived(x_in.at[i], s_sems, 11 + i, to_x)
        place = embed.at[2 * y + i]
        place[...] = x_out[i] + x_in[i]
        copy_to(place, place, s_sems, 13 + 2 * i, to_y_up)
        copy_to(place, place, s_sems, 14 + 2 * i, to_y_down)
    scales(0)
    z_order = (z_far, z_up, z_down, z)
    for k in range(2):
        projected[k] = project(hidden, 0, proj_hidden_ref, z_order[k])
    arrived(embed.at[2 * y_down], s_sems, 13, to_y_down)
    copy_to(embed.at[2 * y_down], embed.at[2 * y_down], s_sems, 17, to_y_up)
    arrived(embed.at[2 * y_up + 1], s_sems, 16, to_y_up)
    copy_to(embed.at[2 * y_up + 1], embed.at[2 * y_up + 1], s_sems, 18, to_y_down)
    for k in range(2, 4):
        projected[k] = project(hidden, 0, proj_hidden_ref, z_order[k])
    arrived(embed.at[2 * y_up], s_sems, 14, to_y_up)
    arrived(embed.at[2 * y_down + 1], s_sems, 15, to_y_down)
    arrived(embed.at[2 * y_far], s_sems, 17, to_y_down)
    arrived(embed.at[2 * y_far + 1], s_sems, 18, to_y_up)
    send_squares(embed, 1)
    scales(1)

    for k in range(4):
        projected[k] += project(embed, 1, proj_embed_ref, z_order[k])
        copy_to(projected.at[k, :, 1 - core], pair_in.at[k], s_sems, 19 + k, to_pair)

    def with_pair(k):
        arrived(pair_in.at[k], s_sems, 19 + k, to_pair)
        return projected[k, :, core] + pair_in[k]

    z_out[0] = with_pair(0).astype(jnp.bfloat16)
    copy_to(z_out.at[0, 0], z_relay.at[0], s_sems, 23, to_z_up)
    copy_to(z_out.at[0, 1], z_relay.at[1], s_sems, 24, to_z_down)
    for k, (via, to) in ((1, (to_z_down, to_z_up)), (2, (to_z_up, to_z_down))):
        both = with_pair(k)
        arrived(z_relay.at[k - 1], s_sems, 22 + k, via)
        for i in range(2):
            handed = both[i] + z_relay[i].astype(jnp.float32) if i == k - 1 else both[i]
            z_out[k, i] = handed.astype(jnp.bfloat16)
        copy_to(z_out.at[k], z_in.at[k - 1], s_sems, 24 + k, to)
    own = with_pair(3)
    arrived(z_in.at[0], s_sems, 25, to_z_down)
    arrived(z_in.at[1], s_sems, 26, to_z_up)
    projected[3, :, core] = own + (z_in[0].astype(jnp.float32) + z_in[1].astype(jnp.float32))
    xl_out[...] = projected[3, 1 - x_lo, core].astype(jnp.bfloat16)
    copy_to(xl_out, xl_in, s_sems, 27, to_xl)
    arrived(xl_in, s_sems, 27, to_xl)
    total = projected[3, x_lo, core] + xl_in[...].astype(jnp.float32)

    spread = jnp.concatenate([lane_sums(total), jnp.zeros((64, 128), jnp.float32)], axis=0)
    final_slots[seq] = jnp.broadcast_to(jnp.sum(jnp.transpose(spread), axis=0, keepdims=True), (8, 128))
    all_to_all(final_slots, seq, seq_peers, q_sems, 7)
    all_from_all(final_slots, seq, seq_peers, q_sems, 7)
    scale = lax.rsqrt(jnp.sum(final_slots[...], axis=0)[0:1] / D + EPSILON)
    finish_block((total * row_to_columns(scale)[0:64, 0:1] * gain_final_ref[...]).astype(jnp.bfloat16))
    return sent


JOIN_SCRATCH = [
    pltpu.VMEM((448, 8192), jnp.bfloat16),
    pltpu.VMEM((8, 2, 128), jnp.int32),
    pltpu.VMEM((8, 448, 128), jnp.bfloat16),
    pltpu.VMEM((8, 448, 128), jnp.bfloat16),
    pltpu.VMEM((2, 448, 128), jnp.float32),
    pltpu.VMEM((4, 2, 448, 128), jnp.bfloat16),
    pltpu.VMEM((2, 448, 128), jnp.bfloat16),
    pltpu.VMEM((2, 2, 448, 128), jnp.bfloat16),
    pltpu.VMEM((2, 448, 128), jnp.bfloat16),
    pltpu.VMEM((2, 448, 128), jnp.bfloat16),
    pltpu.VMEM((2, 8, 128), jnp.float32),
    pltpu.VMEM((2, 16, 8, 128), jnp.float32),
    pltpu.VMEM((4, 2, 2, 64, 896), jnp.float32),
    pltpu.VMEM((4, 2, 64, 896), jnp.float32),
    pltpu.VMEM((3, 2, 64, 896), jnp.bfloat16),
    pltpu.VMEM((2, 64, 896), jnp.bfloat16),
    pltpu.VMEM((2, 2, 64, 896), jnp.bfloat16),
    pltpu.VMEM((64, 896), jnp.bfloat16),
    pltpu.VMEM((64, 896), jnp.bfloat16),
    pltpu.VMEM((8, 128), jnp.float32),
    pltpu.VMEM((8, 8, 128), jnp.float32),
    pltpu.SemaphoreType.DMA((28,)),
    pltpu.SemaphoreType.DMA((28,)),
    pltpu.SemaphoreType.DMA((30,)),
    pltpu.SemaphoreType.DMA((30,)),
    pltpu.SemaphoreType.DMA((14,)),
    pltpu.SemaphoreType.DMA((14,)),
    pltpu.SemaphoreType.DMA((1,)),
]


def order_targets(tokens, target_ref):
    natural = tokens[:, 1]
    turned = {0: natural}
    lane = lax.broadcasted_iota(jnp.int32, (1, 128), 1)
    for part, (first, count) in enumerate(ROWS):
        for group in range(16):
            vocab = 4 * (group // 2 % 4) + 2 * (group // 8) + group % 2
            start = 16 * first + count * group
            done = 0
            while done < count:
                place, origin = start + done, 64 * vocab + first + done
                to, at = divmod(place, 128)
                size = min(count - done, 128 - at)
                turn = (at - origin) % 128
                if turn not in turned:
                    turned[turn] = pltpu.roll(natural, turn, 1)
                row = turned[turn][origin // 128 : origin // 128 + 1]
                if at == 0:
                    line = row
                else:
                    line = jnp.where(lane < at, line, row)
                if at + size == 128:
                    target_ref[to : to + 1] = line
                done += size


def whole_kernel(*refs):
    inputs, (head_ref, grad_ref, loss_ref, rows_out) = refs[:9], refs[9:13]
    join_scratch = refs[13 : 13 + len(JOIN_SCRATCH)]
    (
        rows, head, scores, stats, vstats, sstats, target_ref,
        ring_send, ring_recv, pair_send, pair_recv, stat_send, stat_recv, local_sem, out_sem,
    ) = refs[13 + len(JOIN_SCRATCH) :]
    pos, core = coordinates()
    seq, vocab = lax.axis_index("seq"), lax.axis_index("vocab")
    x, y, z = pos
    head_copies = [
        pltpu.make_async_copy(
            head_ref.at[:, pl.ds(896 * i, 896)], head.at[i], local_sem.at[i]
        )
        for i in range(8)
    ]
    for copy in head_copies:
        copy.start()
    vocab_peers = [(seq, lax.rem(vocab + i, 16)) for i in range(1, 16)]
    seq_peers = [(lax.rem(seq + i, 8), vocab) for i in range(1, 8)]
    across = device(shifted(pos, 0, 1 - 2 * (1 - lax.rem(x, 2))), core)
    greet(vocab_peers + seq_peers + [across])

    def finish_block(block):
        rows[x, y, z, core] = block

    sent = join_kernel(*inputs, *join_scratch, vocab_peers, seq_peers, finish_block)
    order_targets(join_scratch[1], target_ref)

    def unit(part, at, axis, half=None):
        index = list(at)
        if axis is not None:
            index[axis] = pl.ds(0, 4) if half is None else pl.ds(2 * half, 2)
        return index, ROWS[part]

    def ref_of(where, which):
        index, (first, count) = where
        return rows.at[index[0], index[1], index[2], which, pl.ds(first, count), :]

    def ring(mine, part, number, where, to):
        target = device(to, mine)
        piece = ref_of(where, mine)
        return pltpu.make_async_remote_copy(
            src_ref=piece, dst_ref=piece,
            send_sem=ring_send.at[part, number], recv_sem=ring_recv.at[part, number],
            device_id=target, device_id_type=MESH,
        )

    def pair(part, number, where, which, mine):
        piece = ref_of(where, which)
        return pltpu.make_async_remote_copy(
            src_ref=piece, dst_ref=piece,
            send_sem=pair_send.at[part, number], recv_sem=pair_recv.at[part, number],
            device_id=device(pos, 1 - mine), device_id_type=MESH,
        )

    def line_units(order, part):
        a, b, c = order
        lines = [(1, pos)]
        lines += [(2, shifted(pos, b, -1)), (2, shifted(pos, b, 1)), (3, shifted(pos, b, 2))]
        middles = [lines[i][1] for i in range(4)]
        for j, middle in enumerate(middles):
            lines += [(4 + j, shifted(middle, c, -1)), (4 + j, shifted(middle, c, 1))]
        for j, middle in enumerate(middles):
            lines.append((8 + j, shifted(middle, c, 2)))
        return [(step, unit(part, at, a)) for step, at in lines]

    def own_step(mine, step):
        for part in range(2):
            a, b, c = ORDERS[mine][part]

            def send(number, where, to):
                ring(mine, part, number, where, to).start()

            def recv(number, where):
                ring(mine, part, number, where, pos).wait_recv()

            def up(axis):
                return shifted(pos, axis, 1)

            def down(axis):
                return shifted(pos, axis, -1)

            middles = [pos, down(b), up(b), shifted(pos, b, 2)]

            def spread(j):
                send(7 + 4 * j, unit(part, middles[j], a), up(c))
                send(8 + 4 * j, unit(part, middles[j], a), down(c))

            if step == 0:
                send(0, unit(part, pos, None), up(a))
                send(1, unit(part, pos, None), down(a))
            elif step == 1:
                recv(0, unit(part, down(a), None))
                send(2, unit(part, down(a), None), up(a))
                recv(1, unit(part, up(a), None))
                recv(2, unit(part, shifted(pos, a, 2), None))
                send(3, unit(part, pos, a), up(b))
                send(4, unit(part, pos, a), down(b))
                spread(0)
            elif step == 2:
                recv(3, unit(part, middles[1], a))
                send(5, unit(part, middles[1], a, 0), up(b))
                recv(4, unit(part, middles[2], a))
                send(6, unit(part, middles[2], a, 1), down(b))
                spread(1)
                spread(2)
            elif step == 3:
                recv(5, unit(part, middles[3], a, 0))
                recv(6, unit(part, middles[3], a, 1))
                spread(3)
            elif step < 8:
                j = step - 4
                before, after = shifted(middles[j], c, -1), shifted(middles[j], c, 1)
                recv(7 + 4 * j, unit(part, before, a))
                send(9 + 4 * j, unit(part, before, a, 0), up(c))
                recv(8 + 4 * j, unit(part, after, a))
                send(10 + 4 * j, unit(part, after, a, 1), down(c))
            else:
                j = step - 8
                far = shifted(middles[j], c, 2)
                recv(9 + 4 * j, unit(part, far, a, 0))
                recv(10 + 4 * j, unit(part, far, a, 1))
            for number, (when, where) in enumerate(line_units(ORDERS[mine][part], part)):
                if when == step:
                    pair(part, number, where, mine, mine).start()

    def pair_step(mine, step):
        for part in range(2):
            for number, (when, where) in enumerate(line_units(ORDERS[1 - mine][part], part)):
                if when == step:
                    pair(part, number, where, 1 - mine, mine).wait_recv()

    def by_core(action, step):
        for mine in range(2):

            @pl.when(core == mine)
            def _():
                action(mine, step)

    x_hi = lax.div(x, 2)

    def multiply(dy, other, part):
        y_at = lax.rem(y + dy + 4, 4)
        hi_at = lax.rem(x_hi + other, 2)
        first, count = ROWS[part]
        taken = rows[pl.ds(2 * hi_at, 2), y_at, :, :, pl.ds(first, count), :].reshape(-1, 896)
        product = lax.dot_general(
            head[2 * y_at + hi_at], taken, (((1,), (1,)), ((), ())), preferred_element_type=jnp.float32
        )
        columns = slice(0, 16 * HIGH) if part == 0 else slice(16 * HIGH, 1024)
        if (dy, other) == (0, 0):
            scores[:, columns] = product
        else:
            scores[:, columns] += product

    out_copies = []

    def write_out(dy, other):
        y_at = lax.rem(y + dy + 4, 4)
        hi_at = lax.rem(x_hi + other, 2)
        piece = (pl.ds(2 * hi_at, 2), y_at)
        copy = pltpu.make_async_copy(rows.at[piece], rows_out.at[piece], out_sem.at[len(out_copies)])
        copy.start()
        out_copies.append(copy)

    ready = {
        4: [(0, 0, 0)],
        6: [(-1, 0, 0), (1, 0, 0)],
        8: [(0, 1, 0)],
        9: [(-1, 1, 0)],
        10: [(2, 0, 0), (1, 1, 0), (0, 0, 1), (-1, 0, 1), (1, 0, 1)],
        11: [(2, 1, 0), (2, 0, 1), (0, 1, 1), (-1, 1, 1), (1, 1, 1), (2, 1, 1)],
    }
    for step in range(13):
        if step < 12:
            by_core(own_step, step)
        if step == 3:
            for copy in head_copies:
                copy.wait()
        if step >= 2:
            by_core(pair_step, step - 1)
            for dy, other, part in ready.get(step - 1, []):
                multiply(dy, other, part)
                if part == 1:
                    write_out(dy, other)

    first_entry = (seq * 16 + vocab) * 512
    entries = first_entry + lax.broadcasted_iota(jnp.int32, (512, 128), 0)
    for q in range(8):
        columns = slice(128 * q, 128 * q + 128)
        part = scores[:, columns]
        peak = jnp.max(part, axis=0, keepdims=True)
        matches = entries == target_ref[q : q + 1, :]
        chosen = jnp.sum(jnp.where(matches, part, 0.0), axis=0, keepdims=True)
        powers = jnp.exp(part - peak)
        scores[:, columns] = powers
        stats[0, q : q + 1, :] = peak
        stats[1, q : q + 1, :] = jnp.sum(powers, axis=0, keepdims=True)
        stats[2, q : q + 1, :] = chosen

    def exchange(slots, me, peers, count, base):
        slots[me] = stats[...]
        copies = []
        for i, peer in enumerate(peers):
            copies.append(pltpu.make_async_remote_copy(
                src_ref=stats, dst_ref=slots.at[me],
                send_sem=stat_send.at[base + i], recv_sem=stat_recv.at[base + i],
                device_id=peer, device_id_type=MESH,
            ))
            copies[-1].start()
        for i in range(len(peers)):
            sender = lax.rem(me - (i + 1) + count, count)
            pltpu.make_async_remote_copy(
                src_ref=stats, dst_ref=slots.at[sender],
                send_sem=stat_send.at[base + i], recv_sem=stat_recv.at[base + i],
                device_id=peers[i], device_id_type=MESH,
            ).wait_recv()
        for copy in copies:
            copy.wait_send()
        peaks = slots[:, 0]
        top = jnp.max(peaks, axis=0)
        total = jnp.sum(slots[:, 1] * jnp.exp(peaks - top[None]), axis=0)
        chosen = jnp.sum(slots[:, 2], axis=0)
        return top, total, chosen

    own_peak = stats[0]
    top, total, chosen = exchange(vstats, vocab, vocab_peers, 16, 0)
    stats[0], stats[1], stats[2] = top, total, chosen
    top, total, chosen = exchange(sstats, seq, seq_peers, 8, 15)
    log_total = top + jnp.log(total)
    loss_ref[0, 0] = jnp.sum(log_total - chosen) / 1024
    stats[0] = jnp.exp(own_peak - log_total)
    for q in range(8):
        columns = slice(128 * q, 128 * q + 128)
        matches = entries == target_ref[q : q + 1, :]
        grad = scores[:, columns] * stats[0, q : q + 1, :] - jnp.where(matches, 1.0, 0.0)
        grad_ref[:, columns] = grad.astype(jnp.bfloat16)

    def finish(mine, _):
        for part in range(2):
            a, b, c = ORDERS[mine][part]
            sizes = [(pos, None, None)] * 3 + [(pos, a, None)] * 2 + [(pos, a, 0)] * 2
            sizes += ([(pos, a, None)] * 2 + [(pos, a, 0)] * 2) * 4
            for number, (at, axis, half) in enumerate(sizes):
                ring(mine, part, number, unit(part, at, axis, half), pos).wait_send()
            for number, (_, where) in enumerate(line_units(ORDERS[mine][part], part)):
                pair(part, number, where, mine, mine).wait_send()

    by_core(finish, 0)
    for copy in sent:
        copy.wait_send()
    for copy in out_copies:
        copy.wait()


def whole(*arguments):
    return pl.pallas_call(
        whole_kernel,
        out_shape=(
            jax.ShapeDtypeStruct((512, 1024), jnp.bfloat16),
            jax.ShapeDtypeStruct((1, 1), jnp.float32),
            jax.ShapeDtypeStruct((4, 4, 4, 2, 64, 896), jnp.bfloat16),
        ),
        in_specs=[pl.BlockSpec(memory_space=pltpu.VMEM)] * 3
        + [pl.BlockSpec(memory_space=pl.ANY)]
        + [pl.BlockSpec(memory_space=pltpu.VMEM)] * 5
        + [pl.BlockSpec(memory_space=pl.ANY)],
        out_specs=(
            pl.BlockSpec(memory_space=pltpu.VMEM),
            pl.BlockSpec(memory_space=pltpu.SMEM),
            pl.BlockSpec(memory_space=pl.ANY),
        ),
        scratch_shapes=JOIN_SCRATCH + [
            pltpu.VMEM((4, 4, 4, 2, 64, 896), jnp.bfloat16),
            pltpu.VMEM((8, 512, 896), jnp.bfloat16),
            pltpu.VMEM((512, 1024), jnp.float32),
            pltpu.VMEM((3, 8, 128), jnp.float32),
            pltpu.VMEM((16, 3, 8, 128), jnp.float32),
            pltpu.VMEM((8, 3, 8, 128), jnp.float32),
            pltpu.VMEM((8, 128), jnp.int32),
            pltpu.SemaphoreType.DMA((2, 23)),
            pltpu.SemaphoreType.DMA((2, 23)),
            pltpu.SemaphoreType.DMA((2, 16)),
            pltpu.SemaphoreType.DMA((2, 16)),
            pltpu.SemaphoreType.DMA((22,)),
            pltpu.SemaphoreType.DMA((22,)),
            pltpu.SemaphoreType.DMA((8,)),
            pltpu.SemaphoreType.DMA((8,)),
        ],
        compiler_params=pltpu.CompilerParams(
            collective_id=2, has_side_effects=True, vmem_limit_bytes=60 * 1024 * 1024
        ),
    )(*arguments)


def grad_kernel(grad_ref, rows_ref, out_ref):
    high = rows_ref[:, 0, :, :, 0:HIGH, :].reshape(16 * HIGH, 896)
    low = rows_ref[:, 0, :, :, HIGH:64, :].reshape(16 * LOW, 896)
    out_ref[...] = (
        jnp.dot(grad_ref[:, : 16 * HIGH], high, preferred_element_type=jnp.float32)
        + jnp.dot(grad_ref[:, 16 * HIGH :], low, preferred_element_type=jnp.float32)
    ).astype(jnp.bfloat16)


def head_gradient(grad, rows):
    return pl.pallas_call(
        grad_kernel,
        out_shape=jax.ShapeDtypeStruct((512, D), jnp.bfloat16),
        grid=(8,),
        in_specs=[
            pl.BlockSpec((512, 1024), lambda i: (0, 0)),
            pl.BlockSpec((2, 1, 4, 2, 64, 896), lambda i: (i % 2, i // 2, 0, 0, 0, 0)),
        ],
        out_specs=pl.BlockSpec((512, 896), lambda i: (0, i)),
        compiler_params=pltpu.CompilerParams(vmem_limit_bytes=60 * 1024 * 1024),
    )(grad, rows)


def body(
    hidden,
    next_ids,
    targets,
    embed_table,
    gain_hidden,
    gain_embed,
    proj_hidden,
    proj_embed,
    gain_final,
    head_weight,
):
    grad, loss, rows = whole(
        hidden.T,
        next_ids[None],
        targets[None],
        embed_table.T,
        gain_hidden[None],
        gain_embed[None],
        proj_hidden,
        proj_embed,
        gain_final[None],
        head_weight,
    )
    return loss[0, 0], head_gradient(grad, rows)


def solution(mesh):
    in_specs = (
        P("seq", "vocab"),
        P("seq"),
        P("seq"),
        P("seq", "vocab"),
        P("vocab"),
        P("vocab"),
        P("vocab", "seq"),
        P("vocab", "seq"),
        P("seq"),
        P(("seq", "vocab"), None),
    )
    out_specs = (P(), P(("seq", "vocab"), None))
    return jax.shard_map(body, mesh=mesh, in_specs=in_specs, out_specs=out_specs, check_vma=False)
```

```python
import functools

import jax
import jax.numpy as jnp
from jax import lax
from jax.experimental import pallas as pl
from jax.experimental.pallas import tpu as pltpu
from jax.sharding import PartitionSpec as P

MESH = pl.DeviceIdType.MESH
D = 7168
EPSILON = 1e-06
HIGH, LOW = 48, 16
ORDERS = (((2, 0, 1), (0, 1, 2)), ((2, 1, 0), (1, 0, 2)))
ROWS = ((0, HIGH), (HIGH, LOW))


def coordinates():
    seq, vocab = lax.axis_index("seq"), lax.axis_index("vocab")
    return (
        (2 * lax.rem(seq, 2) + lax.rem(lax.div(vocab, 2), 2), lax.div(seq, 2), lax.div(vocab, 4)),
        lax.rem(vocab, 2),
    )


def device(pos, core):
    x, y, z = pos
    return (2 * y + lax.div(x, 2), 4 * z + 2 * lax.rem(x, 2) + core)


def shifted(pos, axis, by):
    moved = list(pos)
    moved[axis] = lax.rem(pos[axis] + (by + 4), 4)
    return tuple(moved)


def greet(peers):
    barrier = pltpu.get_barrier_semaphore()
    for peer in peers:
        pl.semaphore_signal(barrier, inc=1, device_id=peer, device_id_type=MESH)
    pl.semaphore_wait(barrier, len(peers))


def start_copy(sent, source, there, sems, number, to):
    copy = pltpu.make_async_remote_copy(
        src_ref=source, dst_ref=there, send_sem=sems[0].at[number], recv_sem=sems[1].at[number],
        device_id=to, device_id_type=MESH,
    )
    copy.start()
    sent.append(copy)


def arrived(place, sems, number, to):
    pltpu.make_async_remote_copy(
        src_ref=place, dst_ref=place, send_sem=sems[0].at[number], recv_sem=sems[1].at[number],
        device_id=to, device_id_type=MESH,
    ).wait_recv()


def all_to_all(copy_to, buffer, me, peers, sems, base):
    for i, peer in enumerate(peers):
        copy_to(buffer.at[me], buffer.at[me], sems, base + i, peer)


def all_from_all(buffer, me, peers, sems, base):
    count = len(peers) + 1
    for i, peer in enumerate(peers):
        arrived(buffer.at[lax.rem(me - (i + 1) + count, count)], sems, base + i, peer)


def greet_all(vocab_peers, seq_peers):
    pos, core = coordinates()
    across = device(shifted(pos, 0, 1 - 2 * (1 - lax.rem(pos[0], 2))), core)
    greet(vocab_peers + seq_peers + [across])


def row_to_columns(row):
    return jnp.transpose(jnp.broadcast_to(row, (128, 128)))


def lane_sums(values):
    total = jnp.zeros((values.shape[0], 128), jnp.float32)
    for first in range(0, values.shape[1], 128):
        total += values[:, first : first + 128] * values[:, first : first + 128]
    return total


def join_kernel(
    hidden_ref, ids_ref, targets_ref, table_ref, gain_hidden_ref, gain_embed_ref,
    proj_hidden_ref, proj_embed_ref, gain_final_ref,
    table, tokens, hidden, embed, gains, parts, sums_in, square_slots, scale_slots,
    projected, pair_in, z_out, z_in,
    h_send, h_recv, r_send, r_recv, g_send, g_recv, v_send, v_recv, q_send, q_recv,
    p_send, p_recv, z_send, z_recv, table_sem,
    vocab_peers, seq_peers,
):
    pos, core = coordinates()
    x, y, z = pos
    seq, vocab = lax.axis_index("seq"), lax.axis_index("vocab")
    x_hi, x_lo = lax.div(x, 2), lax.rem(x, 2)
    y_up, y_down = lax.rem(y + 1, 4), lax.rem(y + 3, 4)
    to_y_up, to_y_down = (2 * y_up + x_hi, vocab), (2 * y_down + x_hi, vocab)
    to_x = (2 * y + 1 - x_hi, vocab)
    to_pair = (seq, 4 * z + 2 * x_lo + 1 - core)
    sent = []
    copy_to = functools.partial(start_copy, sent)
    h_sems, r_sems, g_sems = (h_send, h_recv), (r_send, r_recv), (g_send, g_recv)
    v_sems, q_sems = (v_send, v_recv), (q_send, q_recv)
    p_sems, z_sems = (p_send, p_recv), (z_send, z_recv)

    table_copy = pltpu.make_async_copy(table_ref, table, table_sem.at[0])
    table_copy.start()
    tokens[seq, 0:1] = ids_ref[...]
    tokens[seq, 1:2] = targets_ref[...]
    greet_all(vocab_peers, seq_peers)
    all_to_all(copy_to, tokens, seq, seq_peers, q_sems, 0)
    hidden[seq] = hidden_ref[...]
    copy_to(hidden.at[seq], hidden.at[seq], h_sems, 0, to_x)
    copy_to(hidden.at[seq], hidden.at[seq], h_sems, 1, to_y_up)
    copy_to(hidden.at[seq], hidden.at[seq], h_sems, 2, to_y_down)

    def start_scale(which, block):
        values = block.astype(jnp.float32)
        total = jnp.sum(values * values, axis=0, keepdims=True)
        square_slots[which, vocab] = jnp.broadcast_to(total, (8, 128))
        all_to_all(copy_to, square_slots.at[which], vocab, vocab_peers, v_sems, 15 * which)

    def spread_scale(which):
        all_from_all(square_slots.at[which], vocab, vocab_peers, v_sems, 15 * which)
        total = jnp.sum(square_slots[which], axis=0)
        scale_slots[which, seq] = lax.rsqrt(total / D + EPSILON)
        all_to_all(copy_to, scale_slots.at[which], seq, seq_peers, q_sems, 7 + 7 * which)

    def end_scale(which):
        all_from_all(scale_slots.at[which], seq, seq_peers, q_sems, 7 + 7 * which)

    start_scale(0, hidden_ref[...])
    for which, gain_ref in enumerate((gain_hidden_ref, gain_embed_ref)):
        for first in range(0, 448, 128):
            row = gain_ref[:, first : min(first + 128, 448)]
            if first == 384:
                row = jnp.concatenate([row, jnp.zeros((1, 64), jnp.float32)], axis=1)
            gains[which, first : min(first + 128, 448)] = row_to_columns(row)[: min(448 - first, 128)]
    all_from_all(tokens, seq, seq_peers, q_sems, 0)
    table_copy.wait()

    def look_up(y_at):
        ids = jnp.concatenate([tokens[2 * y_at, 0:1], tokens[2 * y_at + 1, 0:1]], axis=1) - seq * 8192
        total = jnp.zeros((448, 256), jnp.float32)
        for first in range(0, 8192, 1024):
            entries = lax.broadcasted_iota(jnp.int32, (1024, 256), 0) + first
            chosen = jnp.where(entries == ids, 1.0, 0.0).astype(jnp.bfloat16)
            total += jnp.dot(table[:, first : first + 1024], chosen, preferred_element_type=jnp.float32)
        return total.astype(jnp.bfloat16)

    def near_or_other(e):
        return x_hi if e == 0 else 1 - x_hi

    def seq_at(number):
        return 2 * lax.rem(y + number // 2, 4) + near_or_other(number % 2)

    def look_up_and_send(dy):
        y_at = lax.rem(y + dy, 4)
        found = look_up(y_at)
        for i in range(2):
            parts[y_at, i] = found[:, 128 * i : 128 * i + 128]
        for e in range(2):
            number = 2 * dy + e
            if number:
                source = parts.at[y_at, near_or_other(e)]
                copy_to(source, sums_in.at[number], r_sems, number, (seq_at(number), vocab))

    other = 2 * y + 1 - x_hi
    below, above = 2 * y_down + x_hi, 2 * y_up + x_hi
    other_below, other_above = 2 * y_down + 1 - x_hi, 2 * y_up + 1 - x_hi
    far, other_far = seq_at(4), seq_at(5)
    look_up_and_send(2)
    arrived(hidden.at[other], h_sems, 0, to_x)
    copy_to(hidden.at[other], hidden.at[other], h_sems, 3, to_y_up)
    copy_to(hidden.at[other], hidden.at[other], h_sems, 4, to_y_down)
    arrived(hidden.at[below], h_sems, 1, to_y_down)
    copy_to(hidden.at[below], hidden.at[below], h_sems, 5, to_y_up)
    spread_scale(0)
    look_up_and_send(1)
    look_up_and_send(3)
    arrived(hidden.at[other_above], h_sems, 4, to_y_up)
    copy_to(hidden.at[other_above], hidden.at[other_above], h_sems, 6, to_y_down)
    look_up_and_send(0)
    total = parts[y, x_hi]
    for number in range(1, 8):
        arrived(sums_in.at[number], r_sems, number, to_x)
        total += sums_in[number]
    embed[seq] = total
    for number in range(1, 8):
        copy_to(embed.at[seq], embed.at[seq], g_sems, number, (seq_at(number), vocab))
    start_scale(1, total)

    def project(source, which, weight_ref, z_at):
        normed = []
        for i in range(2):
            values = source[2 * z_at + i].astype(jnp.float32) * scale_slots[which, 2 * z_at + i, 0:1]
            normed.append((values * gains[which]).astype(jnp.bfloat16))
        return lax.dot_general(
            jnp.concatenate(normed, axis=1), weight_ref[...], (((0,), (0,)), ((), ())),
            preferred_element_type=jnp.float32,
        ).reshape(2, 2, 64, 896)

    arrived(hidden.at[above], h_sems, 2, to_y_up)
    arrived(hidden.at[other_below], h_sems, 3, to_y_down)
    arrived(hidden.at[far], h_sems, 5, to_y_down)
    arrived(hidden.at[other_far], h_sems, 6, to_y_up)
    end_scale(0)
    distances = (2, 1, 3, 0)
    for k in range(4):
        projected[k] = project(hidden, 0, proj_hidden_ref, lax.rem(z + distances[k], 4))
        if k == 1:
            spread_scale(1)
    for number in range(1, 8):
        sender = 2 * lax.rem(y + 4 - number // 2, 4) + near_or_other(number % 2)
        arrived(embed.at[sender], g_sems, number, to_x)
    end_scale(1)

    def hand_on(k):
        arrived(pair_in.at[k], p_sems, k, to_pair)
        both = projected[k, :, core] + pair_in[k]
        z_out[k] = both.astype(jnp.bfloat16)
        dz = distances[k]
        for e in range(2):
            number = 2 * dz + e
            x_at = x_lo if e == 0 else 1 - x_lo
            if number:
                to = (seq, 4 * lax.rem(z + dz, 4) + 2 * x_at + core)
                copy_to(z_out.at[k, x_at], z_in.at[number], z_sems, number, to)
            else:
                projected[k, :, core] = both

    for k in range(4):
        projected[k] += project(embed, 1, proj_embed_ref, lax.rem(z + distances[k], 4))
        copy_to(projected.at[k, :, 1 - core], pair_in.at[k], p_sems, k, to_pair)
        if k:
            hand_on(k - 1)
    hand_on(3)
    total = projected[3, x_lo, core]
    for number in range(1, 8):
        arrived(z_in.at[number], z_sems, number, to_pair)
        total += z_in[number].astype(jnp.float32)
    return total, sent


JOIN_SCRATCH = [
    pltpu.VMEM((448, 8192), jnp.bfloat16),
    pltpu.VMEM((8, 2, 128), jnp.int32),
    pltpu.VMEM((8, 448, 128), jnp.bfloat16),
    pltpu.VMEM((8, 448, 128), jnp.bfloat16),
    pltpu.VMEM((2, 448, 128), jnp.float32),
    pltpu.VMEM((4, 2, 448, 128), jnp.bfloat16),
    pltpu.VMEM((8, 448, 128), jnp.bfloat16),
    pltpu.VMEM((2, 16, 8, 128), jnp.float32),
    pltpu.VMEM((2, 8, 8, 128), jnp.float32),
    pltpu.VMEM((4, 2, 2, 64, 896), jnp.float32),
    pltpu.VMEM((4, 2, 64, 896), jnp.float32),
    pltpu.VMEM((4, 2, 64, 896), jnp.bfloat16),
    pltpu.VMEM((8, 64, 896), jnp.bfloat16),
    *[pltpu.SemaphoreType.DMA((count,)) for count in (7, 7, 8, 8, 8, 8, 30, 30, 21, 21, 4, 4, 8, 8)],
    pltpu.SemaphoreType.DMA((1,)),
]


def to_score_order(natural, ordered):
    turned = {0: natural}
    lane = lax.broadcasted_iota(jnp.int32, (1, 128), 1)
    for part, (first, count) in enumerate(ROWS):
        for group in range(16):
            vocab = 4 * (group // 2 % 4) + 2 * (group // 8) + group % 2
            start = 16 * first + count * group
            done = 0
            while done < count:
                place, origin = start + done, 64 * vocab + first + done
                to, at = divmod(place, 128)
                size = min(count - done, 128 - at)
                turn = (at - origin) % 128
                if turn not in turned:
                    turned[turn] = pltpu.roll(natural, turn, 1)
                row = turned[turn][origin // 128 : origin // 128 + 1]
                if at == 0:
                    line = row
                else:
                    line = jnp.where(lane < at, line, row)
                if at + size == 128:
                    ordered[to : to + 1] = line
                done += size


def whole_kernel(*refs):
    inputs, (head_ref, grad_ref, loss_ref, rows) = refs[:9], refs[9:13]
    join_scratch = refs[13 : 13 + len(JOIN_SCRATCH)]
    (
        head, scores, stats, vocab_stats, seq_stats, targets, scales, final_slots, row_slots,
        ring_send, ring_recv, pair_send, pair_recv, stat_send, stat_recv, f_send, f_recv, local_sem,
    ) = refs[13 + len(JOIN_SCRATCH) :]
    pos, core = coordinates()
    seq, vocab = lax.axis_index("seq"), lax.axis_index("vocab")
    x, y, z = pos
    head_copies = [
        pltpu.make_async_copy(
            head_ref.at[:, pl.ds(896 * i, 896)], head.at[i], local_sem.at[i]
        )
        for i in range(8)
    ]
    for copy in head_copies:
        copy.start()
    vocab_peers = [(seq, lax.rem(vocab + i, 16)) for i in range(1, 16)]
    seq_peers = [(lax.rem(seq + i, 8), vocab) for i in range(1, 8)]
    total, sent = join_kernel(*inputs, *join_scratch, vocab_peers, seq_peers)
    copy_to = functools.partial(start_copy, sent)
    f_sems, stat_sems = (f_send, f_recv), (stat_send, stat_recv)

    gain = jnp.concatenate([inputs[8][i : i + 1] for i in range(7)], axis=1)
    rows[x, y, z, core] = (total * gain).astype(jnp.bfloat16)

    def start_scale():
        spread = jnp.concatenate([lane_sums(total), jnp.zeros((64, 128), jnp.float32)], axis=0)
        squares = jnp.sum(jnp.transpose(spread), axis=0, keepdims=True)
        final_slots[seq] = jnp.broadcast_to(squares, (8, 128))
        all_to_all(copy_to, final_slots, seq, seq_peers, f_sems, 0)

    def spread_scale():
        all_from_all(final_slots, seq, seq_peers, f_sems, 0)
        row_slots[vocab] = lax.rsqrt(jnp.sum(final_slots[...], axis=0) / D + EPSILON)
        all_to_all(copy_to, row_slots, vocab, vocab_peers, f_sems, 7)

    def end_scale():
        all_from_all(row_slots, vocab, vocab_peers, f_sems, 7)
        lane = lax.broadcasted_iota(jnp.int32, (1, 128), 1)
        natural = []
        for i in range(8):
            later = pltpu.roll(row_slots[2 * i + 1], 64, 1)[0:1]
            natural.append(jnp.where(lane < 64, row_slots[2 * i, 0:1], later))
        to_score_order(jnp.concatenate(natural, axis=0), scales)

    def unit(part, at, axis, half=None):
        index = list(at)
        if axis is not None:
            index[axis] = pl.ds(0, 4) if half is None else pl.ds(2 * half, 2)
        return index, ROWS[part]

    def ref_of(where, which):
        index, (first, count) = where
        return rows.at[index[0], index[1], index[2], which, pl.ds(first, count), :]

    def ring(mine, part, number, where, to):
        target = device(to, mine)
        piece = ref_of(where, mine)
        return pltpu.make_async_remote_copy(
            src_ref=piece, dst_ref=piece,
            send_sem=ring_send.at[part, number], recv_sem=ring_recv.at[part, number],
            device_id=target, device_id_type=MESH,
        )

    def pair(part, number, where, which, mine):
        piece = ref_of(where, which)
        return pltpu.make_async_remote_copy(
            src_ref=piece, dst_ref=piece,
            send_sem=pair_send.at[part, number], recv_sem=pair_recv.at[part, number],
            device_id=device(pos, 1 - mine), device_id_type=MESH,
        )

    def line_units(order, part):
        a, b, c = order
        lines = [(1, pos)]
        lines += [(2, shifted(pos, b, -1)), (2, shifted(pos, b, 1)), (3, shifted(pos, b, 2))]
        middles = [lines[i][1] for i in range(4)]
        for j, middle in enumerate(middles):
            lines += [(4 + j, shifted(middle, c, -1)), (4 + j, shifted(middle, c, 1))]
        for j, middle in enumerate(middles):
            lines.append((8 + j, shifted(middle, c, 2)))
        return [(step, unit(part, at, a)) for step, at in lines]

    def own_step(mine, step):
        for part in range(2):
            a, b, c = ORDERS[mine][part]

            def send(number, where, to):
                ring(mine, part, number, where, to).start()

            def recv(number, where):
                ring(mine, part, number, where, pos).wait_recv()

            def up(axis):
                return shifted(pos, axis, 1)

            def down(axis):
                return shifted(pos, axis, -1)

            middles = [pos, down(b), up(b), shifted(pos, b, 2)]

            def spread(j):
                send(7 + 4 * j, unit(part, middles[j], a), up(c))
                send(8 + 4 * j, unit(part, middles[j], a), down(c))

            if step == 0:
                send(0, unit(part, pos, None), up(a))
                send(1, unit(part, pos, None), down(a))
            elif step == 1:
                recv(0, unit(part, down(a), None))
                send(2, unit(part, down(a), None), up(a))
                recv(1, unit(part, up(a), None))
                recv(2, unit(part, shifted(pos, a, 2), None))
                send(3, unit(part, pos, a), up(b))
                send(4, unit(part, pos, a), down(b))
                spread(0)
            elif step == 2:
                recv(3, unit(part, middles[1], a))
                send(5, unit(part, middles[1], a, 0), up(b))
                recv(4, unit(part, middles[2], a))
                send(6, unit(part, middles[2], a, 1), down(b))
                spread(1)
                spread(2)
            elif step == 3:
                recv(5, unit(part, middles[3], a, 0))
                recv(6, unit(part, middles[3], a, 1))
                spread(3)
            elif step < 8:
                j = step - 4
                before, after = shifted(middles[j], c, -1), shifted(middles[j], c, 1)
                recv(7 + 4 * j, unit(part, before, a))
                send(9 + 4 * j, unit(part, before, a, 0), up(c))
                recv(8 + 4 * j, unit(part, after, a))
                send(10 + 4 * j, unit(part, after, a, 1), down(c))
            else:
                j = step - 8
                far = shifted(middles[j], c, 2)
                recv(9 + 4 * j, unit(part, far, a, 0))
                recv(10 + 4 * j, unit(part, far, a, 1))
            for number, (when, where) in enumerate(line_units(ORDERS[mine][part], part)):
                if when == step:
                    pair(part, number, where, mine, mine).start()

    def pair_step(mine, step):
        for part in range(2):
            for number, (when, where) in enumerate(line_units(ORDERS[1 - mine][part], part)):
                if when == step:
                    pair(part, number, where, 1 - mine, mine).wait_recv()

    def by_core(action, step):
        for mine in range(2):

            @pl.when(core == mine)
            def _():
                action(mine, step)

    x_hi = lax.div(x, 2)

    def multiply(dy, other, part):
        y_at = lax.rem(y + dy + 4, 4)
        hi_at = lax.rem(x_hi + other, 2)
        first, count = ROWS[part]
        taken = rows[pl.ds(2 * hi_at, 2), y_at, :, :, pl.ds(first, count), :].reshape(-1, 896)
        product = lax.dot_general(
            head[2 * y_at + hi_at], taken, (((1,), (1,)), ((), ())), preferred_element_type=jnp.float32
        )
        columns = slice(0, 16 * HIGH) if part == 0 else slice(16 * HIGH, 1024)
        if (dy, other) == (0, 0):
            scores[:, columns] = product
        else:
            scores[:, columns] += product

    ready = {
        4: [(0, 0, 0)],
        6: [(-1, 0, 0), (1, 0, 0)],
        8: [(0, 1, 0)],
        9: [(-1, 1, 0)],
        10: [(2, 0, 0), (1, 1, 0), (0, 0, 1), (-1, 0, 1), (1, 0, 1)],
        11: [(2, 1, 0), (2, 0, 1), (0, 1, 1), (-1, 1, 1), (1, 1, 1), (2, 1, 1)],
    }
    for step in range(13):
        if step < 12:
            by_core(own_step, step)
        if step == 0:
            start_scale()
            to_score_order(join_scratch[1][:, 1], targets)
        elif step == 2:
            spread_scale()
        elif step == 3:
            for copy in head_copies:
                copy.wait()
        elif step == 5:
            end_scale()
        if step >= 2:
            by_core(pair_step, step - 1)
            for dy, other, part in ready.get(step - 1, []):
                multiply(dy, other, part)

    first_entry = (seq * 16 + vocab) * 512
    entries = first_entry + lax.broadcasted_iota(jnp.int32, (512, 128), 0)
    for q in range(8):
        columns = slice(128 * q, 128 * q + 128)
        part = scores[:, columns] * scales[q : q + 1]
        peak = jnp.max(part, axis=0, keepdims=True)
        matches = entries == targets[q : q + 1]
        powers = jnp.exp(part - peak)
        scores[:, columns] = powers
        stats[0, q : q + 1] = peak + jnp.log(jnp.sum(powers, axis=0, keepdims=True))
        stats[1, q : q + 1] = jnp.sum(jnp.where(matches, part, 0.0), axis=0, keepdims=True)
        stats[2, q : q + 1] = peak

    def combine(slots):
        logs = slots[:, 0]
        top = jnp.max(logs, axis=0)
        return top + jnp.log(jnp.sum(jnp.exp(logs - top[None]), axis=0)), jnp.sum(slots[:, 1], axis=0)

    vocab_stats[vocab] = stats[0:2]
    all_to_all(copy_to, vocab_stats, vocab, vocab_peers, stat_sems, 0)
    all_from_all(vocab_stats, vocab, vocab_peers, stat_sems, 0)
    seq_stats[seq, 0], seq_stats[seq, 1] = combine(vocab_stats)
    all_to_all(copy_to, seq_stats, seq, seq_peers, stat_sems, 15)
    all_from_all(seq_stats, seq, seq_peers, stat_sems, 15)
    log_total, chosen = combine(seq_stats)
    loss_ref[0, 0] = jnp.sum(log_total - chosen) / 1024
    stats[0] = jnp.exp(stats[2] - log_total)
    for q in range(8):
        columns = slice(128 * q, 128 * q + 128)
        matches = entries == targets[q : q + 1]
        grad = scores[:, columns] * stats[0, q : q + 1] - jnp.where(matches, 1.0, 0.0)
        grad_ref[:, columns] = (grad * scales[q : q + 1]).astype(jnp.bfloat16)

    def finish(mine, _):
        for part in range(2):
            a, b, c = ORDERS[mine][part]
            sizes = [(pos, None, None)] * 3 + [(pos, a, None)] * 2 + [(pos, a, 0)] * 2
            sizes += ([(pos, a, None)] * 2 + [(pos, a, 0)] * 2) * 4
            for number, (at, axis, half) in enumerate(sizes):
                ring(mine, part, number, unit(part, at, axis, half), pos).wait_send()
            for number, (_, where) in enumerate(line_units(ORDERS[mine][part], part)):
                pair(part, number, where, mine, mine).wait_send()

    by_core(finish, 0)
    for copy in sent:
        copy.wait_send()


def whole(*arguments):
    return pl.pallas_call(
        whole_kernel,
        out_shape=(
            pltpu.VMEM((512, 1024), jnp.bfloat16),
            jax.ShapeDtypeStruct((1, 1), jnp.float32),
            pltpu.VMEM((4, 4, 4, 2, 64, 896), jnp.bfloat16),
        ),
        in_specs=[pl.BlockSpec(memory_space=pltpu.VMEM)] * 3
        + [pl.BlockSpec(memory_space=pl.ANY)]
        + [pl.BlockSpec(memory_space=pltpu.VMEM)] * 5
        + [pl.BlockSpec(memory_space=pl.ANY)],
        out_specs=(
            pl.BlockSpec(memory_space=pltpu.VMEM),
            pl.BlockSpec(memory_space=pltpu.SMEM),
            pl.BlockSpec(memory_space=pltpu.VMEM),
        ),
        scratch_shapes=JOIN_SCRATCH + [
            pltpu.VMEM((8, 512, 896), jnp.bfloat16),
            pltpu.VMEM((512, 1024), jnp.float32),
            pltpu.VMEM((3, 8, 128), jnp.float32),
            pltpu.VMEM((16, 2, 8, 128), jnp.float32),
            pltpu.VMEM((8, 2, 8, 128), jnp.float32),
            pltpu.VMEM((8, 128), jnp.int32),
            pltpu.VMEM((8, 128), jnp.float32),
            pltpu.VMEM((8, 8, 128), jnp.float32),
            pltpu.VMEM((16, 8, 128), jnp.float32),
            pltpu.SemaphoreType.DMA((2, 23)),
            pltpu.SemaphoreType.DMA((2, 23)),
            pltpu.SemaphoreType.DMA((2, 16)),
            pltpu.SemaphoreType.DMA((2, 16)),
            pltpu.SemaphoreType.DMA((22,)),
            pltpu.SemaphoreType.DMA((22,)),
            pltpu.SemaphoreType.DMA((22,)),
            pltpu.SemaphoreType.DMA((22,)),
            pltpu.SemaphoreType.DMA((8,)),
        ],
        compiler_params=pltpu.CompilerParams(
            collective_id=2, has_side_effects=True, vmem_limit_bytes=44 * 1024 * 1024
        ),
    )(*arguments)


def grad_kernel(grad_ref, rows_ref, out_ref):
    y_at, hi_at = lax.div(pl.program_id(0), 2), lax.rem(pl.program_id(0), 2)
    high = rows_ref[pl.ds(2 * hi_at, 2), y_at, :, :, 0:HIGH, :].reshape(16 * HIGH, 896)
    low = rows_ref[pl.ds(2 * hi_at, 2), y_at, :, :, HIGH:64, :].reshape(16 * LOW, 896)
    out_ref[...] = (
        jnp.dot(grad_ref[:, : 16 * HIGH], high, preferred_element_type=jnp.float32)
        + jnp.dot(grad_ref[:, 16 * HIGH :], low, preferred_element_type=jnp.float32)
    ).astype(jnp.bfloat16)


def head_gradient(grad, rows):
    return pl.pallas_call(
        grad_kernel,
        out_shape=jax.ShapeDtypeStruct((512, D), jnp.bfloat16),
        grid=(8,),
        in_specs=[pl.BlockSpec(memory_space=pltpu.VMEM)] * 2,
        out_specs=pl.BlockSpec((512, 896), lambda i: (0, i)),
        compiler_params=pltpu.CompilerParams(vmem_limit_bytes=24 * 1024 * 1024),
    )(pltpu.with_memory_space_constraint(grad, pltpu.VMEM), pltpu.with_memory_space_constraint(rows, pltpu.VMEM))


def body(
    hidden,
    next_ids,
    targets,
    embed_table,
    gain_hidden,
    gain_embed,
    proj_hidden,
    proj_embed,
    gain_final,
    head_weight,
):
    grad, loss, rows = whole(
        hidden.T,
        next_ids[None],
        targets[None],
        embed_table.T,
        gain_hidden[None],
        gain_embed[None],
        proj_hidden,
        proj_embed,
        gain_final.reshape(7, 128),
        head_weight,
    )
    return loss[0, 0], head_gradient(grad, rows)


def solution(mesh):
    in_specs = (
        P("seq", "vocab"),
        P("seq"),
        P("seq"),
        P("seq", "vocab"),
        P("vocab"),
        P("vocab"),
        P("vocab", "seq"),
        P("vocab", "seq"),
        P("seq"),
        P(("seq", "vocab"), None),
    )
    out_specs = (P(), P(("seq", "vocab"), None))
    return jax.shard_map(body, mesh=mesh, in_specs=in_specs, out_specs=out_specs, check_vma=False)
```

```python
import functools

import jax
import jax.numpy as jnp
from jax import lax
from jax.experimental import pallas as pl
from jax.experimental.pallas import tpu as pltpu
from jax.sharding import PartitionSpec as P

MESH = pl.DeviceIdType.MESH
D = 7168
EPSILON = 1e-06
COLUMNS = ((0, 640), (640, 256))
ORDERS = (((0, 2, 1), (0, 1, 2)), ((1, 2, 0), (1, 0, 2)))
OUTSTANDING = 2
NEAR_Z = ((0, 3), (1, 2))
SCHEDULE = (
    (
        (9, 261, 2, 254, 7, 259, 45, 14, 189, 62),
        (9, 261, 2, 254, 7, 259, 45, 14, 189, 62),
        (64,),
    ),
    (
        (260, 252, 44, 12, 29, 237, 205, 110, 78, 256, 309, 278),
        (44, 12, 260, 252, 29, 237, 205, 110, 78, 256, 309, 278),
        (65,),
    ),
    (
        (8, 0, 188, 60, 26, 273, 201, 266, 74, 4, 57, 193, 66, 236, 204, 108, 76, 125, 70, 18, 197, 174, 22, 28, 200,
         72, 49, 53, 141, 94, 221, 138, 272, 264, 24),
        (188, 60, 8, 0, 26, 273, 125, 266, 74, 4, 57, 201, 66, 236, 204, 108, 76, 193, 70, 18, 197, 174, 22, 28, 124,
         72, 49, 53, 141, 94, 221, 138, 272, 264, 24),
        (66,),
    ),
    (
        (192, 64, 276, 269, 90, 42, 217, 290, 308, 56, 124, 68, 122, 134, 196, 172, 321, 313, 129),
        (200, 64, 276, 269, 90, 42, 217, 290, 308, 192, 68, 56, 134, 122, 196, 172, 321, 313, 129),
        (32, 36),
    ),
    (
        (140, 92, 158, 249, 16, 82, 220, 136, 20, 38, 88, 209, 48, 86, 52, 213, 154, 216, 120, 268, 132, 241, 114),
        (140, 92, 158, 249, 16, 82, 220, 136, 20, 38, 88, 209, 48, 86, 52, 213, 154, 216, 132, 268, 120, 241, 114),
        (0, 4),
    ),
    (
        (245, 282, 40, 118, 128, 156, 248, 33, 293, 286, 233, 80, 106, 185, 208, 84, 150, 212, 288, 145, 152, 320,
         312, 36, 229, 102, 240, 112, 178, 244, 317, 181, 116),
        (245, 282, 40, 118, 128, 156, 248, 33, 293, 286, 233, 80, 106, 185, 208, 84, 150, 212, 288, 145, 152, 320,
         312, 36, 229, 102, 240, 112, 178, 244, 317, 181, 116),
        (56, 60, 33, 40, 41, 44, 49, 57),
    ),
    (
        (104, 306, 232, 169, 184),
        (104, 306, 232, 169, 184),
        (24, 28),
    ),
    (
        (148, 297),
        (148, 297),
        (1, 8, 9, 12, 17, 25),
    ),
    (
        (32, 144, 225, 98, 100, 228, 176, 165, 280, 180),
        (144, 32, 225, 98, 100, 228, 176, 165, 280, 180),
        (2, 6),
    ),
    (
        (292, 284, 302, 168),
        (292, 284, 302, 168),
        (5, 13, 16, 20, 21, 29),
    ),
    (
        (224, 96, 162),
        (224, 96, 162),
        (34, 38),
    ),
    (
        (304, 164),
        (304, 164),
        (3, 10, 11, 14, 19, 26, 27, 30),
    ),
    (
        (316,),
        (316,),
        (58, 62),
    ),
    (
        (296, 160),
        (296, 160),
        (37, 45, 48, 52, 53, 61),
    ),
    (
        (300,),
        (300,),
        (35, 42, 43, 46, 51, 59),
    ),
    (
        (),
        (),
        (7, 15, 18, 22, 23, 31),
    ),
    (
        (),
        (),
        (39, 47, 50, 54, 55, 63),
    ),
)


def received(number):
    if number < 63:
        if number < 3:
            return 0, 1, (number + 1, 0, 0)
        if number < 15:
            return 0, 2, ((number - 3) % 4, (number - 3) // 4 + 1, 0)
        return 0, 3, ((number - 15) % 4, (number - 15) // 4 % 4, (number - 15) // 16 + 1)
    number -= 63
    if number < 3:
        return 1, 1, (number + 1, 0, 0)
    if number < 6:
        return 1, 2, (4, number - 2, 0)
    return 1, 3, (4, (number - 6) % 4, (number - 6) // 4 + 1)


def coordinates():
    seq, vocab = lax.axis_index("seq"), lax.axis_index("vocab")
    return (
        (2 * lax.rem(seq, 2) + lax.rem(lax.div(vocab, 2), 2), lax.div(seq, 2), lax.div(vocab, 4)),
        lax.rem(vocab, 2),
    )


def device(pos, core):
    x, y, z = pos
    return (2 * y + lax.div(x, 2), 4 * z + 2 * lax.rem(x, 2) + core)


def shifted(pos, axis, by):
    moved = list(pos)
    moved[axis] = lax.rem(pos[axis] + (by + 4), 4)
    return tuple(moved)


def greet(peers):
    barrier = pltpu.get_barrier_semaphore()
    for peer in peers:
        pl.semaphore_signal(barrier, inc=1, device_id=peer, device_id_type=MESH)
    pl.semaphore_wait(barrier, len(peers))


def start_copy(sent, source, there, sems, number, to):
    copy = pltpu.make_async_remote_copy(
        src_ref=source, dst_ref=there, send_sem=sems[0].at[number], recv_sem=sems[1].at[number],
        device_id=to, device_id_type=MESH,
    )
    copy.start()
    sent.append(copy)


def arrived(place, sems, number, to):
    pltpu.make_async_remote_copy(
        src_ref=place, dst_ref=place, send_sem=sems[0].at[number], recv_sem=sems[1].at[number],
        device_id=to, device_id_type=MESH,
    ).wait_recv()


def all_to_all(copy_to, buffer, me, peers, sems, base):
    for i, peer in enumerate(peers):
        copy_to(buffer.at[me], buffer.at[me], sems, base + i, peer)


def all_from_all(buffer, me, peers, sems, base):
    count = len(peers) + 1
    for i, peer in enumerate(peers):
        arrived(buffer.at[lax.rem(me - (i + 1) + count, count)], sems, base + i, peer)


def greet_all(vocab_peers, seq_peers):
    pos, core = coordinates()
    across = device(shifted(pos, 0, 1 - 2 * (1 - lax.rem(pos[0], 2))), core)
    greet(vocab_peers + seq_peers + [across])


def row_to_columns(row):
    return jnp.transpose(jnp.broadcast_to(row, (128, 128)))


def lane_sums(values):
    total = jnp.zeros((values.shape[0], 128), jnp.float32)
    for first in range(0, values.shape[1], 128):
        total += values[:, first : first + 128] * values[:, first : first + 128]
    return total


def join_kernel(
    hidden_ref, ids_ref, targets_ref, table_ref, gain_hidden_ref, gain_embed_ref,
    proj_hidden_ref, proj_embed_ref, gain_final_ref,
    table, tokens, hidden, embed, gains, parts, sums_in, square_slots, scale_slots,
    projected, pair_in, z_out, z_in,
    h_send, h_recv, r_send, r_recv, g_send, g_recv, v_send, v_recv, q_send, q_recv,
    p_send, p_recv, z_send, z_recv, table_sem,
    vocab_peers, seq_peers,
):
    pos, core = coordinates()
    x, y, z = pos
    seq, vocab = lax.axis_index("seq"), lax.axis_index("vocab")
    x_hi, x_lo = lax.div(x, 2), lax.rem(x, 2)
    y_up, y_down = lax.rem(y + 1, 4), lax.rem(y + 3, 4)
    to_y_up, to_y_down = (2 * y_up + x_hi, vocab), (2 * y_down + x_hi, vocab)
    to_x = (2 * y + 1 - x_hi, vocab)
    to_pair = (seq, 4 * z + 2 * x_lo + 1 - core)
    sent = []
    copy_to = functools.partial(start_copy, sent)
    h_sems, r_sems, g_sems = (h_send, h_recv), (r_send, r_recv), (g_send, g_recv)
    v_sems, q_sems = (v_send, v_recv), (q_send, q_recv)
    p_sems, z_sems = (p_send, p_recv), (z_send, z_recv)

    table_copy = pltpu.make_async_copy(table_ref, table, table_sem.at[0])
    table_copy.start()
    tokens[seq, 0:1] = ids_ref[...]
    tokens[seq, 1:2] = targets_ref[...]
    greet_all(vocab_peers, seq_peers)
    all_to_all(copy_to, tokens, seq, seq_peers, q_sems, 0)
    hidden[seq] = hidden_ref[...]
    copy_to(hidden.at[seq], hidden.at[seq], h_sems, 0, to_x)
    copy_to(hidden.at[seq], hidden.at[seq], h_sems, 1, to_y_up)
    copy_to(hidden.at[seq], hidden.at[seq], h_sems, 2, to_y_down)

    def start_scale(which, block):
        values = block.astype(jnp.float32)
        total = jnp.sum(values * values, axis=0, keepdims=True)
        square_slots[which, vocab] = jnp.broadcast_to(total, (8, 128))
        all_to_all(copy_to, square_slots.at[which], vocab, vocab_peers, v_sems, 15 * which)

    def spread_scale(which):
        all_from_all(square_slots.at[which], vocab, vocab_peers, v_sems, 15 * which)
        total = jnp.sum(square_slots[which], axis=0)
        scale_slots[which, seq] = lax.rsqrt(total / D + EPSILON)
        all_to_all(copy_to, scale_slots.at[which], seq, seq_peers, q_sems, 7 + 7 * which)

    def end_scale(which):
        all_from_all(scale_slots.at[which], seq, seq_peers, q_sems, 7 + 7 * which)

    start_scale(0, hidden_ref[...])
    for which, gain_ref in enumerate((gain_hidden_ref, gain_embed_ref)):
        for first in range(0, 448, 128):
            row = gain_ref[:, first : min(first + 128, 448)]
            if first == 384:
                row = jnp.concatenate([row, jnp.zeros((1, 64), jnp.float32)], axis=1)
            gains[which, first : min(first + 128, 448)] = row_to_columns(row)[: min(448 - first, 128)]
    all_from_all(tokens, seq, seq_peers, q_sems, 0)
    table_copy.wait()

    def look_up(y_at):
        ids = jnp.concatenate([tokens[2 * y_at, 0:1], tokens[2 * y_at + 1, 0:1]], axis=1) - seq * 8192
        total = jnp.zeros((448, 256), jnp.float32)
        for first in range(0, 8192, 1024):
            entries = lax.broadcasted_iota(jnp.int32, (1024, 256), 0) + first
            chosen = jnp.where(entries == ids, 1.0, 0.0).astype(jnp.bfloat16)
            total += jnp.dot(table[:, first : first + 1024], chosen, preferred_element_type=jnp.float32)
        return total.astype(jnp.bfloat16)

    def near_or_other(e):
        return x_hi if e == 0 else 1 - x_hi

    def seq_at(number):
        return 2 * lax.rem(y + number // 2, 4) + near_or_other(number % 2)

    def look_up_and_send(dy):
        y_at = lax.rem(y + dy, 4)
        found = look_up(y_at)
        for i in range(2):
            parts[y_at, i] = found[:, 128 * i : 128 * i + 128]
        for e in range(2):
            number = 2 * dy + e
            if number:
                source = parts.at[y_at, near_or_other(e)]
                copy_to(source, sums_in.at[number], r_sems, number, (seq_at(number), vocab))

    other = 2 * y + 1 - x_hi
    below, above = 2 * y_down + x_hi, 2 * y_up + x_hi
    other_below, other_above = 2 * y_down + 1 - x_hi, 2 * y_up + 1 - x_hi
    far, other_far = seq_at(4), seq_at(5)
    look_up_and_send(2)
    arrived(hidden.at[other], h_sems, 0, to_x)
    copy_to(hidden.at[other], hidden.at[other], h_sems, 3, to_y_up)
    copy_to(hidden.at[other], hidden.at[other], h_sems, 4, to_y_down)
    arrived(hidden.at[below], h_sems, 1, to_y_down)
    copy_to(hidden.at[below], hidden.at[below], h_sems, 5, to_y_up)
    spread_scale(0)
    look_up_and_send(1)
    look_up_and_send(3)
    arrived(hidden.at[other_above], h_sems, 4, to_y_up)
    copy_to(hidden.at[other_above], hidden.at[other_above], h_sems, 6, to_y_down)
    look_up_and_send(0)
    total = parts[y, x_hi]
    for number in range(1, 8):
        arrived(sums_in.at[number], r_sems, number, to_x)
        total += sums_in[number]
    embed[seq] = total
    for number in range(1, 8):
        copy_to(embed.at[seq], embed.at[seq], g_sems, number, (seq_at(number), vocab))
    start_scale(1, total)

    def project(source, which, weight_ref, z_at):
        normed = []
        for i in range(2):
            values = source[2 * z_at + i].astype(jnp.float32) * scale_slots[which, 2 * z_at + i, 0:1]
            normed.append((values * gains[which]).astype(jnp.bfloat16))
        return lax.dot_general(
            jnp.concatenate(normed, axis=1), weight_ref[...], (((0,), (0,)), ((), ())),
            preferred_element_type=jnp.float32,
        ).reshape(2, 2, 64, 896)

    arrived(hidden.at[above], h_sems, 2, to_y_up)
    arrived(hidden.at[other_below], h_sems, 3, to_y_down)
    arrived(hidden.at[far], h_sems, 5, to_y_down)
    arrived(hidden.at[other_far], h_sems, 6, to_y_up)
    end_scale(0)
    distances = (2, 1, 3, 0)
    for k in range(4):
        projected[k] = project(hidden, 0, proj_hidden_ref, lax.rem(z + distances[k], 4))
        if k == 1:
            spread_scale(1)
    for number in range(1, 8):
        sender = 2 * lax.rem(y + 4 - number // 2, 4) + near_or_other(number % 2)
        arrived(embed.at[sender], g_sems, number, to_x)
    end_scale(1)

    def hand_on(k):
        arrived(pair_in.at[k], p_sems, k, to_pair)
        both = projected[k, :, core] + pair_in[k]
        z_out[k] = both.astype(jnp.bfloat16)
        dz = distances[k]
        for e in range(2):
            number = 2 * dz + e
            x_at = x_lo if e == 0 else 1 - x_lo
            if number:
                to = (seq, 4 * lax.rem(z + dz, 4) + 2 * x_at + core)
                copy_to(z_out.at[k, x_at], z_in.at[number], z_sems, number, to)
            else:
                projected[k, :, core] = both

    for k in range(4):
        projected[k] += project(embed, 1, proj_embed_ref, lax.rem(z + distances[k], 4))
        copy_to(projected.at[k, :, 1 - core], pair_in.at[k], p_sems, k, to_pair)
        if k:
            hand_on(k - 1)
    hand_on(3)
    total = projected[3, x_lo, core]
    for number in range(1, 8):
        arrived(z_in.at[number], z_sems, number, to_pair)
        total += z_in[number].astype(jnp.float32)
    return total, sent


JOIN_SCRATCH = [
    pltpu.VMEM((448, 8192), jnp.bfloat16),
    pltpu.VMEM((8, 2, 128), jnp.int32),
    pltpu.VMEM((8, 448, 128), jnp.bfloat16),
    pltpu.VMEM((8, 448, 128), jnp.bfloat16),
    pltpu.VMEM((2, 448, 128), jnp.float32),
    pltpu.VMEM((4, 2, 448, 128), jnp.bfloat16),
    pltpu.VMEM((8, 448, 128), jnp.bfloat16),
    pltpu.VMEM((2, 16, 8, 128), jnp.float32),
    pltpu.VMEM((2, 8, 8, 128), jnp.float32),
    pltpu.VMEM((4, 2, 2, 64, 896), jnp.float32),
    pltpu.VMEM((4, 2, 64, 896), jnp.float32),
    pltpu.VMEM((4, 2, 64, 896), jnp.bfloat16),
    pltpu.VMEM((8, 64, 896), jnp.bfloat16),
    *[pltpu.SemaphoreType.DMA((count,)) for count in (7, 7, 8, 8, 8, 8, 30, 30, 21, 21, 4, 4, 8, 8)],
    pltpu.SemaphoreType.DMA((1,)),
]


def joined(lower, upper, turned):
    lane = lax.broadcasted_iota(jnp.int32, (1, 128), 1)
    if turned:
        return jnp.where(lane < 64, pltpu.roll(lower, 64, 1), upper)[0:1]
    return jnp.where(lane < 64, lower, pltpu.roll(upper, 64, 1))[0:1]


def whole_kernel(*refs):
    inputs, (head_ref, grad_ref, loss_ref, rows) = refs[:9], refs[9:13]
    join_scratch = refs[13 : 13 + len(JOIN_SCRATCH)]
    (
        head, scores, stats, vocab_stats, seq_stats, targets, scales, final_slots, row_slots,
        ring_send, ring_recv, pair_send, pair_recv, stat_send, stat_recv, f_send, f_recv, local_sem,
    ) = refs[13 + len(JOIN_SCRATCH) :]
    pos, core = coordinates()
    seq, vocab = lax.axis_index("seq"), lax.axis_index("vocab")
    x, y, z = pos
    head_copies = [
        pltpu.make_async_copy(
            head_ref.at[:, pl.ds(896 * i, 896)], head.at[i], local_sem.at[i]
        )
        for i in range(8)
    ]
    for copy in head_copies:
        copy.start()
    vocab_peers = [(seq, lax.rem(vocab + i, 16)) for i in range(1, 16)]
    seq_peers = [(lax.rem(seq + i, 8), vocab) for i in range(1, 8)]
    total, sent = join_kernel(*inputs, *join_scratch, vocab_peers, seq_peers)
    copy_to = functools.partial(start_copy, sent)
    f_sems, stat_sems = (f_send, f_recv), (stat_send, stat_recv)

    gain = jnp.concatenate([inputs[8][i : i + 1] for i in range(7)], axis=1)
    rows[x, y, z, core] = (total * gain).astype(jnp.bfloat16)

    def start_scale():
        spread = jnp.concatenate([lane_sums(total), jnp.zeros((64, 128), jnp.float32)], axis=0)
        squares = jnp.sum(jnp.transpose(spread), axis=0, keepdims=True)
        final_slots[seq] = jnp.broadcast_to(squares, (8, 128))
        all_to_all(copy_to, final_slots, seq, seq_peers, f_sems, 0)

    def spread_scale():
        all_from_all(final_slots, seq, seq_peers, f_sems, 0)
        row_slots[vocab] = lax.rsqrt(jnp.sum(final_slots[...], axis=0) / D + EPSILON)
        all_to_all(copy_to, row_slots, vocab, vocab_peers, f_sems, 7)

    def end_scale():
        all_from_all(row_slots, vocab, vocab_peers, f_sems, 7)
        for c in range(2):
            for i in range(4):
                row = joined(row_slots[4 * i + c], row_slots[4 * i + 2 + c], False)
                scales[4 * c + i : 4 * c + i + 1] = row

    def order_targets():
        tokens = join_scratch[1]
        for i in range(4):
            for c in range(2):
                lower = jnp.broadcast_to(tokens[2 * i, 1:2], (8, 128))
                upper = jnp.broadcast_to(tokens[2 * i + 1, 1:2], (8, 128))
                targets[4 * c + i : 4 * c + i + 1] = joined(lower, upper, c == 1)

    def place(part, core_of, axes, distances):
        index = [None] * 3
        for axis, distance in zip(axes, distances):
            index[axis] = pl.ds(0, 4) if distance == 4 else lax.rem(pos[axis] + distance, 4)
        first, width = COLUMNS[part]
        return rows.at[index[0], index[1], index[2], core_of, :, pl.ds(first, width)]

    def ring(mine, code):
        number, kind = divmod(code, 4)
        part, stage, distances = received(number)
        axes = ORDERS[mine][part]
        by = (0, 1, -1, 2)[kind]
        if kind:
            distances = list(distances)
            distances[stage - 1] = 0 if kind == 3 else (distances[stage - 1] + by) % 4
        piece = place(part, mine, axes, distances)
        to = device(shifted(pos, axes[stage - 1], by if kind else 1), mine)
        return pltpu.make_async_remote_copy(
            src_ref=piece, dst_ref=piece, send_sem=ring_send.at[number], recv_sem=ring_recv.at[number],
            device_id=to, device_id_type=MESH,
        ), (axes[stage - 1], by)

    def pair(mine, which, part, line):
        piece = place(part, which, ORDERS[which][part], (4, line[0], line[1]))
        number = 16 * part + 4 * line[1] + line[0]
        return pltpu.make_async_remote_copy(
            src_ref=piece, dst_ref=piece, send_sem=pair_send.at[number], recv_sem=pair_recv.at[number],
            device_id=device(pos, 1 - mine), device_id_type=MESH,
        )

    here = [{}, {}]
    started = [{}, {}]
    paired = [set(), set()]

    def ring_steps(mine, codes):
        for code in codes:
            copy, link = ring(mine, code)
            if code % 4 == 0:
                copy.wait_recv()
                part, _, distances = received(code // 4)
                line = (part, distances[1], distances[2])
                count = here[mine].get(line, 1 if line[1:] == (0, 0) else 0)
                here[mine][line] = count + (4 if distances[0] == 4 else 1)
                if here[mine][line] == 4:
                    pair(mine, mine, part, line[1:]).start()
            else:
                copies = started[mine].setdefault(link, [])
                if len(copies) >= OUTSTANDING and link[1] != 2:
                    ring(mine, copies[len(copies) - OUTSTANDING])[0].wait_send()
                copies.append(code)
                copy.start()

    def needed(which, part, dy, other, distance):
        if which == 0:
            return [(distance, dy) if part == 0 else (dy, distance)]
        along = (2, 1, 3) if other else (0, 1, 3)
        return [(distance, dx) if part == 0 else (dx, distance) for dx in along]

    def pair_steps(mine, products):
        for code in products:
            part, dy, other, near, which = code // 32, code // 8 % 4, code // 4 % 2, code // 2 % 2, code % 2
            for distance in NEAR_Z[near]:
                for line in needed(which, part, dy, other, distance):
                    if which == mine:
                        assert here[mine][(part, *line)] == 4
                    elif (part, line) not in paired[mine]:
                        paired[mine].add((part, line))
                        pair(mine, which, part, line).wait_recv()

    def by_core(action, per_core):
        for mine in range(2):

            @pl.when(core == mine)
            def _():
                action(mine, per_core[mine])

    x_hi = lax.div(x, 2)

    def multiply(code):
        part, dy, other, near, which = code // 32, code // 8 % 4, code // 4 % 2, code // 2 % 2, code % 2
        y_at, hi_at = lax.rem(y + dy, 4), lax.rem(x_hi + other, 2)
        z_at = [lax.rem(z + distance, 4) for distance in NEAR_Z[near]]
        first, width = COLUMNS[part]
        columns = pl.ds(first, width)
        taken = [rows[pl.ds(2 * hi_at, 2), y_at, i, which, :, columns].reshape(128, width) for i in z_at]
        product = lax.dot_general(
            head[2 * y_at + hi_at, :, columns], jnp.concatenate(taken, axis=0), (((1,), (1,)), ((), ())),
            preferred_element_type=jnp.float32,
        )
        for i in range(2):
            scores[4 * which + z_at[i]] += product[:, 128 * i : 128 * i + 128]

    scores[...] = jnp.zeros_like(scores)
    for first_core, second_core, products in SCHEDULE:
        by_core(ring_steps, (first_core, second_core))
        if products[0] == 64:
            start_scale()
            order_targets()
        elif products[0] == 65:
            spread_scale()
        elif products[0] == 66:
            end_scale()
            for copy in head_copies:
                copy.wait()
        else:
            by_core(pair_steps, (products, products))
            for code in products:
                multiply(code)

    first_entry = (seq * 16 + vocab) * 512
    entries = first_entry + lax.broadcasted_iota(jnp.int32, (512, 128), 0)
    for q in range(8):
        part = scores[q] * scales[q : q + 1]
        peak = jnp.max(part, axis=0, keepdims=True)
        matches = entries == targets[q : q + 1]
        powers = jnp.exp(part - peak)
        scores[q] = powers
        stats[0, q : q + 1] = peak + jnp.log(jnp.sum(powers, axis=0, keepdims=True))
        stats[1, q : q + 1] = jnp.sum(jnp.where(matches, part, 0.0), axis=0, keepdims=True)
        stats[2, q : q + 1] = peak

    def combine(slots):
        logs = slots[:, 0]
        top = jnp.max(logs, axis=0)
        return top + jnp.log(jnp.sum(jnp.exp(logs - top[None]), axis=0)), jnp.sum(slots[:, 1], axis=0)

    vocab_stats[vocab] = stats[0:2]
    all_to_all(copy_to, vocab_stats, vocab, vocab_peers, stat_sems, 0)
    all_from_all(vocab_stats, vocab, vocab_peers, stat_sems, 0)
    seq_stats[seq, 0], seq_stats[seq, 1] = combine(vocab_stats)
    all_to_all(copy_to, seq_stats, seq, seq_peers, stat_sems, 15)
    all_from_all(seq_stats, seq, seq_peers, stat_sems, 15)
    log_total, chosen = combine(seq_stats)
    loss_ref[0, 0] = jnp.sum(log_total - chosen) / 1024
    stats[0] = jnp.exp(stats[2] - log_total)
    for q in range(8):
        columns = slice(128 * q, 128 * q + 128)
        matches = entries == targets[q : q + 1]
        grad = scores[q] * stats[0, q : q + 1] - jnp.where(matches, 1.0, 0.0)
        grad_ref[:, columns] = (grad * scales[q : q + 1]).astype(jnp.bfloat16)

    def finish(mine, _):
        for (_, by), copies in started[mine].items():
            for code in copies if by == 2 else copies[-OUTSTANDING:]:
                ring(mine, code)[0].wait_send()
        for part in range(2):
            for number in range(16):
                pair(mine, mine, part, (number % 4, number // 4)).wait_send()

    by_core(finish, (None, None))
    for copy in sent:
        copy.wait_send()


def whole(*arguments):
    return pl.pallas_call(
        whole_kernel,
        out_shape=(
            pltpu.VMEM((512, 1024), jnp.bfloat16),
            jax.ShapeDtypeStruct((1, 1), jnp.float32),
            pltpu.VMEM((4, 4, 4, 2, 64, 896), jnp.bfloat16),
        ),
        in_specs=[pl.BlockSpec(memory_space=pltpu.VMEM)] * 3
        + [pl.BlockSpec(memory_space=pl.ANY)]
        + [pl.BlockSpec(memory_space=pltpu.VMEM)] * 5
        + [pl.BlockSpec(memory_space=pl.ANY)],
        out_specs=(
            pl.BlockSpec(memory_space=pltpu.VMEM),
            pl.BlockSpec(memory_space=pltpu.SMEM),
            pl.BlockSpec(memory_space=pltpu.VMEM),
        ),
        scratch_shapes=JOIN_SCRATCH + [
            pltpu.VMEM((8, 512, 896), jnp.bfloat16),
            pltpu.VMEM((8, 512, 128), jnp.float32),
            pltpu.VMEM((3, 8, 128), jnp.float32),
            pltpu.VMEM((16, 2, 8, 128), jnp.float32),
            pltpu.VMEM((8, 2, 8, 128), jnp.float32),
            pltpu.VMEM((8, 128), jnp.int32),
            pltpu.VMEM((8, 128), jnp.float32),
            pltpu.VMEM((8, 8, 128), jnp.float32),
            pltpu.VMEM((16, 8, 128), jnp.float32),
            pltpu.SemaphoreType.DMA((81,)),
            pltpu.SemaphoreType.DMA((81,)),
            pltpu.SemaphoreType.DMA((32,)),
            pltpu.SemaphoreType.DMA((32,)),
            pltpu.SemaphoreType.DMA((22,)),
            pltpu.SemaphoreType.DMA((22,)),
            pltpu.SemaphoreType.DMA((22,)),
            pltpu.SemaphoreType.DMA((22,)),
            pltpu.SemaphoreType.DMA((8,)),
        ],
        compiler_params=pltpu.CompilerParams(
            collective_id=2, has_side_effects=True, vmem_limit_bytes=44 * 1024 * 1024
        ),
    )(*arguments)


def grad_kernel(grad_ref, rows_ref, out_ref):
    y_at, hi_at = lax.div(pl.program_id(0), 2), lax.rem(pl.program_id(0), 2)
    taken = [rows_ref[pl.ds(2 * hi_at, 2), y_at, i, c].reshape(128, 896) for c in range(2) for i in range(4)]
    out_ref[...] = jnp.dot(
        grad_ref[...], jnp.concatenate(taken, axis=0), preferred_element_type=jnp.float32
    ).astype(jnp.bfloat16)


def head_gradient(grad, rows):
    return pl.pallas_call(
        grad_kernel,
        out_shape=jax.ShapeDtypeStruct((512, D), jnp.bfloat16),
        grid=(8,),
        in_specs=[pl.BlockSpec(memory_space=pltpu.VMEM)] * 2,
        out_specs=pl.BlockSpec((512, 896), lambda i: (0, i)),
        compiler_params=pltpu.CompilerParams(vmem_limit_bytes=24 * 1024 * 1024),
    )(pltpu.with_memory_space_constraint(grad, pltpu.VMEM), pltpu.with_memory_space_constraint(rows, pltpu.VMEM))


def body(
    hidden,
    next_ids,
    targets,
    embed_table,
    gain_hidden,
    gain_embed,
    proj_hidden,
    proj_embed,
    gain_final,
    head_weight,
):
    grad, loss, rows = whole(
        hidden.T,
        next_ids[None],
        targets[None],
        embed_table.T,
        gain_hidden[None],
        gain_embed[None],
        proj_hidden,
        proj_embed,
        gain_final.reshape(7, 128),
        head_weight,
    )
    return loss[0, 0], head_gradient(grad, rows)


def solution(mesh):
    in_specs = (
        P("seq", "vocab"),
        P("seq"),
        P("seq"),
        P("seq", "vocab"),
        P("vocab"),
        P("vocab"),
        P("vocab", "seq"),
        P("vocab", "seq"),
        P("seq"),
        P(("seq", "vocab"), None),
    )
    out_specs = (P(), P(("seq", "vocab"), None))
    return jax.shard_map(body, mesh=mesh, in_specs=in_specs, out_specs=out_specs, check_vma=False)
```

```python
import functools

import jax
import jax.numpy as jnp
from jax import lax
from jax.experimental import pallas as pl
from jax.experimental.pallas import tpu as pltpu
from jax.sharding import PartitionSpec as P

MESH = pl.DeviceIdType.MESH
D = 7168
EPSILON = 1e-06
HIGH, LOW = 48, 16
ORDERS = (((2, 0, 1), (0, 1, 2)), ((2, 1, 0), (1, 0, 2)))
ROWS = ((0, HIGH), (HIGH, LOW))


def coordinates():
    seq, vocab = lax.axis_index("seq"), lax.axis_index("vocab")
    return (
        (2 * lax.rem(seq, 2) + lax.rem(lax.div(vocab, 2), 2), lax.div(seq, 2), lax.div(vocab, 4)),
        lax.rem(vocab, 2),
    )


def device(pos, core):
    x, y, z = pos
    return (2 * y + lax.div(x, 2), 4 * z + 2 * lax.rem(x, 2) + core)


def shifted(pos, axis, by):
    moved = list(pos)
    moved[axis] = lax.rem(pos[axis] + (by + 4), 4)
    return tuple(moved)


def greet(peers):
    barrier = pltpu.get_barrier_semaphore()
    for peer in peers:
        pl.semaphore_signal(barrier, inc=1, device_id=peer, device_id_type=MESH)
    pl.semaphore_wait(barrier, len(peers))


def start_copy(sent, source, there, sems, number, to):
    copy = pltpu.make_async_remote_copy(
        src_ref=source, dst_ref=there, send_sem=sems[0].at[number], recv_sem=sems[1].at[number],
        device_id=to, device_id_type=MESH,
    )
    copy.start()
    sent.append(copy)


def arrived(place, sems, number, to):
    pltpu.make_async_remote_copy(
        src_ref=place, dst_ref=place, send_sem=sems[0].at[number], recv_sem=sems[1].at[number],
        device_id=to, device_id_type=MESH,
    ).wait_recv()


def all_to_all(copy_to, buffer, me, peers, sems, base):
    for i, peer in enumerate(peers):
        copy_to(buffer.at[me], buffer.at[me], sems, base + i, peer)


def all_from_all(buffer, me, peers, sems, base):
    count = len(peers) + 1
    for i, peer in enumerate(peers):
        arrived(buffer.at[lax.rem(me - (i + 1) + count, count)], sems, base + i, peer)


def greet_all(vocab_peers, seq_peers):
    pos, core = coordinates()
    across = device(shifted(pos, 0, 1 - 2 * (1 - lax.rem(pos[0], 2))), core)
    greet(vocab_peers + seq_peers + [across])


def row_to_columns(row):
    return jnp.transpose(jnp.broadcast_to(row, (128, 128)))


def lane_sums(values):
    total = jnp.zeros((values.shape[0], 128), jnp.float32)
    for first in range(0, values.shape[1], 128):
        total += values[:, first : first + 128] * values[:, first : first + 128]
    return total


def join_kernel(
    hidden_ref, ids_ref, targets_ref, table_ref, gain_hidden_ref, gain_embed_ref,
    proj_hidden_ref, proj_embed_ref, gain_final_ref,
    table, tokens, hidden, embed, gains, parts, halves_in, sums_out, sums_in, square_slots, scale_slots,
    embed_scale, projected, pair_in, z_out, z_in, own,
    h_send, h_recv, r_send, r_recv, g_send, g_recv, v_send, v_recv, q_send, q_recv,
    p_send, p_recv, z_send, z_recv, table_sem,
    vocab_peers, seq_peers,
):
    pos, core = coordinates()
    x, y, z = pos
    seq, vocab = lax.axis_index("seq"), lax.axis_index("vocab")
    x_hi, x_lo = lax.div(x, 2), lax.rem(x, 2)
    y_up, y_down = lax.rem(y + 1, 4), lax.rem(y + 3, 4)
    to_y_up, to_y_down = (2 * y_up + x_hi, vocab), (2 * y_down + x_hi, vocab)
    to_x = (2 * y + 1 - x_hi, vocab)
    to_pair = (seq, 4 * z + 2 * x_lo + 1 - core)
    sent = []
    copy_to = functools.partial(start_copy, sent)
    h_sems, r_sems, g_sems = (h_send, h_recv), (r_send, r_recv), (g_send, g_recv)
    v_sems, q_sems = (v_send, v_recv), (q_send, q_recv)
    p_sems = (p_send, p_recv)
    mine = 2 * z + x_lo

    table_copy = pltpu.make_async_copy(table_ref, table, table_sem.at[0])
    table_copy.start()
    tokens[seq, 0:1] = ids_ref[...]
    tokens[seq, 1:2] = targets_ref[...]
    greet_all(vocab_peers, seq_peers)
    all_to_all(copy_to, tokens, seq, seq_peers, q_sems, 0)
    hidden[seq] = hidden_ref[...]
    copy_to(hidden.at[seq], hidden.at[seq], h_sems, 0, to_x)
    copy_to(hidden.at[seq], hidden.at[seq], h_sems, 1, to_y_up)
    copy_to(hidden.at[seq], hidden.at[seq], h_sems, 2, to_y_down)

    def start_hidden_scale():
        values = hidden_ref[...].astype(jnp.float32)
        total = jnp.sum(values * values, axis=0, keepdims=True)
        square_slots[0, vocab] = jnp.broadcast_to(total, (8, 128))
        all_to_all(copy_to, square_slots.at[0], vocab, vocab_peers, v_sems, 0)

    def start_embed_scale():
        for i in range(8):
            values = parts[i // 2, i % 2].astype(jnp.float32)
            square_slots[1, vocab, i : i + 1] = jnp.sum(values * values, axis=0, keepdims=True)
        all_to_all(copy_to, square_slots.at[1], vocab, vocab_peers, v_sems, 15)

    def spread_scale(which):
        all_from_all(square_slots.at[which], vocab, vocab_peers, v_sems, 15 * which)
        total = jnp.sum(square_slots[which], axis=0)
        scale_slots[which, seq] = total if which else lax.rsqrt(total / D + EPSILON)
        all_to_all(copy_to, scale_slots.at[which], seq, seq_peers, q_sems, 7 + 7 * which)

    def end_scale(which):
        all_from_all(scale_slots.at[which], seq, seq_peers, q_sems, 7 + 7 * which)
        if which:
            embed_scale[...] = lax.rsqrt(jnp.sum(scale_slots[1], axis=0) / D + EPSILON)

    start_hidden_scale()
    for which, gain_ref in enumerate((gain_hidden_ref, gain_embed_ref)):
        for first in range(0, 448, 128):
            row = gain_ref[:, first : min(first + 128, 448)]
            if first == 384:
                row = jnp.concatenate([row, jnp.zeros((1, 64), jnp.float32)], axis=1)
            gains[which, first : min(first + 128, 448)] = row_to_columns(row)[: min(448 - first, 128)]
    all_from_all(tokens, seq, seq_peers, q_sems, 0)
    table_copy.wait()

    def look_up(y_at):
        ids = jnp.concatenate([tokens[2 * y_at, 0:1], tokens[2 * y_at + 1, 0:1]], axis=1) - seq * 8192
        total = jnp.zeros((448, 256), jnp.float32)
        for first in range(0, 8192, 1024):
            entries = lax.broadcasted_iota(jnp.int32, (1024, 256), 0) + first
            chosen = jnp.where(entries == ids, 1.0, 0.0).astype(jnp.bfloat16)
            total += jnp.dot(table[:, first : first + 1024], chosen, preferred_element_type=jnp.float32)
        return total.astype(jnp.bfloat16)

    def near_or_other(e):
        return x_hi if e == 0 else 1 - x_hi

    def seq_at(number):
        return 2 * lax.rem(y + number // 2, 4) + near_or_other(number % 2)

    def look_up_and_send(dy):
        y_at = lax.rem(y + dy, 4)
        found = look_up(y_at)
        for i in range(2):
            parts[y_at, i] = found[:, 128 * i : 128 * i + 128]
        copy_to(parts.at[y_at, 1 - x_hi], halves_in.at[dy], r_sems, dy, to_x)

    def sum_and_send(dy):
        y_at = lax.rem(y + dy, 4)
        arrived(halves_in.at[dy], r_sems, dy, to_x)
        total = parts[y_at, x_hi] + halves_in[dy]
        if dy:
            sums_out[dy] = total
            copy_to(sums_out.at[dy], sums_in.at[dy], r_sems, 3 + dy, (2 * y_at + x_hi, vocab))
        return total

    other = 2 * y + 1 - x_hi
    below, above = 2 * y_down + x_hi, 2 * y_up + x_hi
    other_below, other_above = 2 * y_down + 1 - x_hi, 2 * y_up + 1 - x_hi
    far, other_far = seq_at(4), seq_at(5)
    look_up_and_send(2)
    look_up_and_send(1)
    arrived(hidden.at[other], h_sems, 0, to_x)
    copy_to(hidden.at[other], hidden.at[other], h_sems, 3, to_y_up)
    copy_to(hidden.at[other], hidden.at[other], h_sems, 4, to_y_down)
    arrived(hidden.at[below], h_sems, 1, to_y_down)
    copy_to(hidden.at[below], hidden.at[below], h_sems, 5, to_y_up)
    spread_scale(0)
    look_up_and_send(3)
    sum_and_send(2)
    look_up_and_send(0)
    sum_and_send(1)
    start_embed_scale()
    arrived(hidden.at[other_above], h_sems, 4, to_y_up)
    copy_to(hidden.at[other_above], hidden.at[other_above], h_sems, 6, to_y_down)
    sum_and_send(3)

    total = sum_and_send(0)
    spread_scale(1)
    for dy in (1, 3, 2):
        arrived(sums_in.at[dy], r_sems, 3 + dy, to_x)
        total += sums_in[dy]
    embed[seq] = total

    def send_embedded(number):
        copy_to(embed.at[seq], embed.at[seq], g_sems, number, (seq_at(number), vocab))

    order = (0, 2, 6, 1, 4, 3, 7, 5)
    blocks = [seq] + [2 * lax.rem(y + 4 - n // 2, 4) + near_or_other(n % 2) for n in order[1:]]
    for number in order[1:]:
        send_embedded(number)

    def project(source, scale, gain, weight_ref):
        values = source.astype(jnp.float32) * scale * gain
        return lax.dot_general(
            values.astype(jnp.bfloat16), weight_ref[...], (((0,), (0,)), ((), ())),
            preferred_element_type=jnp.float32,
        ).reshape(2, 64, 896)

    arrived(hidden.at[above], h_sems, 2, to_y_up)
    arrived(hidden.at[other_below], h_sems, 3, to_y_down)
    arrived(hidden.at[far], h_sems, 5, to_y_down)
    arrived(hidden.at[other_far], h_sems, 6, to_y_up)
    end_scale(0)
    for k, block in enumerate(blocks):
        projected[k] = project(hidden[block], scale_slots[0, block, 0:1], gains[0], proj_hidden_ref)
    end_scale(1)

    late = []

    def hand_on(k):
        block = blocks[k]
        arrived(pair_in.at[k], p_sems, k, to_pair)
        both = projected[k, core] + pair_in[k]
        copy = pltpu.make_async_remote_copy(
            src_ref=z_out.at[k], dst_ref=z_in.at[mine], send_sem=z_send.at[k], recv_sem=z_recv.at[mine],
            device_id=(seq, 2 * block + core), device_id_type=MESH,
        )
        late.append((copy, block != mine))

        @pl.when(block != mine)
        def _():
            z_out[k] = both.astype(jnp.bfloat16)
            copy.start()

        @pl.when(block == mine)
        def _():
            own[...] = both

    for k, block in enumerate(blocks):
        if k:
            arrived(embed.at[block], g_sems, order[k], to_x)
        projected[k] += project(embed[block], embed_scale[pl.ds(block, 1)], gains[1], proj_embed_ref)
        copy_to(projected.at[k, 1 - core], pair_in.at[k], p_sems, k, to_pair)
        if k:
            hand_on(k - 1)
    hand_on(7)

    total = own[...]
    for number in range(1, 8):
        x_at = x_lo if number % 2 == 0 else 1 - x_lo
        sender = 2 * lax.rem(z + number // 2, 4) + x_at
        pltpu.make_async_remote_copy(
            src_ref=z_in.at[sender], dst_ref=z_in.at[sender], send_sem=z_send.at[0], recv_sem=z_recv.at[sender],
            device_id=to_pair, device_id_type=MESH,
        ).wait_recv()
        total += z_in[sender].astype(jnp.float32)
    for copy, there in late:

        @pl.when(there)
        def _():
            copy.wait_send()

    return total, sent


JOIN_SCRATCH = [
    pltpu.VMEM((448, 8192), jnp.bfloat16),
    pltpu.VMEM((8, 2, 128), jnp.int32),
    pltpu.VMEM((8, 448, 128), jnp.bfloat16),
    pltpu.VMEM((8, 448, 128), jnp.bfloat16),
    pltpu.VMEM((2, 448, 128), jnp.float32),
    pltpu.VMEM((4, 2, 448, 128), jnp.bfloat16),
    pltpu.VMEM((4, 448, 128), jnp.bfloat16),
    pltpu.VMEM((4, 448, 128), jnp.bfloat16),
    pltpu.VMEM((4, 448, 128), jnp.bfloat16),
    pltpu.VMEM((2, 16, 8, 128), jnp.float32),
    pltpu.VMEM((2, 8, 8, 128), jnp.float32),
    pltpu.VMEM((8, 128), jnp.float32),
    pltpu.VMEM((8, 2, 64, 896), jnp.float32),
    pltpu.VMEM((8, 64, 896), jnp.float32),
    pltpu.VMEM((8, 64, 896), jnp.bfloat16),
    pltpu.VMEM((8, 64, 896), jnp.bfloat16),
    pltpu.VMEM((64, 896), jnp.float32),
    *[pltpu.SemaphoreType.DMA((count,)) for count in (7, 7, 8, 8, 8, 8, 30, 30, 21, 21, 8, 8, 8, 8)],
    pltpu.SemaphoreType.DMA((1,)),
]


def to_score_order(natural, ordered):
    turned = {0: natural}
    lane = lax.broadcasted_iota(jnp.int32, (1, 128), 1)
    for part, (first, count) in enumerate(ROWS):
        for group in range(16):
            vocab = 4 * (group // 2 % 4) + 2 * (group // 8) + group % 2
            start = 16 * first + count * group
            done = 0
            while done < count:
                place, origin = start + done, 64 * vocab + first + done
                to, at = divmod(place, 128)
                size = min(count - done, 128 - at)
                turn = (at - origin) % 128
                if turn not in turned:
                    turned[turn] = pltpu.roll(natural, turn, 1)
                row = turned[turn][origin // 128 : origin // 128 + 1]
                if at == 0:
                    line = row
                else:
                    line = jnp.where(lane < at, line, row)
                if at + size == 128:
                    ordered[to : to + 1] = line
                done += size


def whole_kernel(*refs):
    inputs, (head_ref, grad_ref, loss_ref, rows) = refs[:9], refs[9:13]
    join_scratch = refs[13 : 13 + len(JOIN_SCRATCH)]
    (
        head, scores, stats, vocab_stats, seq_stats, targets, scales, final_slots, row_slots,
        ring_send, ring_recv, pair_send, pair_recv, stat_send, stat_recv, f_send, f_recv, local_sem,
    ) = refs[13 + len(JOIN_SCRATCH) :]
    pos, core = coordinates()
    seq, vocab = lax.axis_index("seq"), lax.axis_index("vocab")
    x, y, z = pos
    head_copies = [
        pltpu.make_async_copy(
            head_ref.at[:, pl.ds(896 * i, 896)], head.at[i], local_sem.at[i]
        )
        for i in range(8)
    ]
    for copy in head_copies:
        copy.start()
    vocab_peers = [(seq, lax.rem(vocab + i, 16)) for i in range(1, 16)]
    seq_peers = [(lax.rem(seq + i, 8), vocab) for i in range(1, 8)]
    total, sent = join_kernel(*inputs, *join_scratch, vocab_peers, seq_peers)
    copy_to = functools.partial(start_copy, sent)
    f_sems, stat_sems = (f_send, f_recv), (stat_send, stat_recv)

    gain = jnp.concatenate([inputs[8][i : i + 1] for i in range(7)], axis=1)
    rows[x, y, z, core] = (total * gain).astype(jnp.bfloat16)

    def start_scale():
        spread = jnp.concatenate([lane_sums(total), jnp.zeros((64, 128), jnp.float32)], axis=0)
        squares = jnp.sum(jnp.transpose(spread), axis=0, keepdims=True)
        final_slots[seq] = jnp.broadcast_to(squares, (8, 128))
        all_to_all(copy_to, final_slots, seq, seq_peers, f_sems, 0)

    def spread_scale():
        all_from_all(final_slots, seq, seq_peers, f_sems, 0)
        row_slots[vocab] = lax.rsqrt(jnp.sum(final_slots[...], axis=0) / D + EPSILON)
        all_to_all(copy_to, row_slots, vocab, vocab_peers, f_sems, 7)

    def end_scale():
        all_from_all(row_slots, vocab, vocab_peers, f_sems, 7)
        lane = lax.broadcasted_iota(jnp.int32, (1, 128), 1)
        natural = []
        for i in range(8):
            later = pltpu.roll(row_slots[2 * i + 1], 64, 1)[0:1]
            natural.append(jnp.where(lane < 64, row_slots[2 * i, 0:1], later))
        to_score_order(jnp.concatenate(natural, axis=0), scales)

    def unit(part, at, axis, half=None):
        index = list(at)
        if axis is not None:
            index[axis] = pl.ds(0, 4) if half is None else pl.ds(2 * half, 2)
        return index, ROWS[part]

    def ref_of(where, which):
        index, (first, count) = where
        return rows.at[index[0], index[1], index[2], which, pl.ds(first, count), :]

    def ring(mine, part, number, where, to):
        target = device(to, mine)
        piece = ref_of(where, mine)
        return pltpu.make_async_remote_copy(
            src_ref=piece, dst_ref=piece,
            send_sem=ring_send.at[part, number], recv_sem=ring_recv.at[part, number],
            device_id=target, device_id_type=MESH,
        )

    def pair(part, number, where, which, mine):
        piece = ref_of(where, which)
        return pltpu.make_async_remote_copy(
            src_ref=piece, dst_ref=piece,
            send_sem=pair_send.at[part, number], recv_sem=pair_recv.at[part, number],
            device_id=device(pos, 1 - mine), device_id_type=MESH,
        )

    def line_units(order, part):
        a, b, c = order
        lines = [(1, pos)]
        lines += [(2, shifted(pos, b, -1)), (2, shifted(pos, b, 1)), (3, shifted(pos, b, 2))]
        middles = [lines[i][1] for i in range(4)]
        for j, middle in enumerate(middles):
            lines += [(4 + j, shifted(middle, c, -1)), (4 + j, shifted(middle, c, 1))]
        for j, middle in enumerate(middles):
            lines.append((8 + j, shifted(middle, c, 2)))
        return [(step, unit(part, at, a)) for step, at in lines]

    def own_step(mine, step):
        for part in range(2):
            a, b, c = ORDERS[mine][part]

            def send(number, where, to):
                ring(mine, part, number, where, to).start()

            def recv(number, where):
                ring(mine, part, number, where, pos).wait_recv()

            def up(axis):
                return shifted(pos, axis, 1)

            def down(axis):
                return shifted(pos, axis, -1)

            middles = [pos, down(b), up(b), shifted(pos, b, 2)]

            def spread(j):
                send(7 + 4 * j, unit(part, middles[j], a), up(c))
                send(8 + 4 * j, unit(part, middles[j], a), down(c))

            if step == 0:
                send(0, unit(part, pos, None), up(a))
                send(1, unit(part, pos, None), down(a))
            elif step == 1:
                recv(0, unit(part, down(a), None))
                send(2, unit(part, down(a), None), up(a))
                recv(1, unit(part, up(a), None))
                recv(2, unit(part, shifted(pos, a, 2), None))
                send(3, unit(part, pos, a), up(b))
                send(4, unit(part, pos, a), down(b))
                spread(0)
            elif step == 2:
                recv(3, unit(part, middles[1], a))
                send(5, unit(part, middles[1], a, 0), up(b))
                recv(4, unit(part, middles[2], a))
                send(6, unit(part, middles[2], a, 1), down(b))
                spread(1)
                spread(2)
            elif step == 3:
                recv(5, unit(part, middles[3], a, 0))
                recv(6, unit(part, middles[3], a, 1))
                spread(3)
            elif step < 8:
                j = step - 4
                before, after = shifted(middles[j], c, -1), shifted(middles[j], c, 1)
                recv(7 + 4 * j, unit(part, before, a))
                send(9 + 4 * j, unit(part, before, a, 0), up(c))
                recv(8 + 4 * j, unit(part, after, a))
                send(10 + 4 * j, unit(part, after, a, 1), down(c))
            else:
                j = step - 8
                far = shifted(middles[j], c, 2)
                recv(9 + 4 * j, unit(part, far, a, 0))
                recv(10 + 4 * j, unit(part, far, a, 1))
            for number, (when, where) in enumerate(line_units(ORDERS[mine][part], part)):
                if when == step:
                    pair(part, number, where, mine, mine).start()

    def pair_step(mine, step):
        for part in range(2):
            for number, (when, where) in enumerate(line_units(ORDERS[1 - mine][part], part)):
                if when == step:
                    pair(part, number, where, 1 - mine, mine).wait_recv()

    def by_core(action, step):
        for mine in range(2):

            @pl.when(core == mine)
            def _():
                action(mine, step)

    x_hi = lax.div(x, 2)

    def multiply(dy, other, part):
        y_at = lax.rem(y + dy + 4, 4)
        hi_at = lax.rem(x_hi + other, 2)
        first, count = ROWS[part]
        taken = rows[pl.ds(2 * hi_at, 2), y_at, :, :, pl.ds(first, count), :].reshape(-1, 896)
        product = lax.dot_general(
            head[2 * y_at + hi_at], taken, (((1,), (1,)), ((), ())), preferred_element_type=jnp.float32
        )
        columns = slice(0, 16 * HIGH) if part == 0 else slice(16 * HIGH, 1024)
        if (dy, other) == (0, 0):
            scores[:, columns] = product
        else:
            scores[:, columns] += product

    ready = {
        4: [(0, 0, 0)],
        6: [(-1, 0, 0), (1, 0, 0)],
        8: [(0, 1, 0)],
        9: [(-1, 1, 0)],
        10: [(2, 0, 0), (1, 1, 0), (0, 0, 1), (-1, 0, 1), (1, 0, 1)],
        11: [(2, 1, 0), (2, 0, 1), (0, 1, 1), (-1, 1, 1), (1, 1, 1), (2, 1, 1)],
    }
    for step in range(13):
        if step < 12:
            by_core(own_step, step)
        if step == 0:
            start_scale()
            to_score_order(join_scratch[1][:, 1], targets)
        elif step == 2:
            spread_scale()
        elif step == 3:
            for copy in head_copies:
                copy.wait()
        elif step == 5:
            end_scale()
        if step >= 2:
            by_core(pair_step, step - 1)
            for dy, other, part in ready.get(step - 1, []):
                multiply(dy, other, part)

    first_entry = (seq * 16 + vocab) * 512
    entries = first_entry + lax.broadcasted_iota(jnp.int32, (512, 128), 0)
    for q in range(8):
        columns = slice(128 * q, 128 * q + 128)
        part = scores[:, columns] * scales[q : q + 1]
        peak = jnp.max(part, axis=0, keepdims=True)
        matches = entries == targets[q : q + 1]
        powers = jnp.exp(part - peak)
        scores[:, columns] = powers
        stats[0, q : q + 1] = peak + jnp.log(jnp.sum(powers, axis=0, keepdims=True))
        stats[1, q : q + 1] = jnp.sum(jnp.where(matches, part, 0.0), axis=0, keepdims=True)
        stats[2, q : q + 1] = peak

    def combine(slots):
        logs = slots[:, 0]
        top = jnp.max(logs, axis=0)
        return top + jnp.log(jnp.sum(jnp.exp(logs - top[None]), axis=0)), jnp.sum(slots[:, 1], axis=0)

    vocab_stats[vocab] = stats[0:2]
    all_to_all(copy_to, vocab_stats, vocab, vocab_peers, stat_sems, 0)
    all_from_all(vocab_stats, vocab, vocab_peers, stat_sems, 0)
    seq_stats[seq, 0], seq_stats[seq, 1] = combine(vocab_stats)
    all_to_all(copy_to, seq_stats, seq, seq_peers, stat_sems, 15)
    all_from_all(seq_stats, seq, seq_peers, stat_sems, 15)
    log_total, chosen = combine(seq_stats)
    loss_ref[0, 0] = jnp.sum(log_total - chosen) / 1024
    stats[0] = jnp.exp(stats[2] - log_total)
    for q in range(8):
        columns = slice(128 * q, 128 * q + 128)
        matches = entries == targets[q : q + 1]
        grad = scores[:, columns] * stats[0, q : q + 1] - jnp.where(matches, 1.0, 0.0)
        grad_ref[:, columns] = (grad * scales[q : q + 1]).astype(jnp.bfloat16)

    def finish(mine, _):
        for part in range(2):
            a, b, c = ORDERS[mine][part]
            sizes = [(pos, None, None)] * 3 + [(pos, a, None)] * 2 + [(pos, a, 0)] * 2
            sizes += ([(pos, a, None)] * 2 + [(pos, a, 0)] * 2) * 4
            for number, (at, axis, half) in enumerate(sizes):
                ring(mine, part, number, unit(part, at, axis, half), pos).wait_send()
            for number, (_, where) in enumerate(line_units(ORDERS[mine][part], part)):
                pair(part, number, where, mine, mine).wait_send()

    by_core(finish, 0)
    for copy in sent:
        copy.wait_send()


def whole(*arguments):
    return pl.pallas_call(
        whole_kernel,
        out_shape=(
            pltpu.VMEM((512, 1024), jnp.bfloat16),
            jax.ShapeDtypeStruct((1, 1), jnp.float32),
            pltpu.VMEM((4, 4, 4, 2, 64, 896), jnp.bfloat16),
        ),
        in_specs=[pl.BlockSpec(memory_space=pltpu.VMEM)] * 3
        + [pl.BlockSpec(memory_space=pl.ANY)]
        + [pl.BlockSpec(memory_space=pltpu.VMEM)] * 5
        + [pl.BlockSpec(memory_space=pl.ANY)],
        out_specs=(
            pl.BlockSpec(memory_space=pltpu.VMEM),
            pl.BlockSpec(memory_space=pltpu.SMEM),
            pl.BlockSpec(memory_space=pltpu.VMEM),
        ),
        scratch_shapes=JOIN_SCRATCH + [
            pltpu.VMEM((8, 512, 896), jnp.bfloat16),
            pltpu.VMEM((512, 1024), jnp.float32),
            pltpu.VMEM((3, 8, 128), jnp.float32),
            pltpu.VMEM((16, 2, 8, 128), jnp.float32),
            pltpu.VMEM((8, 2, 8, 128), jnp.float32),
            pltpu.VMEM((8, 128), jnp.int32),
            pltpu.VMEM((8, 128), jnp.float32),
            pltpu.VMEM((8, 8, 128), jnp.float32),
            pltpu.VMEM((16, 8, 128), jnp.float32),
            pltpu.SemaphoreType.DMA((2, 23)),
            pltpu.SemaphoreType.DMA((2, 23)),
            pltpu.SemaphoreType.DMA((2, 16)),
            pltpu.SemaphoreType.DMA((2, 16)),
            pltpu.SemaphoreType.DMA((22,)),
            pltpu.SemaphoreType.DMA((22,)),
            pltpu.SemaphoreType.DMA((22,)),
            pltpu.SemaphoreType.DMA((22,)),
            pltpu.SemaphoreType.DMA((8,)),
        ],
        compiler_params=pltpu.CompilerParams(
            collective_id=2, has_side_effects=True, vmem_limit_bytes=44 * 1024 * 1024
        ),
    )(*arguments)


def grad_kernel(grad_ref, rows_ref, out_ref):
    y_at, hi_at = lax.div(pl.program_id(0), 2), lax.rem(pl.program_id(0), 2)
    high = rows_ref[pl.ds(2 * hi_at, 2), y_at, :, :, 0:HIGH, :].reshape(16 * HIGH, 896)
    low = rows_ref[pl.ds(2 * hi_at, 2), y_at, :, :, HIGH:64, :].reshape(16 * LOW, 896)
    out_ref[...] = (
        jnp.dot(grad_ref[:, : 16 * HIGH], high, preferred_element_type=jnp.float32)
        + jnp.dot(grad_ref[:, 16 * HIGH :], low, preferred_element_type=jnp.float32)
    ).astype(jnp.bfloat16)


def head_gradient(grad, rows):
    return pl.pallas_call(
        grad_kernel,
        out_shape=jax.ShapeDtypeStruct((512, D), jnp.bfloat16),
        grid=(8,),
        in_specs=[pl.BlockSpec(memory_space=pltpu.VMEM)] * 2,
        out_specs=pl.BlockSpec((512, 896), lambda i: (0, i)),
        compiler_params=pltpu.CompilerParams(vmem_limit_bytes=24 * 1024 * 1024),
    )(pltpu.with_memory_space_constraint(grad, pltpu.VMEM), pltpu.with_memory_space_constraint(rows, pltpu.VMEM))


def body(
    hidden,
    next_ids,
    targets,
    embed_table,
    gain_hidden,
    gain_embed,
    proj_hidden,
    proj_embed,
    gain_final,
    head_weight,
):
    grad, loss, rows = whole(
        hidden.T,
        next_ids[None],
        targets[None],
        embed_table.T,
        gain_hidden[None],
        gain_embed[None],
        proj_hidden,
        proj_embed,
        gain_final.reshape(7, 128),
        head_weight,
    )
    return loss[0, 0], head_gradient(grad, rows)


def solution(mesh):
    in_specs = (
        P("seq", "vocab"),
        P("seq"),
        P("seq"),
        P("seq", "vocab"),
        P("vocab"),
        P("vocab"),
        P("vocab", "seq"),
        P("vocab", "seq"),
        P("seq"),
        P(("seq", "vocab"), None),
    )
    out_specs = (P(), P(("seq", "vocab"), None))
    return jax.shard_map(body, mesh=mesh, in_specs=in_specs, out_specs=out_specs, check_vma=False)
```

```python
import functools

import jax
import jax.numpy as jnp
from jax import lax
from jax.experimental import pallas as pl
from jax.experimental.pallas import tpu as pltpu
from jax.sharding import PartitionSpec as P

MESH = pl.DeviceIdType.MESH
D = 7168
EPSILON = 1e-06
HIGH, LOW = 48, 16
ORDERS = (((2, 0, 1), (0, 1, 2)), ((2, 1, 0), (1, 0, 2)))
ROWS = ((0, HIGH), (HIGH, LOW))


def coordinates():
    seq, vocab = lax.axis_index("seq"), lax.axis_index("vocab")
    return (
        (2 * lax.rem(seq, 2) + lax.rem(lax.div(vocab, 2), 2), lax.div(seq, 2), lax.div(vocab, 4)),
        lax.rem(vocab, 2),
    )


def device(pos, core):
    x, y, z = pos
    return (2 * y + lax.div(x, 2), 4 * z + 2 * lax.rem(x, 2) + core)


def shifted(pos, axis, by):
    moved = list(pos)
    moved[axis] = lax.rem(pos[axis] + (by + 4), 4)
    return tuple(moved)


def greet(peers):
    barrier = pltpu.get_barrier_semaphore()
    for peer in peers:
        pl.semaphore_signal(barrier, inc=1, device_id=peer, device_id_type=MESH)
    pl.semaphore_wait(barrier, len(peers))


def start_copy(sent, source, there, sems, number, to):
    copy = pltpu.make_async_remote_copy(
        src_ref=source, dst_ref=there, send_sem=sems[0].at[number], recv_sem=sems[1].at[number],
        device_id=to, device_id_type=MESH,
    )
    copy.start()
    sent.append(copy)


def arrived(place, sems, number, to):
    pltpu.make_async_remote_copy(
        src_ref=place, dst_ref=place, send_sem=sems[0].at[number], recv_sem=sems[1].at[number],
        device_id=to, device_id_type=MESH,
    ).wait_recv()


def all_to_all(copy_to, buffer, me, peers, sems, base):
    for i, peer in enumerate(peers):
        copy_to(buffer.at[me], buffer.at[me], sems, base + i, peer)


def all_from_all(buffer, me, peers, sems, base):
    count = len(peers) + 1
    for i, peer in enumerate(peers):
        arrived(buffer.at[lax.rem(me - (i + 1) + count, count)], sems, base + i, peer)


def greet_all(vocab_peers, seq_peers):
    pos, core = coordinates()
    across = device(shifted(pos, 0, 1 - 2 * (1 - lax.rem(pos[0], 2))), core)
    greet(vocab_peers + seq_peers + [across])


def row_to_columns(row):
    return jnp.transpose(jnp.broadcast_to(row, (128, 128)))


def lane_sums(values):
    total = jnp.zeros((values.shape[0], 128), jnp.float32)
    for first in range(0, values.shape[1], 128):
        total += values[:, first : first + 128] * values[:, first : first + 128]
    return total


def join_kernel(
    hidden_ref, ids_ref, targets_ref, table_ref, gain_hidden_ref, gain_embed_ref,
    proj_hidden_ref, proj_embed_ref, gain_final_ref,
    table, tokens, hidden, embed, gains, parts, halves_in, sums_out, sums_in, square_slots, scale_slots,
    embed_scale, projected, pair_in, z_out, z_in, own,
    h_send, h_recv, r_send, r_recv, g_send, g_recv, v_send, v_recv, q_send, q_recv,
    p_send, p_recv, z_send, z_recv, table_sem,
    vocab_peers, seq_peers, start_head,
):
    pos, core = coordinates()
    x, y, z = pos
    seq, vocab = lax.axis_index("seq"), lax.axis_index("vocab")
    x_hi, x_lo = lax.div(x, 2), lax.rem(x, 2)
    y_up, y_down = lax.rem(y + 1, 4), lax.rem(y + 3, 4)
    to_y_up, to_y_down = (2 * y_up + x_hi, vocab), (2 * y_down + x_hi, vocab)
    to_x = (2 * y + 1 - x_hi, vocab)
    to_pair = (seq, 4 * z + 2 * x_lo + 1 - core)
    sent = []
    copy_to = functools.partial(start_copy, sent)
    h_sems, r_sems, g_sems = (h_send, h_recv), (r_send, r_recv), (g_send, g_recv)
    v_sems, q_sems = (v_send, v_recv), (q_send, q_recv)
    p_sems = (p_send, p_recv)
    mine = 2 * z + x_lo

    table_copy = pltpu.make_async_copy(table_ref, table, table_sem.at[0])
    table_copy.start()
    tokens[seq, 0:1] = ids_ref[...]
    tokens[seq, 1:2] = targets_ref[...]
    greet_all(vocab_peers, seq_peers)
    all_to_all(copy_to, tokens, seq, seq_peers, q_sems, 0)
    hidden[seq] = hidden_ref[...]
    copy_to(hidden.at[seq], hidden.at[seq], h_sems, 0, to_x)
    copy_to(hidden.at[seq], hidden.at[seq], h_sems, 1, to_y_up)
    copy_to(hidden.at[seq], hidden.at[seq], h_sems, 2, to_y_down)

    def start_hidden_scale():
        values = hidden_ref[...].astype(jnp.float32)
        total = jnp.sum(values * values, axis=0, keepdims=True)
        square_slots[0, vocab] = jnp.broadcast_to(total, (8, 128))
        all_to_all(copy_to, square_slots.at[0], vocab, vocab_peers, v_sems, 0)

    def start_embed_scale():
        for i in range(8):
            values = parts[i // 2, i % 2].astype(jnp.float32)
            square_slots[1, vocab, i : i + 1] = jnp.sum(values * values, axis=0, keepdims=True)
        all_to_all(copy_to, square_slots.at[1], vocab, vocab_peers, v_sems, 15)

    def spread_scale(which):
        all_from_all(square_slots.at[which], vocab, vocab_peers, v_sems, 15 * which)
        total = jnp.sum(square_slots[which], axis=0)
        scale_slots[which, seq] = total if which else lax.rsqrt(total / D + EPSILON)
        all_to_all(copy_to, scale_slots.at[which], seq, seq_peers, q_sems, 7 + 7 * which)

    def end_scale(which):
        all_from_all(scale_slots.at[which], seq, seq_peers, q_sems, 7 + 7 * which)
        if which:
            embed_scale[...] = lax.rsqrt(jnp.sum(scale_slots[1], axis=0) / D + EPSILON)

    start_hidden_scale()
    for which, gain_ref in enumerate((gain_hidden_ref, gain_embed_ref)):
        for first in range(0, 448, 128):
            row = gain_ref[:, first : min(first + 128, 448)]
            if first == 384:
                row = jnp.concatenate([row, jnp.zeros((1, 64), jnp.float32)], axis=1)
            gains[which, first : min(first + 128, 448)] = row_to_columns(row)[: min(448 - first, 128)]
    all_from_all(tokens, seq, seq_peers, q_sems, 0)
    table_copy.wait()
    start_head()

    def look_up(y_at):
        ids = jnp.concatenate([tokens[2 * y_at, 0:1], tokens[2 * y_at + 1, 0:1]], axis=1) - seq * 8192
        total = jnp.zeros((448, 256), jnp.float32)
        for first in range(0, 8192, 1024):
            entries = lax.broadcasted_iota(jnp.int32, (1024, 256), 0) + first
            chosen = jnp.where(entries == ids, 1.0, 0.0).astype(jnp.bfloat16)
            total += jnp.dot(table[:, first : first + 1024], chosen, preferred_element_type=jnp.float32)
        return total.astype(jnp.bfloat16)

    def near_or_other(e):
        return x_hi if e == 0 else 1 - x_hi

    def seq_at(number):
        return 2 * lax.rem(y + number // 2, 4) + near_or_other(number % 2)

    def look_up_and_send(dy):
        y_at = lax.rem(y + dy, 4)
        found = look_up(y_at)
        for i in range(2):
            parts[y_at, i] = found[:, 128 * i : 128 * i + 128]
        copy_to(parts.at[y_at, 1 - x_hi], halves_in.at[dy], r_sems, dy, to_x)

    def sum_and_send(dy):
        y_at = lax.rem(y + dy, 4)
        arrived(halves_in.at[dy], r_sems, dy, to_x)
        total = parts[y_at, x_hi] + halves_in[dy]
        if dy:
            sums_out[dy] = total
            copy_to(sums_out.at[dy], sums_in.at[dy], r_sems, 3 + dy, (2 * y_at + x_hi, vocab))
        return total

    other = 2 * y + 1 - x_hi
    below, above = 2 * y_down + x_hi, 2 * y_up + x_hi
    other_below, other_above = 2 * y_down + 1 - x_hi, 2 * y_up + 1 - x_hi
    far, other_far = seq_at(4), seq_at(5)
    look_up_and_send(2)
    look_up_and_send(1)
    arrived(hidden.at[other], h_sems, 0, to_x)
    copy_to(hidden.at[other], hidden.at[other], h_sems, 3, to_y_up)
    copy_to(hidden.at[other], hidden.at[other], h_sems, 4, to_y_down)
    arrived(hidden.at[below], h_sems, 1, to_y_down)
    copy_to(hidden.at[below], hidden.at[below], h_sems, 5, to_y_up)
    spread_scale(0)
    look_up_and_send(3)
    sum_and_send(2)
    look_up_and_send(0)
    sum_and_send(1)
    start_embed_scale()
    arrived(hidden.at[other_above], h_sems, 4, to_y_up)
    copy_to(hidden.at[other_above], hidden.at[other_above], h_sems, 6, to_y_down)
    sum_and_send(3)

    total = sum_and_send(0)
    spread_scale(1)
    for dy in (1, 3, 2):
        arrived(sums_in.at[dy], r_sems, 3 + dy, to_x)
        total += sums_in[dy]
    embed[seq] = total

    def send_embedded(number):
        copy_to(embed.at[seq], embed.at[seq], g_sems, number, (seq_at(number), vocab))

    order = (0, 2, 6, 1, 4, 3, 7, 5)
    blocks = [seq] + [2 * lax.rem(y + 4 - n // 2, 4) + near_or_other(n % 2) for n in order[1:]]
    for number in order[1:]:
        send_embedded(number)

    def project(source, scale, gain, weight_ref):
        values = source.astype(jnp.float32) * scale * gain
        return lax.dot_general(
            values.astype(jnp.bfloat16), weight_ref[...], (((0,), (0,)), ((), ())),
            preferred_element_type=jnp.float32,
        ).reshape(2, 64, 896)

    arrived(hidden.at[above], h_sems, 2, to_y_up)
    arrived(hidden.at[other_below], h_sems, 3, to_y_down)
    arrived(hidden.at[far], h_sems, 5, to_y_down)
    arrived(hidden.at[other_far], h_sems, 6, to_y_up)
    end_scale(0)
    for k, block in enumerate(blocks):
        projected[k] = project(hidden[block], scale_slots[0, block, 0:1], gains[0], proj_hidden_ref)
    end_scale(1)

    late = []

    def hand_on(k):
        block = blocks[k]
        arrived(pair_in.at[k], p_sems, k, to_pair)
        both = projected[k, core] + pair_in[k]
        copy = pltpu.make_async_remote_copy(
            src_ref=z_out.at[k], dst_ref=z_in.at[mine], send_sem=z_send.at[k], recv_sem=z_recv.at[mine],
            device_id=(seq, 2 * block + core), device_id_type=MESH,
        )
        late.append((copy, block != mine))

        @pl.when(block != mine)
        def _():
            z_out[k] = both.astype(jnp.bfloat16)
            copy.start()

        @pl.when(block == mine)
        def _():
            own[...] = both

    for k, block in enumerate(blocks):
        if k:
            arrived(embed.at[block], g_sems, order[k], to_x)
        projected[k] += project(embed[block], embed_scale[pl.ds(block, 1)], gains[1], proj_embed_ref)
        copy_to(projected.at[k, 1 - core], pair_in.at[k], p_sems, k, to_pair)
        if k:
            hand_on(k - 1)
    hand_on(7)

    total = own[...]
    for number in range(1, 8):
        x_at = x_lo if number % 2 == 0 else 1 - x_lo
        sender = 2 * lax.rem(z + number // 2, 4) + x_at
        pltpu.make_async_remote_copy(
            src_ref=z_in.at[sender], dst_ref=z_in.at[sender], send_sem=z_send.at[0], recv_sem=z_recv.at[sender],
            device_id=to_pair, device_id_type=MESH,
        ).wait_recv()
        total += z_in[sender].astype(jnp.float32)
    for copy, there in late:

        @pl.when(there)
        def _():
            copy.wait_send()

    return total, sent


JOIN_SCRATCH = [
    pltpu.VMEM((448, 8192), jnp.bfloat16),
    pltpu.VMEM((8, 2, 128), jnp.int32),
    pltpu.VMEM((8, 448, 128), jnp.bfloat16),
    pltpu.VMEM((8, 448, 128), jnp.bfloat16),
    pltpu.VMEM((2, 448, 128), jnp.float32),
    pltpu.VMEM((4, 2, 448, 128), jnp.bfloat16),
    pltpu.VMEM((4, 448, 128), jnp.bfloat16),
    pltpu.VMEM((4, 448, 128), jnp.bfloat16),
    pltpu.VMEM((4, 448, 128), jnp.bfloat16),
    pltpu.VMEM((2, 16, 8, 128), jnp.float32),
    pltpu.VMEM((2, 8, 8, 128), jnp.float32),
    pltpu.VMEM((8, 128), jnp.float32),
    pltpu.VMEM((8, 2, 64, 896), jnp.float32),
    pltpu.VMEM((8, 64, 896), jnp.float32),
    pltpu.VMEM((8, 64, 896), jnp.bfloat16),
    pltpu.VMEM((8, 64, 896), jnp.bfloat16),
    pltpu.VMEM((64, 896), jnp.float32),
    *[pltpu.SemaphoreType.DMA((count,)) for count in (7, 7, 8, 8, 8, 8, 30, 30, 21, 21, 8, 8, 8, 8)],
    pltpu.SemaphoreType.DMA((1,)),
]


def to_score_order(natural, ordered):
    turned = {0: natural}
    lane = lax.broadcasted_iota(jnp.int32, (1, 128), 1)
    for part, (first, count) in enumerate(ROWS):
        for group in range(16):
            vocab = 4 * (group // 2 % 4) + 2 * (group // 8) + group % 2
            start = 16 * first + count * group
            done = 0
            while done < count:
                place, origin = start + done, 64 * vocab + first + done
                to, at = divmod(place, 128)
                size = min(count - done, 128 - at)
                turn = (at - origin) % 128
                if turn not in turned:
                    turned[turn] = pltpu.roll(natural, turn, 1)
                row = turned[turn][origin // 128 : origin // 128 + 1]
                if at == 0:
                    line = row
                else:
                    line = jnp.where(lane < at, line, row)
                if at + size == 128:
                    ordered[to : to + 1] = line
                done += size


def whole_kernel(*refs):
    inputs, (head_ref, grad_ref, loss_ref, rows) = refs[:9], refs[9:13]
    join_scratch = refs[13 : 13 + len(JOIN_SCRATCH)]
    (
        head, scores, stats, vocab_stats, seq_stats, targets, scales, final_slots, row_slots,
        ring_send, ring_recv, pair_send, pair_recv, stat_send, stat_recv, f_send, f_recv, local_sem,
    ) = refs[13 + len(JOIN_SCRATCH) :]
    pos, core = coordinates()
    seq, vocab = lax.axis_index("seq"), lax.axis_index("vocab")
    x, y, z = pos
    head_copies = [
        pltpu.make_async_copy(
            head_ref.at[:, pl.ds(896 * i, 896)], head.at[i], local_sem.at[i]
        )
        for i in range(8)
    ]

    def start_head():
        for copy in head_copies:
            copy.start()

    vocab_peers = [(seq, lax.rem(vocab + i, 16)) for i in range(1, 16)]
    seq_peers = [(lax.rem(seq + i, 8), vocab) for i in range(1, 8)]
    total, sent = join_kernel(*inputs, *join_scratch, vocab_peers, seq_peers, start_head)
    copy_to = functools.partial(start_copy, sent)
    f_sems, stat_sems = (f_send, f_recv), (stat_send, stat_recv)

    gain = jnp.concatenate([inputs[8][i : i + 1] for i in range(7)], axis=1)
    rows[x, y, z, core] = (total * gain).astype(jnp.bfloat16)

    def start_scale():
        spread = jnp.concatenate([lane_sums(total), jnp.zeros((64, 128), jnp.float32)], axis=0)
        squares = jnp.sum(jnp.transpose(spread), axis=0, keepdims=True)
        final_slots[seq] = jnp.broadcast_to(squares, (8, 128))
        all_to_all(copy_to, final_slots, seq, seq_peers, f_sems, 0)

    def spread_scale():
        all_from_all(final_slots, seq, seq_peers, f_sems, 0)
        row_slots[vocab] = lax.rsqrt(jnp.sum(final_slots[...], axis=0) / D + EPSILON)
        all_to_all(copy_to, row_slots, vocab, vocab_peers, f_sems, 7)

    def end_scale():
        all_from_all(row_slots, vocab, vocab_peers, f_sems, 7)
        lane = lax.broadcasted_iota(jnp.int32, (1, 128), 1)
        natural = []
        for i in range(8):
            later = pltpu.roll(row_slots[2 * i + 1], 64, 1)[0:1]
            natural.append(jnp.where(lane < 64, row_slots[2 * i, 0:1], later))
        to_score_order(jnp.concatenate(natural, axis=0), scales)

    def unit(part, at, axis, half=None):
        index = list(at)
        if axis is not None:
            index[axis] = pl.ds(0, 4) if half is None else pl.ds(2 * half, 2)
        return index, ROWS[part]

    def ref_of(where, which):
        index, (first, count) = where
        return rows.at[index[0], index[1], index[2], which, pl.ds(first, count), :]

    def ring(mine, part, number, where, to):
        target = device(to, mine)
        piece = ref_of(where, mine)
        return pltpu.make_async_remote_copy(
            src_ref=piece, dst_ref=piece,
            send_sem=ring_send.at[part, number], recv_sem=ring_recv.at[part, number],
            device_id=target, device_id_type=MESH,
        )

    def pair(part, number, where, which, mine):
        piece = ref_of(where, which)
        return pltpu.make_async_remote_copy(
            src_ref=piece, dst_ref=piece,
            send_sem=pair_send.at[part, number], recv_sem=pair_recv.at[part, number],
            device_id=device(pos, 1 - mine), device_id_type=MESH,
        )

    def line_units(order, part):
        a, b, c = order
        lines = [(1, pos)]
        lines += [(2, shifted(pos, b, -1)), (2, shifted(pos, b, 1)), (3, shifted(pos, b, 2))]
        middles = [lines[i][1] for i in range(4)]
        for j, middle in enumerate(middles):
            lines += [(4 + j, shifted(middle, c, -1)), (4 + j, shifted(middle, c, 1))]
        for j, middle in enumerate(middles):
            lines.append((8 + j, shifted(middle, c, 2)))
        return [(step, unit(part, at, a)) for step, at in lines]

    def own_step(mine, step):
        for part in range(2):
            a, b, c = ORDERS[mine][part]

            def send(number, where, to):
                ring(mine, part, number, where, to).start()

            def recv(number, where):
                ring(mine, part, number, where, pos).wait_recv()

            def up(axis):
                return shifted(pos, axis, 1)

            def down(axis):
                return shifted(pos, axis, -1)

            middles = [pos, down(b), up(b), shifted(pos, b, 2)]

            def spread(j):
                send(7 + 4 * j, unit(part, middles[j], a), up(c))
                send(8 + 4 * j, unit(part, middles[j], a), down(c))

            if step == 0:
                send(0, unit(part, pos, None), up(a))
                send(1, unit(part, pos, None), down(a))
                send(2, unit(part, pos, None), shifted(pos, a, 2))
            elif step == 1:
                recv(0, unit(part, down(a), None))
                recv(1, unit(part, up(a), None))
                recv(2, unit(part, shifted(pos, a, 2), None))
                send(3, unit(part, pos, a), up(b))
                send(4, unit(part, pos, a), down(b))
                spread(0)
            elif step == 2:
                recv(3, unit(part, middles[1], a))
                send(5, unit(part, middles[1], a, 0), up(b))
                recv(4, unit(part, middles[2], a))
                send(6, unit(part, middles[2], a, 1), down(b))
                spread(1)
                spread(2)
            elif step == 3:
                recv(5, unit(part, middles[3], a, 0))
                recv(6, unit(part, middles[3], a, 1))
                spread(3)
            elif step < 8:
                j = step - 4
                before, after = shifted(middles[j], c, -1), shifted(middles[j], c, 1)
                recv(7 + 4 * j, unit(part, before, a))
                send(9 + 4 * j, unit(part, before, a, 0), up(c))
                recv(8 + 4 * j, unit(part, after, a))
                send(10 + 4 * j, unit(part, after, a, 1), down(c))
            else:
                j = step - 8
                far = shifted(middles[j], c, 2)
                recv(9 + 4 * j, unit(part, far, a, 0))
                recv(10 + 4 * j, unit(part, far, a, 1))
            for number, (when, where) in enumerate(line_units(ORDERS[mine][part], part)):
                if when == step:
                    pair(part, number, where, mine, mine).start()

    def pair_step(mine, step):
        for part in range(2):
            for number, (when, where) in enumerate(line_units(ORDERS[1 - mine][part], part)):
                if when == step:
                    pair(part, number, where, 1 - mine, mine).wait_recv()

    def by_core(action, step):
        for mine in range(2):

            @pl.when(core == mine)
            def _():
                action(mine, step)

    x_hi = lax.div(x, 2)

    def multiply(dy, other, part):
        y_at = lax.rem(y + dy + 4, 4)
        hi_at = lax.rem(x_hi + other, 2)
        first, count = ROWS[part]
        taken = rows[pl.ds(2 * hi_at, 2), y_at, :, :, pl.ds(first, count), :].reshape(-1, 896)
        product = lax.dot_general(
            head[2 * y_at + hi_at], taken, (((1,), (1,)), ((), ())), preferred_element_type=jnp.float32
        )
        columns = slice(0, 16 * HIGH) if part == 0 else slice(16 * HIGH, 1024)
        if (dy, other) == (0, 0):
            scores[:, columns] = product
        else:
            scores[:, columns] += product

    ready = {
        4: [(0, 0, 0)],
        6: [(-1, 0, 0), (1, 0, 0)],
        8: [(0, 1, 0)],
        9: [(-1, 1, 0)],
        10: [(2, 0, 0), (1, 1, 0), (0, 0, 1), (-1, 0, 1), (1, 0, 1)],
        11: [(2, 1, 0), (2, 0, 1), (0, 1, 1), (-1, 1, 1), (1, 1, 1), (2, 1, 1)],
    }
    turns = (0, 1, 2, 4, 3, 5, 6, 7, 8, 9, 10, 11)
    for step in range(13):
        if step < 12:
            by_core(own_step, turns[step])
        if step == 0:
            start_scale()
            to_score_order(join_scratch[1][:, 1], targets)
        elif step == 2:
            spread_scale()
        elif step == 3:
            for copy in head_copies:
                copy.wait()
        elif step == 5:
            end_scale()
        if step >= 2:
            by_core(pair_step, turns[step - 1])
            for dy, other, part in ready.get(step - 1, []):
                multiply(dy, other, part)

    first_entry = (seq * 16 + vocab) * 512
    entries = first_entry + lax.broadcasted_iota(jnp.int32, (512, 128), 0)
    for q in range(8):
        columns = slice(128 * q, 128 * q + 128)
        part = scores[:, columns] * scales[q : q + 1]
        peak = jnp.max(part, axis=0, keepdims=True)
        matches = entries == targets[q : q + 1]
        powers = jnp.exp(part - peak)
        scores[:, columns] = powers
        stats[0, q : q + 1] = peak + jnp.log(jnp.sum(powers, axis=0, keepdims=True))
        stats[1, q : q + 1] = jnp.sum(jnp.where(matches, part, 0.0), axis=0, keepdims=True)
        stats[2, q : q + 1] = peak

    def combine(slots):
        logs = slots[:, 0]
        top = jnp.max(logs, axis=0)
        return top + jnp.log(jnp.sum(jnp.exp(logs - top[None]), axis=0)), jnp.sum(slots[:, 1], axis=0)

    vocab_stats[vocab] = stats[0:2]
    all_to_all(copy_to, vocab_stats, vocab, vocab_peers, stat_sems, 0)
    all_from_all(vocab_stats, vocab, vocab_peers, stat_sems, 0)
    seq_stats[seq, 0], seq_stats[seq, 1] = combine(vocab_stats)
    all_to_all(copy_to, seq_stats, seq, seq_peers, stat_sems, 15)
    all_from_all(seq_stats, seq, seq_peers, stat_sems, 15)
    log_total, chosen = combine(seq_stats)
    loss_ref[0, 0] = jnp.sum(log_total - chosen) / 1024
    stats[0] = jnp.exp(stats[2] - log_total)
    for q in range(8):
        columns = slice(128 * q, 128 * q + 128)
        matches = entries == targets[q : q + 1]
        grad = scores[:, columns] * stats[0, q : q + 1] - jnp.where(matches, 1.0, 0.0)
        grad_ref[:, columns] = (grad * scales[q : q + 1]).astype(jnp.bfloat16)

    def finish(mine, _):
        for part in range(2):
            a, b, c = ORDERS[mine][part]
            sizes = [(pos, None, None)] * 3 + [(pos, a, None)] * 2 + [(pos, a, 0)] * 2
            sizes += ([(pos, a, None)] * 2 + [(pos, a, 0)] * 2) * 4
            for number, (at, axis, half) in enumerate(sizes):
                ring(mine, part, number, unit(part, at, axis, half), pos).wait_send()
            for number, (_, where) in enumerate(line_units(ORDERS[mine][part], part)):
                pair(part, number, where, mine, mine).wait_send()

    by_core(finish, 0)
    for copy in sent:
        copy.wait_send()


def whole(*arguments):
    return pl.pallas_call(
        whole_kernel,
        out_shape=(
            pltpu.VMEM((512, 1024), jnp.bfloat16),
            jax.ShapeDtypeStruct((1, 1), jnp.float32),
            pltpu.VMEM((4, 4, 4, 2, 64, 896), jnp.bfloat16),
        ),
        in_specs=[pl.BlockSpec(memory_space=pltpu.VMEM)] * 3
        + [pl.BlockSpec(memory_space=pl.ANY)]
        + [pl.BlockSpec(memory_space=pltpu.VMEM)] * 5
        + [pl.BlockSpec(memory_space=pl.ANY)],
        out_specs=(
            pl.BlockSpec(memory_space=pltpu.VMEM),
            pl.BlockSpec(memory_space=pltpu.SMEM),
            pl.BlockSpec(memory_space=pltpu.VMEM),
        ),
        scratch_shapes=JOIN_SCRATCH + [
            pltpu.VMEM((8, 512, 896), jnp.bfloat16),
            pltpu.VMEM((512, 1024), jnp.float32),
            pltpu.VMEM((3, 8, 128), jnp.float32),
            pltpu.VMEM((16, 2, 8, 128), jnp.float32),
            pltpu.VMEM((8, 2, 8, 128), jnp.float32),
            pltpu.VMEM((8, 128), jnp.int32),
            pltpu.VMEM((8, 128), jnp.float32),
            pltpu.VMEM((8, 8, 128), jnp.float32),
            pltpu.VMEM((16, 8, 128), jnp.float32),
            pltpu.SemaphoreType.DMA((2, 23)),
            pltpu.SemaphoreType.DMA((2, 23)),
            pltpu.SemaphoreType.DMA((2, 16)),
            pltpu.SemaphoreType.DMA((2, 16)),
            pltpu.SemaphoreType.DMA((22,)),
            pltpu.SemaphoreType.DMA((22,)),
            pltpu.SemaphoreType.DMA((22,)),
            pltpu.SemaphoreType.DMA((22,)),
            pltpu.SemaphoreType.DMA((8,)),
        ],
        compiler_params=pltpu.CompilerParams(
            collective_id=2, has_side_effects=True, vmem_limit_bytes=44 * 1024 * 1024
        ),
    )(*arguments)


GRAD_COLUMNS = 1024


def grad_kernel(grad_ref, rows_ref, out_ref, results, sems):
    def taken(first, last):
        pieces = []
        while first < last:
            block = first // 896
            stop = min(last, 896 * block + 896)
            rows = [
                rows_ref[2 * (block % 2) : 2 * (block % 2) + 2, block // 2, :, :, start : start + count]
                .reshape(16 * count, 896)[:, first - 896 * block : stop - 896 * block]
                for start, count in ROWS
            ]
            pieces.append(jnp.concatenate(rows, axis=0))
            first = stop
        return pieces[0] if len(pieces) == 1 else jnp.concatenate(pieces, axis=1)

    copies = []
    for first in range(0, D, GRAD_COLUMNS):
        product = jnp.dot(
            grad_ref[...], taken(first, first + GRAD_COLUMNS), preferred_element_type=jnp.float32
        )
        columns = pl.ds(first, GRAD_COLUMNS)
        results[:, columns] = product.astype(jnp.bfloat16)
        copies.append(pltpu.make_async_copy(results.at[:, columns], out_ref.at[:, columns], sems.at[len(copies)]))
        copies[-1].start()
    for copy in copies:
        copy.wait()


def head_gradient(grad, rows):
    return pl.pallas_call(
        grad_kernel,
        out_shape=jax.ShapeDtypeStruct((512, D), jnp.bfloat16),
        in_specs=[pl.BlockSpec(memory_space=pltpu.VMEM)] * 2,
        out_specs=pl.BlockSpec(memory_space=pl.ANY),
        scratch_shapes=[
            pltpu.VMEM((512, D), jnp.bfloat16),
            pltpu.SemaphoreType.DMA((D // GRAD_COLUMNS,)),
        ],
        compiler_params=pltpu.CompilerParams(vmem_limit_bytes=34 * 1024 * 1024),
    )(pltpu.with_memory_space_constraint(grad, pltpu.VMEM), pltpu.with_memory_space_constraint(rows, pltpu.VMEM))


def body(
    hidden,
    next_ids,
    targets,
    embed_table,
    gain_hidden,
    gain_embed,
    proj_hidden,
    proj_embed,
    gain_final,
    head_weight,
):
    grad, loss, rows = whole(
        hidden.T,
        next_ids[None],
        targets[None],
        embed_table.T,
        gain_hidden[None],
        gain_embed[None],
        proj_hidden,
        proj_embed,
        gain_final.reshape(7, 128),
        head_weight,
    )
    return loss[0, 0], head_gradient(grad, rows)


def solution(mesh):
    in_specs = (
        P("seq", "vocab"),
        P("seq"),
        P("seq"),
        P("seq", "vocab"),
        P("vocab"),
        P("vocab"),
        P("vocab", "seq"),
        P("vocab", "seq"),
        P("seq"),
        P(("seq", "vocab"), None),
    )
    out_specs = (P(), P(("seq", "vocab"), None))
    return jax.shard_map(body, mesh=mesh, in_specs=in_specs, out_specs=out_specs, check_vma=False)
```

```python
import functools

import jax
import jax.numpy as jnp
from jax import lax
from jax.experimental import pallas as pl
from jax.experimental.pallas import tpu as pltpu
from jax.sharding import PartitionSpec as P

MESH = pl.DeviceIdType.MESH
D = 7168
EPSILON = 1e-06
HIGH, LOW = 48, 16
ORDERS = (((2, 0, 1), (0, 1, 2)), ((2, 1, 0), (1, 0, 2)))
ROWS = ((0, HIGH), (HIGH, LOW))


def coordinates():
    seq, vocab = lax.axis_index("seq"), lax.axis_index("vocab")
    return (
        (2 * lax.rem(seq, 2) + lax.rem(lax.div(vocab, 2), 2), lax.div(seq, 2), lax.div(vocab, 4)),
        lax.rem(vocab, 2),
    )


def device(pos, core):
    x, y, z = pos
    return (2 * y + lax.div(x, 2), 4 * z + 2 * lax.rem(x, 2) + core)


def shifted(pos, axis, by):
    moved = list(pos)
    moved[axis] = lax.rem(pos[axis] + (by + 4), 4)
    return tuple(moved)


def greet(peers):
    barrier = pltpu.get_barrier_semaphore()
    for peer in peers:
        pl.semaphore_signal(barrier, inc=1, device_id=peer, device_id_type=MESH)
    pl.semaphore_wait(barrier, len(peers))


def start_copy(sent, source, there, sems, number, to):
    copy = pltpu.make_async_remote_copy(
        src_ref=source, dst_ref=there, send_sem=sems[0].at[number], recv_sem=sems[1].at[number],
        device_id=to, device_id_type=MESH,
    )
    copy.start()
    sent.append(copy)


def arrived(place, sems, number, to):
    pltpu.make_async_remote_copy(
        src_ref=place, dst_ref=place, send_sem=sems[0].at[number], recv_sem=sems[1].at[number],
        device_id=to, device_id_type=MESH,
    ).wait_recv()


def all_to_all(copy_to, buffer, me, peers, sems, base):
    for i, peer in enumerate(peers):
        copy_to(buffer.at[me], buffer.at[me], sems, base + i, peer)


def all_from_all(buffer, me, peers, sems, base):
    count = len(peers) + 1
    for i, peer in enumerate(peers):
        arrived(buffer.at[lax.rem(me - (i + 1) + count, count)], sems, base + i, peer)


def greet_all(vocab_peers, seq_peers):
    pos, core = coordinates()
    across = device(shifted(pos, 0, 1 - 2 * (1 - lax.rem(pos[0], 2))), core)
    greet(vocab_peers + seq_peers + [across])


def row_to_columns(row):
    return jnp.transpose(jnp.broadcast_to(row, (128, 128)))


def lane_sums(values):
    total = jnp.zeros((values.shape[0], 128), jnp.float32)
    for first in range(0, values.shape[1], 128):
        total += values[:, first : first + 128] * values[:, first : first + 128]
    return total


def join_kernel(
    hidden_ref, ids_ref, targets_ref, table_ref, gain_hidden_ref, gain_embed_ref,
    proj_hidden_ref, proj_embed_ref, gain_final_ref,
    table, tokens, hidden, embed, gains, parts, halves_in, sums_out, sums_in, square_slots, scale_slots,
    embed_scale, projected, pair_in, z_out, z_in, own,
    h_send, h_recv, r_send, r_recv, g_send, g_recv, v_send, v_recv, q_send, q_recv,
    p_send, p_recv, z_send, z_recv, table_sem,
    vocab_peers, seq_peers, start_head,
):
    pos, core = coordinates()
    x, y, z = pos
    seq, vocab = lax.axis_index("seq"), lax.axis_index("vocab")
    x_hi, x_lo = lax.div(x, 2), lax.rem(x, 2)
    y_up, y_down = lax.rem(y + 1, 4), lax.rem(y + 3, 4)
    to_y_up, to_y_down = (2 * y_up + x_hi, vocab), (2 * y_down + x_hi, vocab)
    to_x = (2 * y + 1 - x_hi, vocab)
    to_pair = (seq, 4 * z + 2 * x_lo + 1 - core)
    sent = []
    copy_to = functools.partial(start_copy, sent)
    h_sems, r_sems, g_sems = (h_send, h_recv), (r_send, r_recv), (g_send, g_recv)
    v_sems, q_sems = (v_send, v_recv), (q_send, q_recv)
    p_sems = (p_send, p_recv)
    mine = 2 * z + x_lo

    table_copy = pltpu.make_async_copy(table_ref, table, table_sem.at[0])
    table_copy.start()
    tokens[seq, 0:1] = ids_ref[...]
    tokens[seq, 1:2] = targets_ref[...]
    greet_all(vocab_peers, seq_peers)
    all_to_all(copy_to, tokens, seq, seq_peers, q_sems, 0)
    hidden[seq] = hidden_ref[...]
    copy_to(hidden.at[seq], hidden.at[seq], h_sems, 0, to_x)
    copy_to(hidden.at[seq], hidden.at[seq], h_sems, 1, to_y_up)
    copy_to(hidden.at[seq], hidden.at[seq], h_sems, 2, to_y_down)

    def start_hidden_scale():
        values = hidden_ref[...].astype(jnp.float32)
        total = jnp.sum(values * values, axis=0, keepdims=True)
        square_slots[0, vocab] = jnp.broadcast_to(total, (8, 128))
        all_to_all(copy_to, square_slots.at[0], vocab, vocab_peers, v_sems, 0)

    def start_embed_scale():
        for i in range(8):
            values = parts[i // 2, i % 2].astype(jnp.float32)
            square_slots[1, vocab, i : i + 1] = jnp.sum(values * values, axis=0, keepdims=True)
        all_to_all(copy_to, square_slots.at[1], vocab, vocab_peers, v_sems, 15)

    def spread_scale(which):
        all_from_all(square_slots.at[which], vocab, vocab_peers, v_sems, 15 * which)
        total = jnp.sum(square_slots[which], axis=0)
        scale_slots[which, seq] = total if which else lax.rsqrt(total / D + EPSILON)
        all_to_all(copy_to, scale_slots.at[which], seq, seq_peers, q_sems, 7 + 7 * which)

    def end_scale(which):
        all_from_all(scale_slots.at[which], seq, seq_peers, q_sems, 7 + 7 * which)
        if which:
            embed_scale[...] = lax.rsqrt(jnp.sum(scale_slots[1], axis=0) / D + EPSILON)

    start_hidden_scale()
    for which, gain_ref in enumerate((gain_hidden_ref, gain_embed_ref)):
        for first in range(0, 448, 128):
            row = gain_ref[:, first : min(first + 128, 448)]
            if first == 384:
                row = jnp.concatenate([row, jnp.zeros((1, 64), jnp.float32)], axis=1)
            gains[which, first : min(first + 128, 448)] = row_to_columns(row)[: min(448 - first, 128)]
    all_from_all(tokens, seq, seq_peers, q_sems, 0)
    table_copy.wait()
    start_head()

    def look_up(y_at):
        ids = jnp.concatenate([tokens[2 * y_at, 0:1], tokens[2 * y_at + 1, 0:1]], axis=1) - seq * 8192
        total = jnp.zeros((448, 256), jnp.float32)
        for first in range(0, 8192, 1024):
            entries = lax.broadcasted_iota(jnp.int32, (1024, 256), 0) + first
            chosen = jnp.where(entries == ids, 1.0, 0.0).astype(jnp.bfloat16)
            total += jnp.dot(table[:, first : first + 1024], chosen, preferred_element_type=jnp.float32)
        return total.astype(jnp.bfloat16)

    def near_or_other(e):
        return x_hi if e == 0 else 1 - x_hi

    def seq_at(number):
        return 2 * lax.rem(y + number // 2, 4) + near_or_other(number % 2)

    def look_up_and_send(dy):
        y_at = lax.rem(y + dy, 4)
        found = look_up(y_at)
        for i in range(2):
            parts[y_at, i] = found[:, 128 * i : 128 * i + 128]
        copy_to(parts.at[y_at, 1 - x_hi], halves_in.at[dy], r_sems, dy, to_x)

    def sum_and_send(dy):
        y_at = lax.rem(y + dy, 4)
        arrived(halves_in.at[dy], r_sems, dy, to_x)
        total = parts[y_at, x_hi] + halves_in[dy]
        if dy:
            sums_out[dy] = total
            copy_to(sums_out.at[dy], sums_in.at[dy], r_sems, 3 + dy, (2 * y_at + x_hi, vocab))
        return total

    other = 2 * y + 1 - x_hi
    below, above = 2 * y_down + x_hi, 2 * y_up + x_hi
    other_below, other_above = 2 * y_down + 1 - x_hi, 2 * y_up + 1 - x_hi
    far, other_far = seq_at(4), seq_at(5)
    look_up_and_send(2)
    look_up_and_send(1)
    arrived(hidden.at[other], h_sems, 0, to_x)
    copy_to(hidden.at[other], hidden.at[other], h_sems, 3, to_y_up)
    copy_to(hidden.at[other], hidden.at[other], h_sems, 4, to_y_down)
    arrived(hidden.at[below], h_sems, 1, to_y_down)
    copy_to(hidden.at[below], hidden.at[below], h_sems, 5, to_y_up)
    spread_scale(0)
    look_up_and_send(3)
    sum_and_send(2)
    look_up_and_send(0)
    sum_and_send(1)
    start_embed_scale()
    arrived(hidden.at[other_above], h_sems, 4, to_y_up)
    copy_to(hidden.at[other_above], hidden.at[other_above], h_sems, 6, to_y_down)
    sum_and_send(3)

    total = sum_and_send(0)
    spread_scale(1)
    for dy in (1, 3, 2):
        arrived(sums_in.at[dy], r_sems, 3 + dy, to_x)
        total += sums_in[dy]
    embed[seq] = total

    def send_embedded(number):
        copy_to(embed.at[seq], embed.at[seq], g_sems, number, (seq_at(number), vocab))

    order = (0, 2, 6, 1, 4, 3, 7, 5)
    blocks = [seq] + [2 * lax.rem(y + 4 - n // 2, 4) + near_or_other(n % 2) for n in order[1:]]
    for number in order[1:]:
        send_embedded(number)

    def project(source, scale, gain, weight_ref):
        values = source.astype(jnp.float32) * scale * gain
        return lax.dot_general(
            values.astype(jnp.bfloat16), weight_ref[...], (((0,), (0,)), ((), ())),
            preferred_element_type=jnp.float32,
        ).reshape(2, 64, 896)

    arrived(hidden.at[above], h_sems, 2, to_y_up)
    arrived(hidden.at[other_below], h_sems, 3, to_y_down)
    arrived(hidden.at[far], h_sems, 5, to_y_down)
    arrived(hidden.at[other_far], h_sems, 6, to_y_up)
    end_scale(0)
    for k, block in enumerate(blocks):
        projected[k] = project(hidden[block], scale_slots[0, block, 0:1], gains[0], proj_hidden_ref)
    end_scale(1)

    late = []

    def hand_on(k):
        block = blocks[k]
        arrived(pair_in.at[k], p_sems, k, to_pair)
        both = projected[k, core] + pair_in[k]
        copy = pltpu.make_async_remote_copy(
            src_ref=z_out.at[k], dst_ref=z_in.at[mine], send_sem=z_send.at[k], recv_sem=z_recv.at[mine],
            device_id=(seq, 2 * block + core), device_id_type=MESH,
        )
        late.append((copy, block != mine))

        @pl.when(block != mine)
        def _():
            z_out[k] = both.astype(jnp.bfloat16)
            copy.start()

        @pl.when(block == mine)
        def _():
            own[...] = both

    for k, block in enumerate(blocks):
        if k:
            arrived(embed.at[block], g_sems, order[k], to_x)
        projected[k] += project(embed[block], embed_scale[pl.ds(block, 1)], gains[1], proj_embed_ref)
        copy_to(projected.at[k, 1 - core], pair_in.at[k], p_sems, k, to_pair)
        if k:
            hand_on(k - 1)
    hand_on(7)

    total = own[...]
    for number in range(1, 8):
        x_at = x_lo if number % 2 == 0 else 1 - x_lo
        sender = 2 * lax.rem(z + number // 2, 4) + x_at
        pltpu.make_async_remote_copy(
            src_ref=z_in.at[sender], dst_ref=z_in.at[sender], send_sem=z_send.at[0], recv_sem=z_recv.at[sender],
            device_id=to_pair, device_id_type=MESH,
        ).wait_recv()
        total += z_in[sender].astype(jnp.float32)
    return total, sent, late


JOIN_SCRATCH = [
    pltpu.VMEM((448, 8192), jnp.bfloat16),
    pltpu.VMEM((8, 2, 128), jnp.int32),
    pltpu.VMEM((8, 448, 128), jnp.bfloat16),
    pltpu.VMEM((8, 448, 128), jnp.bfloat16),
    pltpu.VMEM((2, 448, 128), jnp.float32),
    pltpu.VMEM((4, 2, 448, 128), jnp.bfloat16),
    pltpu.VMEM((4, 448, 128), jnp.bfloat16),
    pltpu.VMEM((4, 448, 128), jnp.bfloat16),
    pltpu.VMEM((4, 448, 128), jnp.bfloat16),
    pltpu.VMEM((2, 16, 8, 128), jnp.float32),
    pltpu.VMEM((2, 8, 8, 128), jnp.float32),
    pltpu.VMEM((8, 128), jnp.float32),
    pltpu.VMEM((8, 2, 64, 896), jnp.float32),
    pltpu.VMEM((8, 64, 896), jnp.float32),
    pltpu.VMEM((8, 64, 896), jnp.bfloat16),
    pltpu.VMEM((8, 64, 896), jnp.bfloat16),
    pltpu.VMEM((64, 896), jnp.float32),
    *[pltpu.SemaphoreType.DMA((count,)) for count in (7, 7, 8, 8, 8, 8, 30, 30, 21, 21, 8, 8, 8, 8)],
    pltpu.SemaphoreType.DMA((1,)),
]


def to_score_order(natural, ordered):
    turned = {0: natural}
    lane = lax.broadcasted_iota(jnp.int32, (1, 128), 1)
    for part, (first, count) in enumerate(ROWS):
        for group in range(16):
            vocab = 4 * (group // 2 % 4) + 2 * (group // 8) + group % 2
            start = 16 * first + count * group
            done = 0
            while done < count:
                place, origin = start + done, 64 * vocab + first + done
                to, at = divmod(place, 128)
                size = min(count - done, 128 - at)
                turn = (at - origin) % 128
                if turn not in turned:
                    turned[turn] = pltpu.roll(natural, turn, 1)
                row = turned[turn][origin // 128 : origin // 128 + 1]
                if at == 0:
                    line = row
                else:
                    line = jnp.where(lane < at, line, row)
                if at + size == 128:
                    ordered[to : to + 1] = line
                done += size


def whole_kernel(*refs):
    inputs, (head_ref, grad_ref, loss_ref, rows) = refs[:9], refs[9:13]
    join_scratch = refs[13 : 13 + len(JOIN_SCRATCH)]
    (
        head, scores, stats, vocab_stats, seq_stats, targets, scales, final_slots, row_slots,
        ring_send, ring_recv, pair_send, pair_recv, stat_send, stat_recv, f_send, f_recv, local_sem,
    ) = refs[13 + len(JOIN_SCRATCH) :]
    pos, core = coordinates()
    seq, vocab = lax.axis_index("seq"), lax.axis_index("vocab")
    x, y, z = pos
    head_copies = [
        pltpu.make_async_copy(
            head_ref.at[:, pl.ds(896 * i, 896)], head.at[i], local_sem.at[i]
        )
        for i in range(8)
    ]

    def start_head():
        for copy in head_copies:
            copy.start()

    vocab_peers = [(seq, lax.rem(vocab + i, 16)) for i in range(1, 16)]
    seq_peers = [(lax.rem(seq + i, 8), vocab) for i in range(1, 8)]
    total, sent, late = join_kernel(*inputs, *join_scratch, vocab_peers, seq_peers, start_head)
    copy_to = functools.partial(start_copy, sent)
    f_sems, stat_sems = (f_send, f_recv), (stat_send, stat_recv)

    gain = jnp.concatenate([inputs[8][i : i + 1] for i in range(7)], axis=1)
    rows[x, y, z, core] = (total * gain).astype(jnp.bfloat16)

    def start_scale():
        spread = jnp.concatenate([lane_sums(total), jnp.zeros((64, 128), jnp.float32)], axis=0)
        squares = jnp.sum(jnp.transpose(spread), axis=0, keepdims=True)
        final_slots[seq] = jnp.broadcast_to(squares, (8, 128))
        all_to_all(copy_to, final_slots, seq, seq_peers, f_sems, 0)

    def spread_scale():
        all_from_all(final_slots, seq, seq_peers, f_sems, 0)
        row_slots[vocab] = lax.rsqrt(jnp.sum(final_slots[...], axis=0) / D + EPSILON)
        all_to_all(copy_to, row_slots, vocab, vocab_peers, f_sems, 7)

    def end_scale():
        all_from_all(row_slots, vocab, vocab_peers, f_sems, 7)
        lane = lax.broadcasted_iota(jnp.int32, (1, 128), 1)
        natural = []
        for i in range(8):
            later = pltpu.roll(row_slots[2 * i + 1], 64, 1)[0:1]
            natural.append(jnp.where(lane < 64, row_slots[2 * i, 0:1], later))
        to_score_order(jnp.concatenate(natural, axis=0), scales)

    def unit(part, at, axis, half=None):
        index = list(at)
        if axis is not None:
            index[axis] = pl.ds(0, 4) if half is None else pl.ds(2 * half, 2)
        return index, ROWS[part]

    def ref_of(where, which):
        index, (first, count) = where
        return rows.at[index[0], index[1], index[2], which, pl.ds(first, count), :]

    def ring(mine, part, number, where, to):
        target = device(to, mine)
        piece = ref_of(where, mine)
        return pltpu.make_async_remote_copy(
            src_ref=piece, dst_ref=piece,
            send_sem=ring_send.at[part, number], recv_sem=ring_recv.at[part, number],
            device_id=target, device_id_type=MESH,
        )

    def pair(part, number, where, which, mine):
        piece = ref_of(where, which)
        return pltpu.make_async_remote_copy(
            src_ref=piece, dst_ref=piece,
            send_sem=pair_send.at[part, number], recv_sem=pair_recv.at[part, number],
            device_id=device(pos, 1 - mine), device_id_type=MESH,
        )

    def line_units(order, part):
        a, b, c = order
        lines = [(1, pos)]
        lines += [(2, shifted(pos, b, -1)), (2, shifted(pos, b, 1)), (3, shifted(pos, b, 2))]
        middles = [lines[i][1] for i in range(4)]
        for j, middle in enumerate(middles):
            lines += [(4 + j, shifted(middle, c, -1)), (4 + j, shifted(middle, c, 1))]
        for j, middle in enumerate(middles):
            lines.append((8 + j, shifted(middle, c, 2)))
        return [(step, unit(part, at, a)) for step, at in lines]

    def own_step(mine, step):
        for part in range(2):
            a, b, c = ORDERS[mine][part]

            def send(number, where, to):
                ring(mine, part, number, where, to).start()

            def recv(number, where):
                ring(mine, part, number, where, pos).wait_recv()

            def up(axis):
                return shifted(pos, axis, 1)

            def down(axis):
                return shifted(pos, axis, -1)

            middles = [pos, down(b), up(b), shifted(pos, b, 2)]

            def spread(j):
                send(7 + 4 * j, unit(part, middles[j], a), up(c))
                send(8 + 4 * j, unit(part, middles[j], a), down(c))

            if step == 0:
                send(0, unit(part, pos, None), up(a))
                send(1, unit(part, pos, None), down(a))
                send(2, unit(part, pos, None), shifted(pos, a, 2))
            elif step == 1:
                recv(0, unit(part, down(a), None))
                recv(1, unit(part, up(a), None))
                recv(2, unit(part, shifted(pos, a, 2), None))
                send(3, unit(part, pos, a), up(b))
                send(4, unit(part, pos, a), down(b))
                spread(0)
            elif step == 2:
                recv(3, unit(part, middles[1], a))
                send(5, unit(part, middles[1], a, 0), up(b))
                recv(4, unit(part, middles[2], a))
                send(6, unit(part, middles[2], a, 1), down(b))
                spread(1)
                spread(2)
            elif step == 3:
                recv(5, unit(part, middles[3], a, 0))
                recv(6, unit(part, middles[3], a, 1))
                spread(3)
            elif step < 8:
                j = step - 4
                before, after = shifted(middles[j], c, -1), shifted(middles[j], c, 1)
                recv(7 + 4 * j, unit(part, before, a))
                send(9 + 4 * j, unit(part, before, a, 0), up(c))
                recv(8 + 4 * j, unit(part, after, a))
                send(10 + 4 * j, unit(part, after, a, 1), down(c))
            else:
                j = step - 8
                far = shifted(middles[j], c, 2)
                recv(9 + 4 * j, unit(part, far, a, 0))
                recv(10 + 4 * j, unit(part, far, a, 1))
            for number, (when, where) in enumerate(line_units(ORDERS[mine][part], part)):
                if when == step:
                    pair(part, number, where, mine, mine).start()

    def pair_step(mine, step):
        for part in range(2):
            for number, (when, where) in enumerate(line_units(ORDERS[1 - mine][part], part)):
                if when == step:
                    pair(part, number, where, 1 - mine, mine).wait_recv()

    def by_core(action, step):
        for mine in range(2):

            @pl.when(core == mine)
            def _():
                action(mine, step)

    x_hi = lax.div(x, 2)

    def multiply(part, groups):
        total = None
        for dy, other in groups:
            y_at, hi_at = lax.rem(y + dy + 4, 4), lax.rem(x_hi + other, 2)
            first, count = ROWS[part]
            taken = rows[pl.ds(2 * hi_at, 2), y_at, :, :, pl.ds(first, count), :].reshape(-1, 896)
            product = lax.dot_general(
                head[2 * y_at + hi_at], taken, (((1,), (1,)), ((), ())), preferred_element_type=jnp.float32
            )
            total = product if total is None else total + product
        columns = slice(0, 16 * HIGH) if part == 0 else slice(16 * HIGH, 1024)
        if (0, 0) in groups:
            scores[:, columns] = total
        else:
            scores[:, columns] += total

    ready = {
        4: [(0, [(0, 0)])],
        6: [(0, [(-1, 0), (1, 0)])],
        8: [(0, [(0, 1)])],
        9: [(0, [(-1, 1)])],
        10: [(0, [(2, 0), (1, 1)]), (1, [(0, 0), (-1, 0), (1, 0)])],
        11: [(0, [(2, 1)]), (1, [(2, 0), (0, 1), (-1, 1), (1, 1), (2, 1)])],
    }
    turns = (0, 1, 2, 4, 3, 5, 6, 7, 8, 9, 10, 11)
    for step in range(13):
        if step < 12:
            by_core(own_step, turns[step])
        if step == 0:
            start_scale()
            to_score_order(join_scratch[1][:, 1], targets)
        elif step == 2:
            spread_scale()
        elif step == 3:
            for copy in head_copies:
                copy.wait()
        elif step == 5:
            end_scale()
        if step >= 2:
            by_core(pair_step, turns[step - 1])
            for part, groups in ready.get(step - 1, []):
                multiply(part, groups)

    first_entry = (seq * 16 + vocab) * 512
    entries = first_entry + lax.broadcasted_iota(jnp.int32, (512, 128), 0)
    for q in range(8):
        columns = slice(128 * q, 128 * q + 128)
        part = scores[:, columns] * scales[q : q + 1]
        peak = jnp.max(part, axis=0, keepdims=True)
        matches = entries == targets[q : q + 1]
        powers = jnp.exp(part - peak)
        scores[:, columns] = powers
        stats[0, q : q + 1] = peak + jnp.log(jnp.sum(powers, axis=0, keepdims=True))
        stats[1, q : q + 1] = jnp.sum(jnp.where(matches, part, 0.0), axis=0, keepdims=True)
        stats[2, q : q + 1] = peak

    def combine(slots):
        logs = slots[:, 0]
        top = jnp.max(logs, axis=0)
        return top + jnp.log(jnp.sum(jnp.exp(logs - top[None]), axis=0)), jnp.sum(slots[:, 1], axis=0)

    vocab_stats[vocab] = stats[0:2]
    all_to_all(copy_to, vocab_stats, vocab, vocab_peers, stat_sems, 0)
    all_from_all(vocab_stats, vocab, vocab_peers, stat_sems, 0)
    seq_stats[seq, 0], seq_stats[seq, 1] = combine(vocab_stats)
    all_to_all(copy_to, seq_stats, seq, seq_peers, stat_sems, 15)
    all_from_all(seq_stats, seq, seq_peers, stat_sems, 15)
    log_total, chosen = combine(seq_stats)
    loss_ref[0, 0] = jnp.sum(log_total - chosen) / 1024
    stats[0] = jnp.exp(stats[2] - log_total)
    for q in range(8):
        columns = slice(128 * q, 128 * q + 128)
        matches = entries == targets[q : q + 1]
        grad = scores[:, columns] * stats[0, q : q + 1] - jnp.where(matches, 1.0, 0.0)
        grad_ref[:, columns] = (grad * scales[q : q + 1]).astype(jnp.bfloat16)

    def finish(mine, _):
        for part in range(2):
            a, b, c = ORDERS[mine][part]
            sizes = [(pos, None, None)] * 3 + [(pos, a, None)] * 2 + [(pos, a, 0)] * 2
            sizes += ([(pos, a, None)] * 2 + [(pos, a, 0)] * 2) * 4
            for number, (at, axis, half) in enumerate(sizes):
                ring(mine, part, number, unit(part, at, axis, half), pos).wait_send()
            for number, (_, where) in enumerate(line_units(ORDERS[mine][part], part)):
                pair(part, number, where, mine, mine).wait_send()

    by_core(finish, 0)
    for copy in sent:
        copy.wait_send()
    for copy, there in late:

        @pl.when(there)
        def _():
            copy.wait_send()


def whole(*arguments):
    return pl.pallas_call(
        whole_kernel,
        out_shape=(
            pltpu.VMEM((512, 1024), jnp.bfloat16),
            jax.ShapeDtypeStruct((1, 1), jnp.float32),
            pltpu.VMEM((4, 4, 4, 2, 64, 896), jnp.bfloat16),
        ),
        in_specs=[pl.BlockSpec(memory_space=pltpu.VMEM)] * 3
        + [pl.BlockSpec(memory_space=pl.ANY)]
        + [pl.BlockSpec(memory_space=pltpu.VMEM)] * 5
        + [pl.BlockSpec(memory_space=pl.ANY)],
        out_specs=(
            pl.BlockSpec(memory_space=pltpu.VMEM),
            pl.BlockSpec(memory_space=pltpu.SMEM),
            pl.BlockSpec(memory_space=pltpu.VMEM),
        ),
        scratch_shapes=JOIN_SCRATCH + [
            pltpu.VMEM((8, 512, 896), jnp.bfloat16),
            pltpu.VMEM((512, 1024), jnp.float32),
            pltpu.VMEM((3, 8, 128), jnp.float32),
            pltpu.VMEM((16, 2, 8, 128), jnp.float32),
            pltpu.VMEM((8, 2, 8, 128), jnp.float32),
            pltpu.VMEM((8, 128), jnp.int32),
            pltpu.VMEM((8, 128), jnp.float32),
            pltpu.VMEM((8, 8, 128), jnp.float32),
            pltpu.VMEM((16, 8, 128), jnp.float32),
            pltpu.SemaphoreType.DMA((2, 23)),
            pltpu.SemaphoreType.DMA((2, 23)),
            pltpu.SemaphoreType.DMA((2, 16)),
            pltpu.SemaphoreType.DMA((2, 16)),
            pltpu.SemaphoreType.DMA((22,)),
            pltpu.SemaphoreType.DMA((22,)),
            pltpu.SemaphoreType.DMA((22,)),
            pltpu.SemaphoreType.DMA((22,)),
            pltpu.SemaphoreType.DMA((8,)),
        ],
        compiler_params=pltpu.CompilerParams(
            collective_id=2, has_side_effects=True, vmem_limit_bytes=44 * 1024 * 1024
        ),
    )(*arguments)


GRAD_COLUMNS = 1024


def grad_kernel(grad_ref, rows_ref, out_ref, results, sems):
    def taken(first, last):
        pieces = []
        while first < last:
            block = first // 896
            stop = min(last, 896 * block + 896)
            rows = [
                rows_ref[2 * (block % 2) : 2 * (block % 2) + 2, block // 2, :, :, start : start + count]
                .reshape(16 * count, 896)[:, first - 896 * block : stop - 896 * block]
                for start, count in ROWS
            ]
            pieces.append(jnp.concatenate(rows, axis=0))
            first = stop
        return pieces[0] if len(pieces) == 1 else jnp.concatenate(pieces, axis=1)

    copies = []
    for first in range(0, D, GRAD_COLUMNS):
        product = jnp.dot(
            grad_ref[...], taken(first, first + GRAD_COLUMNS), preferred_element_type=jnp.float32
        )
        columns = pl.ds(first, GRAD_COLUMNS)
        results[:, columns] = product.astype(jnp.bfloat16)
        copies.append(pltpu.make_async_copy(results.at[:, columns], out_ref.at[:, columns], sems.at[len(copies)]))
        copies[-1].start()
    for copy in copies:
        copy.wait()


def head_gradient(grad, rows):
    return pl.pallas_call(
        grad_kernel,
        out_shape=jax.ShapeDtypeStruct((512, D), jnp.bfloat16),
        in_specs=[pl.BlockSpec(memory_space=pltpu.VMEM)] * 2,
        out_specs=pl.BlockSpec(memory_space=pl.ANY),
        scratch_shapes=[
            pltpu.VMEM((512, D), jnp.bfloat16),
            pltpu.SemaphoreType.DMA((D // GRAD_COLUMNS,)),
        ],
        compiler_params=pltpu.CompilerParams(vmem_limit_bytes=34 * 1024 * 1024),
    )(pltpu.with_memory_space_constraint(grad, pltpu.VMEM), pltpu.with_memory_space_constraint(rows, pltpu.VMEM))


def body(
    hidden,
    next_ids,
    targets,
    embed_table,
    gain_hidden,
    gain_embed,
    proj_hidden,
    proj_embed,
    gain_final,
    head_weight,
):
    grad, loss, rows = whole(
        hidden.T,
        next_ids[None],
        targets[None],
        embed_table.T,
        gain_hidden[None],
        gain_embed[None],
        proj_hidden,
        proj_embed,
        gain_final.reshape(7, 128),
        head_weight,
    )
    return loss[0, 0], head_gradient(grad, rows)


def solution(mesh):
    in_specs = (
        P("seq", "vocab"),
        P("seq"),
        P("seq"),
        P("seq", "vocab"),
        P("vocab"),
        P("vocab"),
        P("vocab", "seq"),
        P("vocab", "seq"),
        P("seq"),
        P(("seq", "vocab"), None),
    )
    out_specs = (P(), P(("seq", "vocab"), None))
    return jax.shard_map(body, mesh=mesh, in_specs=in_specs, out_specs=out_specs, check_vma=False)
```
